32 devices in a mesh: dp: 8 (over z, y), blk: 4 (over x, core).
Axes of the slice: x: 2, y: 2, z: 4, core: 2. Of those that a mesh axis runs over, the one named last changes fastest.
Arguments:
- tokens: bfloat16 [8, 2, 256, 1152], P('dp', None, 'blk'), may hold values from -6 to 6
- timestep: int32 [8], replicated, may hold values from 0 to 999
- mod_table: bfloat16 [1000, 6912], P(None, ('dp', 'blk')), may hold values from -4 to 4
- w_qkv: bfloat16 [1152, 3456], P('blk', 'dp'), may hold values from -0.1875 to 0.1875
- w_out: bfloat16 [1152, 1152], P('blk', 'dp'), may hold values from -1.5 to 1.5
- w_up: bfloat16 [1152, 4608], P('blk', 'dp'), may hold values from -0.1875 to 0.1875
- w_down: bfloat16 [4608, 1152], P('blk', 'dp'), may hold values from -0.09375 to 0.09375
- cotangent: bfloat16 [8, 2, 256, 1152], P('dp', None, 'blk'), may hold values from -6 to 6
Outputs:
- output: float32 [8, 2, 256, 1152], P('dp', None, 'blk')
- grad_tokens: float32 [8, 2, 256, 1152], P('dp', None, 'blk')
- grad_table: float32 [1000, 6912], P(None, ('dp', 'blk'))
- grad_qkv: float32 [1152, 3456], P('blk', 'dp')
- grad_out: float32 [1152, 1152], P('blk', 'dp')
- grad_up: float32 [1152, 4608], P('blk', 'dp')
- grad_down: float32 [4608, 1152], P('blk', 'dp')
The draws below stay inside these ranges and needn't reach their ends.
All inputs are finite; a program needn't handle non-finite values.
Results may differ from the reference program's by a relative error of at most 0.014.
The reference program's roundings to bfloat16 on the way count: a program that leaves them out, or rounds other values in their place, can miss the bound.
Values may be sent and summed in bfloat16 or wider, within the bound.
No kernel may reach another device: no remote copies, remote signals or barrier semaphores. Data moves between devices by JAX's collectives and lax.ppermute only.
A program may use at most 192 MiB of HBM per device.

```python
import jax
import jax.numpy as jnp
from jax import lax

D = 1152
HEADS = 16
HEAD_DIM = 72
FF = 4608
NT = 1000
FRAMES = 2
CLIPS = 8
PATCHES = 256


def touch_ends(values, own_key, smallest, high):
    shape = values.shape
    place = [jax.random.randint(jax.random.fold_in(own_key, axis), (), 0, shape[axis]) for axis in range(len(shape))]
    values = values.at[tuple(place)].set(smallest)
    longest = shape.index(max(shape))
    place[longest] = (place[longest] + 1) % shape[longest]
    return values.at[tuple(place)].set(high)


def steps_of(stream_key, shape, pieces, low, high):
    gain, own = 1.0, jax.random.fold_in(stream_key, 6)
    for dim, blocks in pieces:
        heights = jnp.exp(jax.random.uniform(jax.random.fold_in(own, dim), (blocks,), jnp.float32, low / len(pieces), high / len(pieces)))
        gain = gain * jnp.repeat(heights, shape[dim] // blocks).reshape([-1 if axis == dim else 1 for axis in range(len(shape))])
    return gain


def noise(rng, extent, width, limit, pieces=(), kind=jnp.bfloat16):
    factor_of = steps_of(rng, extent, pieces, -0.22, 0.18) if pieces else 1.0
    drawn = jax.random.normal(rng, extent, jnp.float32) * width * factor_of
    return jnp.minimum(jnp.maximum(drawn, -limit), limit).astype(kind)


def setup_inputs(seed: int = 0) -> dict:
    splits = jax.random.split(jax.random.key(seed), 9)
    return {
        "tokens": noise(splits[0], (CLIPS, FRAMES, PATCHES, D), 1.0, 6.0, ((0, 8), (2, 4))),
        "timestep": touch_ends(jax.random.randint(splits[1], (CLIPS,), 0, NT), jax.random.fold_in(splits[1], 1), 0, NT - 1).astype(jnp.int32),
        "mod_table": noise(splits[2], (NT, 6 * D), 0.7, 4.0, ((1, 32),)),
        "w_qkv": noise(splits[3], (D, 3 * D), D ** -0.5, 0.1875, ((0, 4), (1, 8))),
        "w_out": noise(splits[4], (D, D), (D // 64) ** -0.5, 1.5, ((0, 4), (1, 8))),
        "w_up": noise(splits[5], (D, FF), D ** -0.5, 0.1875, ((0, 4), (1, 8))),
        "w_down": noise(splits[6], (FF, D), FF ** -0.5, 0.09375, ((0, 4), (1, 8))),
        "cotangent": noise(splits[7], (CLIPS, FRAMES, PATCHES, D), 1.0, 6.0, ((0, 8), (2, 4))),
    }


@jax.custom_vjp
def low(v):
    return lax.optimization_barrier(v.astype(jnp.bfloat16)).astype(jnp.float32)

@jax.custom_vjp
def low_back(v):
    return v

def low_keep(v):
    return (low(v), None)

def low_pass(kept, grad):
    return (grad,)

def back_keep(v):
    return (v, None)

def back_low(kept, grad):
    return (low(grad),)
low.defvjp(low_keep, low_pass)
low_back.defvjp(back_keep, back_low)
HIGHEST = lax.Precision.HIGHEST

def layer_norm(values):
    center = values - lax.optimization_barrier(jnp.mean(values, axis=-1, keepdims=True))
    spread = lax.optimization_barrier(jnp.mean(center * center, axis=-1, keepdims=True))
    return center * lax.rsqrt(spread + 1e-06)

def frame_attend(parts):
    query_f, key_f, value_f = parts
    scores = low_back(jnp.einsum('phe,khe->hpk', query_f, key_f, precision=HIGHEST) * HEAD_DIM ** (-0.5))
    probs = low(jax.nn.softmax(scores, axis=-1))
    return jnp.einsum('hpk,khe->phe', probs, value_f, precision=HIGHEST)

def clip_forward(tok_clip, mod_row, qkv_weight, out_weight, up_weight, down_weight):
    shift_a, scale_a, gate_a, shift_b, scale_b, gate_b = jnp.split(mod_row, 6)
    normed_a = layer_norm(tok_clip)
    hidden_a = low(normed_a * (1.0 + scale_a) + shift_a)
    projected = low(low_back(jnp.dot(hidden_a, qkv_weight, precision=HIGHEST)))
    shaped = projected.reshape(FRAMES, PATCHES, 3, HEADS, HEAD_DIM)
    attended = lax.map(jax.checkpoint(frame_attend), (shaped[:, :, 0], shaped[:, :, 1], shaped[:, :, 2]))
    attn_low = low(low_back(attended.reshape(FRAMES, PATCHES, D)))
    branch_a = low_back(jnp.dot(attn_low, out_weight, precision=HIGHEST))
    middle = tok_clip + gate_a * branch_a
    normed_b = layer_norm(middle)
    hidden_b = low(normed_b * (1.0 + scale_b) + shift_b)
    pre_act = low_back(jnp.dot(hidden_b, up_weight, precision=HIGHEST))
    activated = low(jax.nn.gelu(pre_act, approximate=True))
    branch_b = low_back(jnp.dot(activated, down_weight, precision=HIGHEST))
    return middle + gate_b * branch_b

def reference(tokens, timestep, mod_table, w_qkv, w_out, w_up, w_down, cotangent):
    qkv_full = w_qkv.astype(jnp.float32)
    out_full = w_out.astype(jnp.float32)
    up_full = w_up.astype(jnp.float32)
    down_full = w_down.astype(jnp.float32)
    mod_rows = mod_table.astype(jnp.float32)[timestep]

    def one_clip(weight_sums, inputs):
        tok_clip, mod_row, cot_clip = inputs
        result, pullback = jax.vjp(clip_forward, tok_clip, mod_row, qkv_full, out_full, up_full, down_full)
        grads = pullback(cot_clip)
        weight_sums = tuple((total_sum + piece_grad for total_sum, piece_grad in zip(weight_sums, grads[2:])))
        return (weight_sums, (result, grads[0], grads[1]))
    start_sums = (jnp.zeros(qkv_full.shape, jnp.float32), jnp.zeros(out_full.shape, jnp.float32), jnp.zeros(up_full.shape, jnp.float32), jnp.zeros(down_full.shape, jnp.float32))
    weight_sums, outputs = lax.scan(one_clip, start_sums, (tokens.astype(jnp.float32), mod_rows, cotangent.astype(jnp.float32)))
    output, grad_tokens, mod_grads = outputs
    grad_table = jnp.zeros((NT, 6 * D), jnp.float32).at[timestep].add(mod_grads)
    return (output, grad_tokens, grad_table, weight_sums[0], weight_sums[1], weight_sums[2], weight_sums[3])
```

```python
from functools import partial

import jax
import jax.numpy as jnp
from jax import lax
from jax.sharding import PartitionSpec as P

HEADS = 16
HEAD_DIM = 72
EPS = 1e-06
HIGHEST = lax.Precision.HIGHEST
BF16 = jnp.bfloat16
F32 = jnp.float32


def norm_rows(values):
    center = values - jnp.mean(values, axis=-1, keepdims=True)
    spread = jnp.mean(center * center, axis=-1, keepdims=True)
    root_inv = lax.rsqrt(spread + EPS)
    return (center * root_inv, root_inv)


def norm_back(d_normed, normed, root_inv):
    mean_one = jnp.mean(d_normed, axis=-1, keepdims=True)
    mean_two = jnp.mean(d_normed * normed, axis=-1, keepdims=True)
    return root_inv * (d_normed - mean_one - normed * mean_two)


def dot_nn(left, right):
    return jnp.dot(left, right, preferred_element_type=F32)


def dot_tn(left, right):
    return lax.dot_general(left, right, (((0,), (0,)), ((), ())), preferred_element_type=F32)


def dot_nt(left, right):
    return lax.dot_general(left, right, (((1,), (1,)), ((), ())), preferred_element_type=F32)


class Ring:
    def __init__(self, size, index):
        self.size = size
        self.order = list(range(0, size, 2)) + list(range(size - 1, 0, -2))
        place = [0] * size
        for spot, member in enumerate(self.order):
            place[member] = spot
        self.spot = jnp.array(place, jnp.int32)[index]
        self.table = jnp.array(self.order, jnp.int32)
        self.ahead = [(self.order[i], self.order[(i + 1) % size]) for i in range(size)]
        self.back = [(right, left) for left, right in self.ahead]

    def member(self, offset):
        return self.table[(self.spot + offset) % self.size]

    def gather(self, chunk):
        half = self.size // 2
        cut = chunk.shape[0] // 2
        out = jnp.zeros((self.size,) + chunk.shape, chunk.dtype)

        def put(out, piece, offset, row=0):
            return lax.dynamic_update_slice(out, piece[None], (self.member(offset), row, 0))

        out = put(out, chunk, 0)
        fore = rear = chunk
        for step in range(1, half):
            fore = lax.ppermute(fore, "dp", self.ahead)
            rear = lax.ppermute(rear, "dp", self.back)
            out = put(put(out, fore, -step), rear, step)
        fore = lax.ppermute(fore[:cut], "dp", self.ahead)
        rear = lax.ppermute(rear[cut:], "dp", self.back)
        return put(put(out, fore, half), rear, half, cut)

    def scatter(self, parts):
        half = self.size // 2
        cut = parts.shape[1] // 2

        def own(offset):
            return lax.dynamic_index_in_dim(parts, self.member(offset), 0, keepdims=False)

        far = own(half)
        fore = lax.ppermute(far[:cut], "dp", self.ahead)
        rear = lax.ppermute(far[cut:], "dp", self.back)
        for step in range(half - 1, 0, -1):
            mine_fore = own(step).astype(F32)
            mine_rear = own(-step).astype(F32)
            if step == half - 1:
                fore = jnp.concatenate([mine_fore[:cut] + fore.astype(F32), mine_fore[cut:]], axis=0)
                rear = jnp.concatenate([mine_rear[:cut], mine_rear[cut:] + rear.astype(F32)], axis=0)
            else:
                fore = mine_fore + fore.astype(F32)
                rear = mine_rear + rear.astype(F32)
            fore = lax.ppermute(fore.astype(BF16), "dp", self.ahead)
            rear = lax.ppermute(rear.astype(BF16), "dp", self.back)
        return own(0).astype(F32) + fore.astype(F32) + rear.astype(F32)


class Group:
    def __init__(self, size, index):
        self.size = size
        self.index = index
        self.bits = []
        bit = size // 2
        while bit:
            self.bits.append(bit)
            bit //= 2

    def swap(self, values, bit):
        return lax.ppermute(values, "blk", [(i, i ^ bit) for i in range(self.size)])

    def exchange(self, pieces):
        if self.size > 4:
            return lax.all_to_all(pieces, "blk", 0, 0, tiled=True)
        got = []
        for r in range(self.size):
            piece = lax.dynamic_index_in_dim(pieces, self.index ^ r, 0, keepdims=False)
            got.append(self.swap(piece, r) if r else piece)
        bit = 1
        while bit < self.size:
            odd = (self.index & bit) != 0
            got = [jnp.where(odd, got[r ^ bit], got[r]) for r in range(self.size)]
            bit *= 2
        return jnp.stack(got)

    def gather(self, block, bits=None):
        for bit in self.bits if bits is None else bits:
            block = jnp.concatenate([block, self.swap(block, bit)], axis=0)
        return block

    def scatter(self, parts, share):
        for bit in reversed(self.bits[1:]):
            half = parts.shape[0] // 2
            parts = parts[:half] + self.swap(parts[half:].astype(BF16), bit).astype(F32)
        top = self.bits[0]
        if share:
            return parts + self.swap(parts.astype(BF16), top)[::-1].astype(F32)
        return parts[:1] + self.swap(parts[1:].astype(BF16), top).astype(F32)


def local(tokens, timestep, mod_table, w_qkv, w_out, w_up, w_down, cotangent):
    frames, patches, width = tokens.shape[1:]
    nd = lax.axis_size("dp")
    nb = lax.axis_size("blk")
    dp = lax.axis_index("dp")
    blk = lax.axis_index("blk")
    ring = Ring(nd, dp)
    group = Group(nb, blk)
    rows = nb * frames * patches
    scale = HEAD_DIM ** (-0.5)
    heads = HEADS // nb
    deep = width // nb
    ff = w_down.shape[0]
    hidden = w_up.shape[1]
    out_cols = w_out.shape[1]

    columns = w_qkv.shape[1] // HEAD_DIM
    slots = -(-columns // nb)
    offset = (columns * dp) % nb
    qkv_t = w_qkv.T.reshape(columns, HEAD_DIM, deep)
    qkv_pos = jnp.zeros((2 * slots * nb, HEAD_DIM, deep), BF16)
    qkv_pos = lax.dynamic_update_slice(qkv_pos, qkv_t, (offset, 0, 0))
    qkv_pos = qkv_pos[: slots * nb] + qkv_pos[slots * nb :]
    qkv_send = qkv_pos.reshape(slots, nb, HEAD_DIM, deep).transpose(1, 0, 2, 3)
    qkv_send = qkv_send.reshape(nb, slots * HEAD_DIM, deep)
    spread = heads // nb
    if spread:
        out_send = w_out.T.reshape(out_cols, spread, nb, HEAD_DIM).transpose(2, 0, 1, 3)
        out_send = out_send.reshape(nb, out_cols, spread * HEAD_DIM)
    up_send = w_up.T.reshape(nb, hidden // nb, deep)
    many = ff // hidden
    down_send = w_down.T.reshape(out_cols, many, nb, hidden // nb).transpose(2, 0, 1, 3)
    down_send = down_send.reshape(nb, out_cols, many * hidden // nb)
    first = group.exchange(jnp.concatenate([qkv_send, out_send], axis=2) if spread else qkv_send)
    up_got = group.exchange(up_send)
    down_got = group.exchange(down_send)
    qkv_own = first[:, :, :deep].transpose(1, 0, 2).reshape(slots * HEAD_DIM, width)
    out_own = first[:, :, deep:].transpose(1, 0, 2).reshape(out_cols, heads * HEAD_DIM) if spread else w_out.T
    up_own = up_got.transpose(1, 0, 2).reshape(hidden // nb, width)
    down_own = down_got.transpose(1, 0, 2).reshape(out_cols, nd * hidden // nb)

    token_all = group.gather(tokens)
    cot_all = group.gather(cotangent)

    picker = (timestep[:, None] == jnp.arange(mod_table.shape[0], dtype=jnp.int32)[None, :]).astype(BF16)
    table_cols = dot_nn(picker, mod_table).astype(BF16)
    piece = table_cols.shape[1]
    mods_send = jnp.broadcast_to(table_cols[:, None, :], (nd, nb, piece)).reshape(nd * nb, piece)
    mod_row = lax.all_to_all(mods_send, ("dp", "blk"), 0, 0, tiled=True).reshape(6, width).astype(F32)
    shift_a, scale_a, gate_a, shift_b, scale_b, gate_b = (mod_row[i] for i in range(6))

    first_all = ring.gather(jnp.concatenate([qkv_own, out_own], axis=1))
    up_full = ring.gather(up_own).reshape(ff, width)
    down_full = ring.gather(down_own).reshape(width, ff)
    out_full = first_all[:, :, width:].reshape(width, heads * HEAD_DIM)
    wanted = blk + nb * jnp.arange(3 * heads, dtype=jnp.int32)
    holder = wanted // columns
    place = ((wanted - columns * holder + (columns * holder) % nb) % (slots * nb)) // nb
    slot_of = holder * slots + place
    qkv_slots = first_all[:, :, :width].reshape(nd * slots, HEAD_DIM, width)
    qkv_full = jnp.take(qkv_slots, slot_of, axis=0).reshape(3 * heads * HEAD_DIM, width)

    inputs = token_all.reshape(rows, width).astype(F32)
    normed_a, root_a = norm_rows(inputs)
    hidden_a = (normed_a * (1.0 + scale_a) + shift_a).astype(BF16)
    projected = dot_nt(hidden_a, qkv_full).astype(BF16)

    def by_head(values, parts):
        split = values.reshape(nb, frames, patches, parts, heads, HEAD_DIM)
        split = split.transpose(3, 1, 4, 0, 2, 5)
        return split.reshape(parts, frames, heads, nb * patches, HEAD_DIM)

    def by_row(values):
        split = values.reshape(-1, frames, heads, nb, patches, HEAD_DIM)
        return split.transpose(3, 1, 4, 0, 2, 5).reshape(rows, -1)

    query, keys, values = by_head(projected, 3)
    scores = jnp.einsum("fhqe,fhke->fhqk", query, keys, preferred_element_type=F32) * scale
    top = jnp.max(scores, axis=-1, keepdims=True)
    weights = jnp.exp(scores - top)
    probs = weights / jnp.sum(weights, axis=-1, keepdims=True)
    probs_low = probs.astype(BF16)
    attended = jnp.einsum("fhqk,fhke->fhqe", probs_low, values, preferred_element_type=F32)
    attn_low = by_row(attended).astype(BF16)
    share = 2 * frames * patches
    own = frames * patches

    def blocks(partial_sum):
        return partial_sum.reshape(nb, own, width)

    branch_a = group.scatter(blocks(dot_nt(attn_low, out_full)), True).reshape(share, width)
    middle = inputs[:share] + gate_a * branch_a
    normed_b, root_b = norm_rows(middle)
    hidden_low = (normed_b * (1.0 + scale_b) + shift_b).astype(BF16)
    hidden_b = group.gather(hidden_low.reshape(2, own, width), group.bits[1:]).reshape(rows, width)
    pre_act = dot_nt(hidden_b, up_full)
    activated, gelu_back = jax.vjp(partial(jax.nn.gelu, approximate=True), pre_act)
    act_low = activated.astype(BF16)
    grad_in = cot_all.reshape(rows, width).astype(F32)
    d_branch_b = (gate_b * grad_in).astype(BF16)
    grad_down = dot_tn(d_branch_b, act_low).astype(BF16)
    down_sum = ring.scatter(grad_down.reshape(nd, out_cols, ff))
    d_act = dot_nn(d_branch_b, down_full)
    d_pre = gelu_back(d_act)[0].astype(BF16)
    grad_up = dot_tn(d_pre, hidden_b).astype(BF16)
    up_sum = ring.scatter(grad_up.reshape(nd, hidden // nb, width))
    d_hidden_b = group.scatter(blocks(dot_nn(d_pre, up_full)), True).reshape(share, width)
    branch_b = group.scatter(blocks(dot_nt(act_low, down_full)), False).reshape(own, width)
    output = (middle[:own] + gate_b * branch_b).reshape(tokens.shape)
    d_gate_b = jnp.sum(grad_in[:own] * branch_b, axis=0)
    d_shift_b = jnp.sum(d_hidden_b[:own], axis=0)
    d_scale_b = jnp.sum(d_hidden_b[:own] * normed_b[:own], axis=0)
    d_middle = grad_in[:share] + norm_back(d_hidden_b * (1.0 + scale_b), normed_b, root_b)
    d_gate_a = jnp.sum(d_middle[:own] * branch_a[:own], axis=0)
    d_branch_a = (gate_a * d_middle).astype(BF16).reshape(2, own, width)
    d_branch_a = group.gather(d_branch_a, group.bits[1:]).reshape(rows, width)
    grad_out = dot_tn(d_branch_a, attn_low).astype(BF16)
    d_attended = dot_nn(d_branch_a, out_full).astype(BF16)
    d_att = by_head(d_attended, 1)[0]
    delta = jnp.sum(d_att.astype(F32) * attended, axis=-1, keepdims=True)
    d_probs = jnp.einsum("fhqe,fhke->fhqk", d_att, values, preferred_element_type=F32)
    d_scores = (probs * (d_probs - delta)).astype(BF16)
    d_query = jnp.einsum("fhqk,fhke->fhqe", d_scores, keys, preferred_element_type=F32) * scale
    d_key = jnp.einsum("fhqk,fhqe->fhke", d_scores, query, preferred_element_type=F32) * scale
    d_value = jnp.einsum("fhqk,fhqe->fhke", probs_low, d_att, preferred_element_type=F32)
    d_projected = by_row(jnp.stack([d_query, d_key, d_value]).astype(BF16))
    grad_qkv = dot_tn(d_projected, hidden_a).astype(BF16).reshape(3 * heads, HEAD_DIM, width)
    grad_slots = jnp.zeros((nd * slots, HEAD_DIM, width), BF16).at[slot_of].set(grad_qkv)
    grad_first = jnp.concatenate(
        [
            grad_slots.reshape(nd, slots * HEAD_DIM, width),
            grad_out.reshape(nd, out_cols, heads * HEAD_DIM),
        ],
        axis=2,
    )
    first_sum = ring.scatter(grad_first)
    d_hidden_a = group.scatter(blocks(dot_nn(d_projected, qkv_full)), False).reshape(own, width)
    d_shift_a = jnp.sum(d_hidden_a, axis=0)
    d_scale_a = jnp.sum(d_hidden_a * normed_a[:own], axis=0)
    d_normed = norm_back(d_hidden_a * (1.0 + scale_a), normed_a[:own], root_a[:own])
    grad_tokens = (d_middle[:own] + d_normed).reshape(tokens.shape)

    d_mod = jnp.concatenate([d_shift_a, d_scale_a, d_gate_a, d_shift_b, d_scale_b, d_gate_b])
    mod_got = lax.all_to_all(d_mod.reshape(nd * nb, piece), ("dp", "blk"), 0, 0, tiled=True)
    mod_sums = jnp.sum(mod_got.reshape(nd, nb, piece), axis=1)
    grad_table = lax.dot_general(
        picker.astype(F32),
        mod_sums,
        (((0,), (0,)), ((), ())),
        precision=HIGHEST,
        preferred_element_type=F32,
    )

    up_back = group.exchange(up_sum.astype(BF16).reshape(hidden // nb, nb, deep).transpose(1, 0, 2))
    final_up = up_back.reshape(hidden, deep).T.astype(F32)
    down_back = down_sum.astype(BF16).reshape(out_cols, nb, many, hidden // nb).transpose(1, 0, 2, 3)
    down_back = group.exchange(down_back.reshape(nb, out_cols, many * hidden // nb))
    down_back = down_back.reshape(nb, out_cols, many, hidden // nb).transpose(2, 0, 3, 1)
    final_down = down_back.reshape(ff, out_cols).astype(F32)
    first_low = first_sum.astype(BF16)
    qkv_back = first_low[:, :width].reshape(slots * HEAD_DIM, nb, deep).transpose(1, 0, 2)
    out_back = first_low[:, width:]
    if spread:
        out_back = out_back.reshape(out_cols, nb, spread * HEAD_DIM).transpose(1, 0, 2)
        back = group.exchange(jnp.concatenate([qkv_back, out_back], axis=2))
        out_back = back[:, :, deep:].reshape(nb, out_cols, spread, HEAD_DIM).transpose(2, 0, 3, 1)
        final_out = out_back.reshape(deep, out_cols).astype(F32)
    else:
        back = group.exchange(qkv_back)
        final_out = out_back.T.astype(F32)
    qkv_back = back[:, :, :deep].reshape(nb, slots, HEAD_DIM, deep).transpose(1, 0, 2, 3)
    qkv_back = qkv_back.reshape(slots * nb, HEAD_DIM, deep)
    qkv_back = lax.dynamic_slice(
        jnp.concatenate([qkv_back, qkv_back], axis=0), (offset, 0, 0), (columns, HEAD_DIM, deep)
    )
    final_qkv = qkv_back.reshape(columns * HEAD_DIM, deep).T.astype(F32)
    return (output, grad_tokens, grad_table, final_qkv, final_out, final_up, final_down)


def solution(mesh):
    in_specs = (
        P("dp", None, "blk", None),
        P(),
        P(None, ("dp", "blk")),
        P("blk", "dp"),
        P("blk", "dp"),
        P("blk", "dp"),
        P("blk", "dp"),
        P("dp", None, "blk", None),
    )
    out_specs = (
        P("dp", None, "blk", None),
        P("dp", None, "blk", None),
        P(None, ("dp", "blk")),
        P("blk", "dp"),
        P("blk", "dp"),
        P("blk", "dp"),
        P("blk", "dp"),
    )
    return jax.shard_map(local, mesh=mesh, in_specs=in_specs, out_specs=out_specs, check_vma=False)
```

```python
import math
from functools import partial

import jax
import jax.numpy as jnp
from jax import lax
from jax.experimental import pallas as pl
from jax.experimental.pallas import tpu as pltpu
from jax.sharding import PartitionSpec as P

HEADS = 16
HEAD_DIM = 72
EPS = 1e-06
HIGHEST = lax.Precision.HIGHEST
BF16 = jnp.bfloat16
F32 = jnp.float32


def norm_rows(values):
    center = values - jnp.mean(values, axis=-1, keepdims=True)
    spread = jnp.mean(center * center, axis=-1, keepdims=True)
    root_inv = lax.rsqrt(spread + EPS)
    return (center * root_inv, root_inv)


def norm_back(d_normed, normed, root_inv):
    mean_one = jnp.mean(d_normed, axis=-1, keepdims=True)
    mean_two = jnp.mean(d_normed * normed, axis=-1, keepdims=True)
    return root_inv * (d_normed - mean_one - normed * mean_two)


def dot_nn(left, right):
    return jnp.dot(left, right, preferred_element_type=F32)


def dot_tn(left, right):
    return lax.dot_general(left, right, (((0,), (0,)), ((), ())), preferred_element_type=F32)


def dot_nt(left, right):
    return lax.dot_general(left, right, (((1,), (1,)), ((), ())), preferred_element_type=F32)


class Ring:
    def __init__(self, size, index):
        self.size = size
        self.order = list(range(0, size, 2)) + list(range(size - 1, 0, -2))
        place = [0] * size
        for spot, member in enumerate(self.order):
            place[member] = spot
        self.spot = jnp.array(place, jnp.int32)[index]
        self.table = jnp.array(self.order, jnp.int32)
        self.ahead = [(self.order[i], self.order[(i + 1) % size]) for i in range(size)]
        self.back = [(right, left) for left, right in self.ahead]

    def member(self, offset):
        return self.table[(self.spot + offset) % self.size]

    def gather(self, chunk):
        half = self.size // 2
        cut = chunk.shape[0] // 2
        out = jnp.zeros((self.size,) + chunk.shape, chunk.dtype)

        def put(out, piece, offset, row=0):
            return lax.dynamic_update_slice(out, piece[None], (self.member(offset), row, 0))

        out = put(out, chunk, 0)
        fore = rear = chunk
        for step in range(1, half):
            fore = lax.ppermute(fore, "dp", self.ahead)
            rear = lax.ppermute(rear, "dp", self.back)
            out = put(put(out, fore, -step), rear, step)
        fore = lax.ppermute(fore[:cut], "dp", self.ahead)
        rear = lax.ppermute(rear[cut:], "dp", self.back)
        return put(put(out, fore, half), rear, half, cut)

    def chunks(self, chunk, forward, holds={}):
        got = [chunk]
        fore = rear = chunk
        half = self.size // 2
        for step in range(1, half + 1):
            if step in holds:
                fore, rear = after((fore, rear), *holds[step])
            if step < half or forward:
                fore = lax.ppermute(fore, "dp", self.ahead)
                got.append(fore)
            if step < half or not forward:
                rear = lax.ppermute(rear, "dp", self.back)
                got.append(rear)
        return got

    def sums(self, parts, forward):
        half = self.size // 2

        def add(mine, got):
            return mine if got is None else (mine.astype(F32) + got.astype(F32)).astype(BF16)

        far = parts[self.size - 1]
        fore, rear = (far, None) if forward else (None, far)
        for step in range(half - 1, -1, -1):
            if fore is not None:
                fore = lax.ppermute(fore, "dp", self.ahead)
            if rear is not None:
                rear = lax.ppermute(rear, "dp", self.back)
            if step:
                fore = add(parts[2 * step], fore)
                rear = add(parts[2 * step - 1], rear)
        return parts[0], fore, rear

    def scatter(self, parts):
        half = self.size // 2
        cut = parts.shape[1] // 2

        def own(offset):
            return lax.dynamic_index_in_dim(parts, self.member(offset), 0, keepdims=False)

        far = own(half)
        fore = lax.ppermute(far[:cut], "dp", self.ahead)
        rear = lax.ppermute(far[cut:], "dp", self.back)
        for step in range(half - 1, 0, -1):
            mine_fore = own(step).astype(F32)
            mine_rear = own(-step).astype(F32)
            if step == half - 1:
                fore = jnp.concatenate([mine_fore[:cut] + fore.astype(F32), mine_fore[cut:]], axis=0)
                rear = jnp.concatenate([mine_rear[:cut], mine_rear[cut:] + rear.astype(F32)], axis=0)
            else:
                fore = mine_fore + fore.astype(F32)
                rear = mine_rear + rear.astype(F32)
            fore = lax.ppermute(fore.astype(BF16), "dp", self.ahead)
            rear = lax.ppermute(rear.astype(BF16), "dp", self.back)
        return own(0).astype(F32) + fore.astype(F32) + rear.astype(F32)


class Group:
    def __init__(self, size, index):
        self.size = size
        self.index = index
        self.bits = []
        bit = size // 2
        while bit:
            self.bits.append(bit)
            bit //= 2

    def swap(self, values, bit):
        return lax.ppermute(values, "blk", [(i, i ^ bit) for i in range(self.size)])

    def exchange(self, pieces):
        if self.size > 4:
            return lax.all_to_all(pieces, "blk", 0, 0, tiled=True)
        got = []
        for r in range(self.size):
            piece = lax.dynamic_index_in_dim(pieces, self.index ^ r, 0, keepdims=False)
            got.append(self.swap(piece, r) if r else piece)
        bit = 1
        while bit < self.size:
            odd = (self.index & bit) != 0
            got = [jnp.where(odd, got[r ^ bit], got[r]) for r in range(self.size)]
            bit *= 2
        return jnp.stack(got)

    def gather(self, block, bits=None):
        for bit in self.bits if bits is None else bits:
            block = jnp.concatenate([block, self.swap(block, bit)], axis=0)
        return block

    def scatter(self, parts, share):
        for bit in reversed(self.bits[1:]):
            half = parts.shape[0] // 2
            parts = parts[:half] + self.swap(parts[half:].astype(BF16), bit).astype(F32)
        top = self.bits[0]
        if share:
            return parts + self.swap(parts.astype(BF16), top)[::-1].astype(F32)
        return parts[:1] + self.swap(parts[1:].astype(BF16), top).astype(F32)


def local_plain(tokens, timestep, mod_table, w_qkv, w_out, w_up, w_down, cotangent):
    frames, patches, width = tokens.shape[1:]
    nd = lax.axis_size("dp")
    nb = lax.axis_size("blk")
    dp = lax.axis_index("dp")
    blk = lax.axis_index("blk")
    ring = Ring(nd, dp)
    group = Group(nb, blk)
    rows = nb * frames * patches
    scale = HEAD_DIM ** (-0.5)
    heads = HEADS // nb
    deep = width // nb
    ff = w_down.shape[0]
    hidden = w_up.shape[1]
    out_cols = w_out.shape[1]

    columns = w_qkv.shape[1] // HEAD_DIM
    slots = -(-columns // nb)
    offset = (columns * dp) % nb
    qkv_t = w_qkv.T.reshape(columns, HEAD_DIM, deep)
    qkv_pos = jnp.zeros((2 * slots * nb, HEAD_DIM, deep), BF16)
    qkv_pos = lax.dynamic_update_slice(qkv_pos, qkv_t, (offset, 0, 0))
    qkv_pos = qkv_pos[: slots * nb] + qkv_pos[slots * nb :]
    qkv_send = qkv_pos.reshape(slots, nb, HEAD_DIM, deep).transpose(1, 0, 2, 3)
    qkv_send = qkv_send.reshape(nb, slots * HEAD_DIM, deep)
    spread = heads // nb
    if spread:
        out_send = w_out.T.reshape(out_cols, spread, nb, HEAD_DIM).transpose(2, 0, 1, 3)
        out_send = out_send.reshape(nb, out_cols, spread * HEAD_DIM)
    up_send = w_up.T.reshape(nb, hidden // nb, deep)
    many = ff // hidden
    down_send = w_down.T.reshape(out_cols, many, nb, hidden // nb).transpose(2, 0, 1, 3)
    down_send = down_send.reshape(nb, out_cols, many * hidden // nb)
    first = group.exchange(jnp.concatenate([qkv_send, out_send], axis=2) if spread else qkv_send)
    up_got = group.exchange(up_send)
    down_got = group.exchange(down_send)
    qkv_own = first[:, :, :deep].transpose(1, 0, 2).reshape(slots * HEAD_DIM, width)
    out_own = first[:, :, deep:].transpose(1, 0, 2).reshape(out_cols, heads * HEAD_DIM) if spread else w_out.T
    up_own = up_got.transpose(1, 0, 2).reshape(hidden // nb, width)
    down_own = down_got.transpose(1, 0, 2).reshape(out_cols, nd * hidden // nb)

    token_all = group.gather(tokens)
    cot_all = group.gather(cotangent)

    picker = (timestep[:, None] == jnp.arange(mod_table.shape[0], dtype=jnp.int32)[None, :]).astype(BF16)
    table_cols = dot_nn(picker, mod_table).astype(BF16)
    piece = table_cols.shape[1]
    mods_send = jnp.broadcast_to(table_cols[:, None, :], (nd, nb, piece)).reshape(nd * nb, piece)
    mod_row = lax.all_to_all(mods_send, ("dp", "blk"), 0, 0, tiled=True).reshape(6, width).astype(F32)
    shift_a, scale_a, gate_a, shift_b, scale_b, gate_b = (mod_row[i] for i in range(6))

    first_all = ring.gather(jnp.concatenate([qkv_own, out_own], axis=1))
    up_full = ring.gather(up_own).reshape(ff, width)
    down_full = ring.gather(down_own).reshape(width, ff)
    out_full = first_all[:, :, width:].reshape(width, heads * HEAD_DIM)
    wanted = blk + nb * jnp.arange(3 * heads, dtype=jnp.int32)
    holder = wanted // columns
    place = ((wanted - columns * holder + (columns * holder) % nb) % (slots * nb)) // nb
    slot_of = holder * slots + place
    qkv_slots = first_all[:, :, :width].reshape(nd * slots, HEAD_DIM, width)
    qkv_full = jnp.take(qkv_slots, slot_of, axis=0).reshape(3 * heads * HEAD_DIM, width)

    inputs = token_all.reshape(rows, width).astype(F32)
    normed_a, root_a = norm_rows(inputs)
    hidden_a = (normed_a * (1.0 + scale_a) + shift_a).astype(BF16)
    projected = dot_nt(hidden_a, qkv_full).astype(BF16)

    def by_head(values, parts):
        split = values.reshape(nb, frames, patches, parts, heads, HEAD_DIM)
        split = split.transpose(3, 1, 4, 0, 2, 5)
        return split.reshape(parts, frames, heads, nb * patches, HEAD_DIM)

    def by_row(values):
        split = values.reshape(-1, frames, heads, nb, patches, HEAD_DIM)
        return split.transpose(3, 1, 4, 0, 2, 5).reshape(rows, -1)

    query, keys, values = by_head(projected, 3)
    scores = jnp.einsum("fhqe,fhke->fhqk", query, keys, preferred_element_type=F32) * scale
    top = jnp.max(scores, axis=-1, keepdims=True)
    weights = jnp.exp(scores - top)
    probs = weights / jnp.sum(weights, axis=-1, keepdims=True)
    probs_low = probs.astype(BF16)
    attended = jnp.einsum("fhqk,fhke->fhqe", probs_low, values, preferred_element_type=F32)
    attn_low = by_row(attended).astype(BF16)
    share = 2 * frames * patches
    own = frames * patches

    def blocks(partial_sum):
        return partial_sum.reshape(nb, own, width)

    branch_a = group.scatter(blocks(dot_nt(attn_low, out_full)), True).reshape(share, width)
    middle = inputs[:share] + gate_a * branch_a
    normed_b, root_b = norm_rows(middle)
    hidden_low = (normed_b * (1.0 + scale_b) + shift_b).astype(BF16)
    hidden_b = group.gather(hidden_low.reshape(2, own, width), group.bits[1:]).reshape(rows, width)
    pre_act = dot_nt(hidden_b, up_full)
    activated, gelu_back = jax.vjp(partial(jax.nn.gelu, approximate=True), pre_act)
    act_low = activated.astype(BF16)
    grad_in = cot_all.reshape(rows, width).astype(F32)
    d_branch_b = (gate_b * grad_in).astype(BF16)
    grad_down = dot_tn(d_branch_b, act_low).astype(BF16)
    down_sum = ring.scatter(grad_down.reshape(nd, out_cols, ff))
    d_act = dot_nn(d_branch_b, down_full)
    d_pre = gelu_back(d_act)[0].astype(BF16)
    grad_up = dot_tn(d_pre, hidden_b).astype(BF16)
    up_sum = ring.scatter(grad_up.reshape(nd, hidden // nb, width))
    d_hidden_b = group.scatter(blocks(dot_nn(d_pre, up_full)), True).reshape(share, width)
    branch_b = group.scatter(blocks(dot_nt(act_low, down_full)), False).reshape(own, width)
    output = (middle[:own] + gate_b * branch_b).reshape(tokens.shape)
    d_gate_b = jnp.sum(grad_in[:own] * branch_b, axis=0)
    d_shift_b = jnp.sum(d_hidden_b[:own], axis=0)
    d_scale_b = jnp.sum(d_hidden_b[:own] * normed_b[:own], axis=0)
    d_middle = grad_in[:share] + norm_back(d_hidden_b * (1.0 + scale_b), normed_b, root_b)
    d_gate_a = jnp.sum(d_middle[:own] * branch_a[:own], axis=0)
    d_branch_a = (gate_a * d_middle).astype(BF16).reshape(2, own, width)
    d_branch_a = group.gather(d_branch_a, group.bits[1:]).reshape(rows, width)
    grad_out = dot_tn(d_branch_a, attn_low).astype(BF16)
    d_attended = dot_nn(d_branch_a, out_full).astype(BF16)
    d_att = by_head(d_attended, 1)[0]
    delta = jnp.sum(d_att.astype(F32) * attended, axis=-1, keepdims=True)
    d_probs = jnp.einsum("fhqe,fhke->fhqk", d_att, values, preferred_element_type=F32)
    d_scores = (probs * (d_probs - delta)).astype(BF16)
    d_query = jnp.einsum("fhqk,fhke->fhqe", d_scores, keys, preferred_element_type=F32) * scale
    d_key = jnp.einsum("fhqk,fhqe->fhke", d_scores, query, preferred_element_type=F32) * scale
    d_value = jnp.einsum("fhqk,fhqe->fhke", probs_low, d_att, preferred_element_type=F32)
    d_projected = by_row(jnp.stack([d_query, d_key, d_value]).astype(BF16))
    grad_qkv = dot_tn(d_projected, hidden_a).astype(BF16).reshape(3 * heads, HEAD_DIM, width)
    grad_slots = jnp.zeros((nd * slots, HEAD_DIM, width), BF16).at[slot_of].set(grad_qkv)
    grad_first = jnp.concatenate(
        [
            grad_slots.reshape(nd, slots * HEAD_DIM, width),
            grad_out.reshape(nd, out_cols, heads * HEAD_DIM),
        ],
        axis=2,
    )
    first_sum = ring.scatter(grad_first)
    d_hidden_a = group.scatter(blocks(dot_nn(d_projected, qkv_full)), False).reshape(own, width)
    d_shift_a = jnp.sum(d_hidden_a, axis=0)
    d_scale_a = jnp.sum(d_hidden_a * normed_a[:own], axis=0)
    d_normed = norm_back(d_hidden_a * (1.0 + scale_a), normed_a[:own], root_a[:own])
    grad_tokens = (d_middle[:own] + d_normed).reshape(tokens.shape)

    d_mod = jnp.concatenate([d_shift_a, d_scale_a, d_gate_a, d_shift_b, d_scale_b, d_gate_b])
    mod_got = lax.all_to_all(d_mod.reshape(nd * nb, piece), ("dp", "blk"), 0, 0, tiled=True)
    mod_sums = jnp.sum(mod_got.reshape(nd, nb, piece), axis=1)
    grad_table = lax.dot_general(
        picker.astype(F32),
        mod_sums,
        (((0,), (0,)), ((), ())),
        precision=HIGHEST,
        preferred_element_type=F32,
    )

    up_back = group.exchange(up_sum.astype(BF16).reshape(hidden // nb, nb, deep).transpose(1, 0, 2))
    final_up = up_back.reshape(hidden, deep).T.astype(F32)
    down_back = down_sum.astype(BF16).reshape(out_cols, nb, many, hidden // nb).transpose(1, 0, 2, 3)
    down_back = group.exchange(down_back.reshape(nb, out_cols, many * hidden // nb))
    down_back = down_back.reshape(nb, out_cols, many, hidden // nb).transpose(2, 0, 3, 1)
    final_down = down_back.reshape(ff, out_cols).astype(F32)
    first_low = first_sum.astype(BF16)
    qkv_back = first_low[:, :width].reshape(slots * HEAD_DIM, nb, deep).transpose(1, 0, 2)
    out_back = first_low[:, width:]
    if spread:
        out_back = out_back.reshape(out_cols, nb, spread * HEAD_DIM).transpose(1, 0, 2)
        back = group.exchange(jnp.concatenate([qkv_back, out_back], axis=2))
        out_back = back[:, :, deep:].reshape(nb, out_cols, spread, HEAD_DIM).transpose(2, 0, 3, 1)
        final_out = out_back.reshape(deep, out_cols).astype(F32)
    else:
        back = group.exchange(qkv_back)
        final_out = out_back.T.astype(F32)
    qkv_back = back[:, :, :deep].reshape(nb, slots, HEAD_DIM, deep).transpose(1, 0, 2, 3)
    qkv_back = qkv_back.reshape(slots * nb, HEAD_DIM, deep)
    qkv_back = lax.dynamic_slice(
        jnp.concatenate([qkv_back, qkv_back], axis=0), (offset, 0, 0), (columns, HEAD_DIM, deep)
    )
    final_qkv = qkv_back.reshape(columns * HEAD_DIM, deep).T.astype(F32)
    return (output, grad_tokens, grad_table, final_qkv, final_out, final_up, final_down)


GELU_IN = 0.7978845608028654
GELU_CUBE = 0.044715
VMEM_LIMIT = 40 << 20


def run_kernel(body, outs, *args, spaces=(), scratch=(), flops=0, name=None):
    places = [pl.ANY if i in spaces else pltpu.VMEM for i in range(len(args))]
    sizes = [jnp.dtype(t).itemsize * math.prod(shape) for shape, t in outs]
    moved = sum(sizes) + sum(a.size * a.dtype.itemsize for a in args)
    return pl.pallas_call(
        body,
        out_shape=[jax.ShapeDtypeStruct(shape, t) for shape, t in outs],
        in_specs=[pl.BlockSpec(memory_space=place) for place in places],
        out_specs=[pl.BlockSpec(memory_space=pltpu.VMEM) for _ in outs],
        scratch_shapes=list(scratch),
        compiler_params=pltpu.CompilerParams(vmem_limit_bytes=VMEM_LIMIT),
        cost_estimate=pl.CostEstimate(flops=flops, bytes_accessed=moved, transcendentals=0),
        name=name,
    )(*args)


def after(value, *others):
    return lax.optimization_barrier((value, *others))[0]


NEAR_FIRST = (0, -1, 1, -2, 2, -3, 3, 4)


def member_at(offset):
    dp = lax.axis_index("dp")
    spot = jnp.where(dp % 2 == 0, dp // 2, 7 - dp // 2)
    at = (spot + offset + 8) % 8
    return jnp.where(at < 4, 2 * at, 15 - 2 * at)


def turn(values):
    return values.astype(F32).T.astype(BF16)


def pack_body(qkv, out, up, down, *refs):
    heads, updown = refs[:4], refs[4:8]
    held_q, held_o, held_u, held_d = refs[8:]
    blk = lax.axis_index("blk")
    offset = (6 * lax.axis_index("dp")) % 4
    held_q[...] = jnp.zeros_like(held_q)
    for i in range(6):
        held_q[i + offset] = turn(qkv[:, 72 * i : 72 * i + 72])
    for t in range(4):
        held_o[t] = out[:, 72 * t : 72 * t + 72]
        held_u[t] = turn(up[:, 144 * t : 144 * t + 144])
        for part in range(2):
            at = 576 * part + 144 * t
            held_d[t, :, 144 * part : 144 * part + 144] = down[:, at : at + 144]
    for r in range(4):
        t = blk ^ r
        heads[r][:, 288:384] = jnp.zeros((144, 96), BF16)
        heads[r][0:72, 0:288] = held_q[t]
        heads[r][72:144, 0:288] = held_q[t + 4]
        heads[r][:, 288:360] = held_o[t]
        updown[r][:, 0:288] = held_u[t]
        updown[r][:, 288:576] = held_d[t]
        updown[r][:, 576:640] = jnp.zeros((144, 64), BF16)


def join_heads_body(*refs):
    pieces, joined, held = refs[:4], refs[4], refs[5]
    blk = lax.axis_index("blk")
    for r in range(4):
        held[blk ^ r] = pieces[r][...]
    joined[:, 1440:1536] = jnp.zeros((144, 96), BF16)
    for s in range(4):
        joined[:, 288 * s : 288 * s + 288] = held[s, :, 0:288]
        joined[:, 1152 + 72 * s : 1224 + 72 * s] = held[s, :, 288:360]


def join_updown_body(*refs):
    pieces, joined, held = refs[:4], refs[4], refs[5]
    blk = lax.axis_index("blk")
    for r in range(4):
        held[blk ^ r] = pieces[r][...]
    for s in range(4):
        joined[0:144, 288 * s : 288 * s + 288] = held[s, :, 0:288]
        joined[144:288, 288 * s : 288 * s + 288] = held[s, :, 288:576]


def hidden_a_body(t0, t1, t2, t3, mod, hidden):
    for i, block in enumerate((t0, t1, t2, t3)):
        for f in range(2):
            normed, _ = norm_rows(block[f].astype(F32))
            row = 256 * f + 64 * i
            hidden[row : row + 64, :] = (normed * (1.0 + mod[1:2, :]) + mod[0:1, :]).astype(BF16)


def load_chunks(chunks, full, sems, rows, lanes):
    copies = []
    for k, chunk in enumerate(chunks):
        at = pl.multiple_of(member_at(NEAR_FIRST[k]) * 144, 144)
        source = chunk.at[pl.ds(*rows), pl.ds(*lanes)]
        copies.append(pltpu.make_async_copy(source, full.at[pl.ds(at, 144), :], sems.at[k]))
    for copy in copies:
        copy.start()
    return copies


def split_halves(total, keep, send):
    for f in range(2):
        keep[128 * f : 128 * f + 128, :] = total[256 * f : 256 * f + 128, :]
        send[128 * f : 128 * f + 128, :] = total[256 * f + 128 : 256 * f + 256, :].astype(BF16)


def split_owners(total, own, far, near, cross):
    for i, block in enumerate((own, far, near, cross)):
        for f in range(2):
            row = 256 * f + 64 * i
            block[64 * f : 64 * f + 64, :] = total[row : row + 64, :].astype(block.dtype)


def join_halves(mine, theirs, full):
    for f in range(2):
        full[256 * f : 256 * f + 128, :] = mine[128 * f : 128 * f + 128, :]
        full[256 * f + 128 : 256 * f + 256, :] = theirs[128 * f : 128 * f + 128, :]


def attend_body(hidden, *refs):
    chunks = refs[:8]
    parts, probs, attended, low, keep, send = refs[8:14]
    full, slots, sems = refs[14:]
    for copy in load_chunks(chunks, full, sems, (0, 144), (0, 1536)):
        copy.wait()
    slots[...] = dot_nt(hidden[...], full[:, 0:1152]).astype(BF16)
    for e in range(4):
        at = 288 * e
        parts[3 * e] = slots[:, at : at + 72]
        parts[3 * e + 1] = slots[:, at + 72 : at + 144] + slots[:, at + 144 : at + 216]
        parts[3 * e + 2] = slots[:, at + 216 : at + 288]
    scale = HEAD_DIM ** (-0.5)
    for f in range(2):
        rows = slice(256 * f, 256 * f + 256)
        for h in range(4):
            scores = dot_nt(parts[h, rows, :], parts[4 + h, rows, :]) * scale
            weights = jnp.exp(scores - jnp.max(scores, axis=-1, keepdims=True))
            prob = weights / jnp.sum(weights, axis=-1, keepdims=True)
            probs[4 * f + h] = prob
            mixed = dot_nn(prob.astype(BF16), parts[8 + h, rows, :])
            attended[h, rows, :] = mixed
            low[rows, 72 * h : 72 * h + 72] = mixed.astype(BF16)
    split_halves(dot_nt(low[...], full[:, 1152:1440]), keep, send)


def middle_body(keep, near, far, t0, t1, mod, hidden, normed, root, branch, middle):
    for f in range(2):
        for i, block in enumerate((t0, t1)):
            rows = slice(128 * f + 64 * i, 128 * f + 64 * i + 64)
            cross = slice(128 * f + 64 * (1 - i), 128 * f + 64 * (1 - i) + 64)
            part = keep[rows, :] + near[rows, :].astype(F32) + far[cross, :].astype(F32)
            mid = block[f].astype(F32) + mod[2:3, :] * part
            norm, inv = norm_rows(mid)
            hidden[rows, :] = (norm * (1.0 + mod[4:5, :]) + mod[3:4, :]).astype(BF16)
            normed[rows, :] = norm
            root[rows, :] = jnp.broadcast_to(inv, (64, 128))
            if i == 0:
                branch[64 * f : 64 * f + 64, :] = part
                middle[64 * f : 64 * f + 64, :] = mid


def mlp_body(mine, theirs, g0, g1, g2, g3, mod, *refs):
    chunks = refs[:8]
    hidden, act, d_branch, d_pre, keep, send = refs[8:14]
    up, down, slope, up_sems, down_sems = refs[14:]
    up_copies = load_chunks(chunks, up, up_sems, (0, 144), (0, 1152))
    down_copies = load_chunks(chunks, down, down_sems, (144, 144), (0, 1152))
    join_halves(mine, theirs, hidden)
    for f in range(2):
        for i, block in enumerate((g0, g1, g2, g3)):
            row = 256 * f + 64 * i
            d_branch[row : row + 64, :] = (mod[5:6, :] * block[f].astype(F32)).astype(BF16)
    for copy in up_copies:
        copy.wait()
    for at in range(0, 512, 128):
        rows = slice(at, at + 128)
        pre = dot_nt(hidden[rows, :], up[...])
        square = pre * pre
        bend = jnp.tanh(GELU_IN * (pre + GELU_CUBE * (square * pre)))
        half = 0.5 * (1.0 + bend)
        act[rows, :] = (pre * half).astype(BF16)
        inner = GELU_IN * (1.0 + (3.0 * GELU_CUBE) * square)
        slope[rows, :] = half + (0.5 * pre) * ((1.0 - bend * bend) * inner)
    for copy in down_copies:
        copy.wait()
    d_pre[...] = (dot_nn(d_branch[...], down[...]) * slope[...]).astype(BF16)
    split_halves(dot_nn(d_pre[...], up[...]), keep, send)


def grad_updown_body(d_pre, hidden, d_branch, act, *refs):
    outs, total = refs[:8], refs[8]
    total[0] = dot_tn(d_pre[...], hidden[...]).astype(BF16)
    total[1] = dot_tn(d_branch[...], act[...]).astype(BF16)
    for k, out in enumerate(outs):
        at = pl.multiple_of(member_at(NEAR_FIRST[k]) * 144, 144)
        out[0:144, :] = total[0, pl.ds(at, 144), :]
        out[144:288, :] = total[1, pl.ds(at, 144), :]


def branch_b_body(act, *refs):
    chunks, owners, full, sems = refs[:8], refs[8:12], refs[12], refs[13]
    for copy in load_chunks(chunks, full, sems, (144, 144), (0, 1152)):
        copy.wait()
    split_owners(dot_nt(act[...], full[...]), *owners)


def d_middle_body(keep, near, far, normed, root, g0, g1, branch, mod, d_low, d_mid, sums):
    d_shift = jnp.zeros((1, 1152), F32)
    d_scale = jnp.zeros((1, 1152), F32)
    d_gate = jnp.zeros((1, 1152), F32)
    for f in range(2):
        for i, block in enumerate((g0, g1)):
            rows = slice(128 * f + 64 * i, 128 * f + 64 * i + 64)
            cross = slice(128 * f + 64 * (1 - i), 128 * f + 64 * (1 - i) + 64)
            d_hidden = keep[rows, :] + near[rows, :].astype(F32) + far[cross, :].astype(F32)
            norm = normed[rows, :]
            back = norm_back(d_hidden * (1.0 + mod[4:5, :]), norm, root[rows, 0:1])
            mid = block[f].astype(F32) + back
            d_low[rows, :] = (mod[2:3, :] * mid).astype(BF16)
            if i == 0:
                own = slice(64 * f, 64 * f + 64)
                d_mid[own, :] = mid
                d_shift = d_shift + jnp.sum(d_hidden, axis=0, keepdims=True)
                d_scale = d_scale + jnp.sum(d_hidden * norm, axis=0, keepdims=True)
                d_gate = d_gate + jnp.sum(mid * branch[own, :], axis=0, keepdims=True)
    sums[0:1, :] = d_gate
    sums[1:2, :] = d_shift
    sums[2:3, :] = d_scale


def d_attend_body(mine, theirs, parts, probs, attended, *refs):
    chunks = refs[:8]
    d_branch, d_slots = refs[8:10]
    full, d_att, sems = refs[10:]
    copies = load_chunks(chunks, full, sems, (0, 144), (1152, 384))
    join_halves(mine, theirs, d_branch)
    for copy in copies:
        copy.wait()
    d_att[...] = dot_nn(d_branch[...], full[...]).astype(BF16)
    scale = HEAD_DIM ** (-0.5)

    def place(rows, m, value):
        e, k = divmod(m, 3)
        low = value.astype(BF16)
        for slot in ((0,), (1, 2), (3,))[k]:
            d_slots[rows, 288 * e + 72 * slot : 288 * e + 72 * slot + 72] = low

    for f in range(2):
        rows = slice(256 * f, 256 * f + 256)
        for h in range(4):
            d_out = d_att[rows, 72 * h : 72 * h + 72]
            delta = jnp.sum(d_out.astype(F32) * attended[h, rows, :], axis=-1, keepdims=True)
            prob = probs[4 * f + h]
            d_prob = dot_nt(d_out, parts[8 + h, rows, :])
            d_score = (prob * (d_prob - delta)).astype(BF16)
            place(rows, h, dot_nn(d_score, parts[4 + h, rows, :]) * scale)
            place(rows, 4 + h, dot_tn(d_score, parts[h, rows, :]) * scale)
            place(rows, 8 + h, dot_tn(prob.astype(BF16), d_out))


def grad_first_body(d_slots, hidden, d_branch, low, *refs):
    outs, total = refs[:8], refs[8]
    total[:, 0:1152] = dot_tn(d_slots[...], hidden[...]).astype(BF16)
    total[:, 1152:1440] = dot_tn(d_branch[...], low[...]).astype(BF16)
    total[:, 1440:1536] = jnp.zeros((1152, 96), BF16)
    for k, out in enumerate(outs):
        at = pl.multiple_of(member_at(NEAR_FIRST[k]) * 144, 144)
        out[...] = total[pl.ds(at, 144), :]


def d_hidden_a_body(d_slots, *refs):
    chunks, owners, full, sems = refs[:8], refs[8:12], refs[12], refs[13]
    for copy in load_chunks(chunks, full, sems, (0, 144), (0, 1152)):
        copy.wait()
    split_owners(dot_nn(d_slots[...], full[...]), *owners)


def output_body(own, far, near, cross, middle, g0, mod, output, d_gate):
    total = jnp.zeros((1, 1152), F32)
    for f in range(2):
        rows = slice(64 * f, 64 * f + 64)
        branch = own[rows, :] + near[rows, :].astype(F32)
        branch = branch + far[rows, :].astype(F32) + cross[rows, :].astype(F32)
        output[f] = middle[rows, :] + mod[5:6, :] * branch
        total = total + jnp.sum(g0[f].astype(F32) * branch, axis=0, keepdims=True)
    d_gate[...] = total


def grad_tokens_body(own, far, near, cross, t0, d_mid, mod, sums_b, d_gate_b, grad, d_mod):
    d_shift = jnp.zeros((1, 1152), F32)
    d_scale = jnp.zeros((1, 1152), F32)
    for f in range(2):
        rows = slice(64 * f, 64 * f + 64)
        norm, inv = norm_rows(t0[f].astype(F32))
        d_hidden = own[rows, :] + near[rows, :].astype(F32)
        d_hidden = d_hidden + far[rows, :].astype(F32) + cross[rows, :].astype(F32)
        grad[f] = d_mid[rows, :] + norm_back(d_hidden * (1.0 + mod[1:2, :]), norm, inv)
        d_shift = d_shift + jnp.sum(d_hidden, axis=0, keepdims=True)
        d_scale = d_scale + jnp.sum(d_hidden * norm, axis=0, keepdims=True)
    d_mod[0:1, :] = d_shift
    d_mod[1:2, :] = d_scale
    d_mod[2:5, :] = sums_b[0:3, :]
    d_mod[5:6, :] = d_gate_b[...]


def cut_updown_body(s0, s1, s2, *refs):
    pieces, held = refs[:4], refs[4]
    blk = lax.axis_index("blk")
    total = s0[...].astype(F32) + s1[...].astype(F32) + s2[...].astype(F32)
    for t in range(4):
        held[t, :, 0:288] = total[0:144, 288 * t : 288 * t + 288].astype(BF16)
        held[t, :, 288:576] = total[144:288, 288 * t : 288 * t + 288].astype(BF16)
        held[t, :, 576:640] = jnp.zeros((144, 64), BF16)
    for r in range(4):
        pieces[r][...] = held[blk ^ r]


def final_updown_body(p0, p1, p2, p3, up, down, held):
    blk = lax.axis_index("blk")
    for r, piece in enumerate((p0, p1, p2, p3)):
        held[blk ^ r] = piece[...]
    for s in range(4):
        up[:, 144 * s : 144 * s + 144] = held[s, :, 0:288].astype(F32).T
        for part in range(2):
            at = 576 * part + 144 * s
            down[:, at : at + 144] = held[s, :, 288 + 144 * part : 432 + 144 * part].astype(F32)


def cut_heads_body(s0, s1, s2, *refs):
    pieces, held = refs[:4], refs[4]
    blk = lax.axis_index("blk")
    total = s0[...].astype(F32) + s1[...].astype(F32) + s2[...].astype(F32)
    for t in range(4):
        held[t, :, 0:288] = total[:, 288 * t : 288 * t + 288].astype(BF16)
        held[t, :, 288:360] = total[:, 1152 + 72 * t : 1224 + 72 * t].astype(BF16)
        held[t, :, 360:384] = jnp.zeros((144, 24), BF16)
    for r in range(4):
        pieces[r][...] = held[blk ^ r]


def final_heads_body(p0, p1, p2, p3, qkv, out, held, placed):
    blk = lax.axis_index("blk")
    offset = (6 * lax.axis_index("dp")) % 4
    for r, piece in enumerate((p0, p1, p2, p3)):
        sender = blk ^ r
        placed[sender] = piece[0:72, 0:288].astype(F32)
        placed[sender + 4] = piece[72:144, 0:288].astype(F32)
        held[sender] = piece[:, 288:360].astype(F32)
    for i in range(6):
        qkv[:, 72 * i : 72 * i + 72] = placed[i + offset].T
    for s in range(4):
        out[:, 72 * s : 72 * s + 72] = held[s]


def vmem(shape, kind=BF16):
    return pltpu.VMEM(shape, kind)


def local_kernels(tokens, timestep, mod_table, w_qkv, w_out, w_up, w_down, cotangent):
    nd, nb = 8, 4
    ring = Ring(nd, lax.axis_index("dp"))
    group = Group(nb, lax.axis_index("blk"))
    width = tokens.shape[3]
    sems = pltpu.SemaphoreType.DMA((8,))
    own_tokens = tokens[0]
    own_cot = cotangent[0]
    full_low = ((512, 1152), BF16)
    half_low = ((256, 1152), BF16)
    half_wide = ((256, 1152), F32)
    own_wide = ((128, 1152), F32)
    owners = [own_wide] + [((128, 1152), BF16)] * 3

    def everyone(block):
        far = group.swap(block, 2)
        return [block, far, group.swap(block, 1), group.swap(far, 1)]

    def send_out(pieces):
        return [pieces[0]] + [group.swap(pieces[r], r) for r in (1, 2, 3)]

    def all_sum(keep, send):
        near = group.swap(send, 1)
        far = group.swap((keep + near.astype(F32)).astype(BF16), 2)
        return keep, near, far

    def own_sum(own, far, near, cross):
        return own, group.swap(far, 2), group.swap(near, 1), group.swap(cross, 3)

    packed = run_kernel(
        pack_body,
        [((144, 384), BF16)] * 4 + [((144, 640), BF16)] * 4,
        w_qkv, w_out.T, w_up, w_down.T,
        scratch=[vmem((8, 72, 288)), vmem((4, 144, 72)), vmem((4, 144, 288)), vmem((4, 144, 288))],
        name="pack",
    )
    heads_got = send_out(packed[:4])
    (first_own,) = run_kernel(
        join_heads_body, [((144, 1536), BF16)], *heads_got, scratch=[vmem((4, 144, 384))], name="join_heads"
    )
    updown_got = send_out(packed[4:])
    (updown_own,) = run_kernel(
        join_updown_body, [((288, 1152), BF16)], *updown_got, scratch=[vmem((4, 144, 640))], name="join_updown"
    )

    picker = (timestep[:, None] == jnp.arange(mod_table.shape[0], dtype=jnp.int32)[None, :]).astype(BF16)
    table_cols = dot_nn(picker, mod_table).astype(BF16)
    piece = table_cols.shape[1]
    mods_send = jnp.broadcast_to(table_cols[:, None, :], (nd, nb, piece)).reshape(nd * nb, piece)
    mods_send = after(mods_send, first_own)
    mod = lax.all_to_all(mods_send, ("dp", "blk"), 0, 0, tiled=True).reshape(6, width).astype(F32)
    token_blocks = everyone(own_tokens)
    cot_blocks = everyone(own_cot)
    (hidden_a,) = run_kernel(hidden_a_body, [full_low], *token_blocks, mod, name="hidden_a")

    first = ring.chunks(first_own, True, holds={2: (mod, updown_own), 3: (hidden_a,)})
    updown = ring.chunks(after(updown_own, first[3], first[4]), False)

    parts, probs, attended, low, keep_a, send_a = run_kernel(
        attend_body,
        [((12, 512, 72), BF16), ((8, 256, 256), F32), ((4, 512, 72), F32), ((512, 288), BF16), half_wide, half_low],
        hidden_a, *first,
        spaces=range(1, 9),
        scratch=[vmem((1152, 1536)), vmem((512, 1152)), sems],
        flops=4 * 10**9,
        name="attend",
    )
    hidden_mine, normed_b, root_b, branch_a, middle = run_kernel(
        middle_body,
        [half_low, half_wide, ((256, 128), F32), own_wide, own_wide],
        *all_sum(keep_a, send_a), *token_blocks[:2], mod,
        name="middle",
    )
    hidden_b, act, d_branch_b, d_pre, keep_d, send_d = run_kernel(
        mlp_body,
        [full_low, full_low, full_low, full_low, half_wide, half_low],
        hidden_mine, group.swap(hidden_mine, 1), *cot_blocks, mod, *updown,
        spaces=range(7, 15),
        scratch=[vmem((1152, 1152)), vmem((1152, 1152)), vmem((512, 1152), F32), sems, sems],
        flops=6 * 10**9,
        name="mlp",
    )
    sums_d = all_sum(keep_d, send_d)
    grad_updown = run_kernel(
        grad_updown_body,
        [((288, 1152), BF16)] * 8,
        d_pre, hidden_b, d_branch_b, act,
        scratch=[vmem((2, 1152, 1152))],
        flops=4 * 10**9,
        name="grad_updown",
    )
    updown_parts = ring.sums(grad_updown, False)
    branch_owners = run_kernel(
        branch_b_body,
        owners,
        act, *updown,
        spaces=range(1, 9),
        scratch=[vmem((1152, 1152)), sems],
        flops=2 * 10**9,
        name="branch_b",
    )
    output, d_gate_b = run_kernel(
        output_body,
        [((2, 64, 1152), F32), ((1, 1152), F32)],
        *own_sum(*branch_owners), middle, own_cot, mod,
        name="output",
    )
    d_low, d_mid, sums_b = run_kernel(
        d_middle_body,
        [half_low, own_wide, ((3, 1152), F32)],
        *sums_d, normed_b, root_b, *cot_blocks[:2], branch_a, mod,
        name="d_middle",
    )
    d_branch_a, d_slots = run_kernel(
        d_attend_body,
        [full_low, full_low],
        d_low, group.swap(d_low, 1), parts, probs, attended, *first,
        spaces=range(5, 13),
        scratch=[vmem((1152, 384)), vmem((512, 384)), sems],
        flops=3 * 10**9,
        name="d_attend",
    )
    grad_first = run_kernel(
        grad_first_body,
        [((144, 1536), BF16)] * 8,
        d_slots, hidden_a, d_branch_a, low,
        scratch=[vmem((1152, 1536))],
        flops=2 * 10**9,
        name="grad_first",
    )
    first_parts = ring.sums(grad_first, True)
    hidden_owners = run_kernel(
        d_hidden_a_body,
        owners,
        d_slots, *first,
        spaces=range(1, 9),
        scratch=[vmem((1152, 1152)), sems],
        flops=2 * 10**9,
        name="d_hidden_a",
    )
    grad_tokens, d_mod = run_kernel(
        grad_tokens_body,
        [((2, 64, 1152), F32), ((6, 1152), F32)],
        *own_sum(*hidden_owners), own_tokens, d_mid, mod, sums_b, d_gate_b,
        name="grad_tokens",
    )
    mod_got = lax.all_to_all(d_mod.reshape(nd * nb, piece), ("dp", "blk"), 0, 0, tiled=True)
    mod_sums = jnp.sum(mod_got.reshape(nd, nb, piece), axis=1)
    grad_table = lax.dot_general(
        picker.astype(F32),
        mod_sums,
        (((0,), (0,)), ((), ())),
        precision=HIGHEST,
        preferred_element_type=F32,
    )
    updown_cut = run_kernel(
        cut_updown_body, [((144, 640), BF16)] * 4, *updown_parts, scratch=[vmem((4, 144, 640))], name="cut_updown"
    )
    final_up, final_down = run_kernel(
        final_updown_body,
        [((288, 576), F32), ((144, 1152), F32)],
        *send_out(updown_cut),
        scratch=[vmem((4, 144, 640))],
        name="final_updown",
    )
    heads_cut = run_kernel(
        cut_heads_body, [((144, 384), BF16)] * 4, *first_parts, scratch=[vmem((4, 144, 384))], name="cut_heads"
    )
    final_qkv, final_out = run_kernel(
        final_heads_body,
        [((288, 432), F32), ((144, 288), F32)],
        *send_out(heads_cut),
        scratch=[vmem((4, 144, 72), F32), vmem((8, 72, 288), F32)],
        name="final_heads",
    )
    return (output[None], grad_tokens[None], grad_table, final_qkv, final_out.T, final_up, final_down.T)


def local(tokens, timestep, mod_table, w_qkv, w_out, w_up, w_down, cotangent):
    sizes = (lax.axis_size("dp"), lax.axis_size("blk"), tokens.shape, w_qkv.shape, w_up.shape, w_down.shape)
    known = (8, 4, (1, 2, 64, 1152), (288, 432), (288, 576), (1152, 144))
    chosen = local_kernels if sizes == known else local_plain
    return chosen(tokens, timestep, mod_table, w_qkv, w_out, w_up, w_down, cotangent)


def solution(mesh):
    in_specs = (
        P("dp", None, "blk", None),
        P(),
        P(None, ("dp", "blk")),
        P("blk", "dp"),
        P("blk", "dp"),
        P("blk", "dp"),
        P("blk", "dp"),
        P("dp", None, "blk", None),
    )
    out_specs = (
        P("dp", None, "blk", None),
        P("dp", None, "blk", None),
        P(None, ("dp", "blk")),
        P("blk", "dp"),
        P("blk", "dp"),
        P("blk", "dp"),
        P("blk", "dp"),
    )
    return jax.shard_map(local, mesh=mesh, in_specs=in_specs, out_specs=out_specs, check_vma=False)
```

```python
import math
from functools import partial

import jax
import jax.numpy as jnp
from jax import lax
from jax.experimental import pallas as pl
from jax.experimental.pallas import tpu as pltpu
from jax.sharding import PartitionSpec as P

HEADS = 16
HEAD_DIM = 72
EPS = 1e-06
HIGHEST = lax.Precision.HIGHEST
BF16 = jnp.bfloat16
F32 = jnp.float32


def norm_rows(values):
    center = values - jnp.mean(values, axis=-1, keepdims=True)
    spread = jnp.mean(center * center, axis=-1, keepdims=True)
    root_inv = lax.rsqrt(spread + EPS)
    return (center * root_inv, root_inv)


def norm_back(d_normed, normed, root_inv):
    mean_one = jnp.mean(d_normed, axis=-1, keepdims=True)
    mean_two = jnp.mean(d_normed * normed, axis=-1, keepdims=True)
    return root_inv * (d_normed - mean_one - normed * mean_two)


def dot_nn(left, right):
    return jnp.dot(left, right, preferred_element_type=F32)


def dot_tn(left, right):
    return lax.dot_general(left, right, (((0,), (0,)), ((), ())), preferred_element_type=F32)


def dot_nt(left, right):
    return lax.dot_general(left, right, (((1,), (1,)), ((), ())), preferred_element_type=F32)


class Ring:
    def __init__(self, size, index):
        self.size = size
        self.order = list(range(0, size, 2)) + list(range(size - 1, 0, -2))
        place = [0] * size
        for spot, member in enumerate(self.order):
            place[member] = spot
        self.spot = jnp.array(place, jnp.int32)[index]
        self.table = jnp.array(self.order, jnp.int32)
        self.ahead = [(self.order[i], self.order[(i + 1) % size]) for i in range(size)]
        self.back = [(right, left) for left, right in self.ahead]

    def member(self, offset):
        return self.table[(self.spot + offset) % self.size]

    def gather(self, chunk):
        half = self.size // 2
        cut = chunk.shape[0] // 2
        out = jnp.zeros((self.size,) + chunk.shape, chunk.dtype)

        def put(out, piece, offset, row=0):
            return lax.dynamic_update_slice(out, piece[None], (self.member(offset), row, 0))

        out = put(out, chunk, 0)
        fore = rear = chunk
        for step in range(1, half):
            fore = lax.ppermute(fore, "dp", self.ahead)
            rear = lax.ppermute(rear, "dp", self.back)
            out = put(put(out, fore, -step), rear, step)
        fore = lax.ppermute(fore[:cut], "dp", self.ahead)
        rear = lax.ppermute(rear[cut:], "dp", self.back)
        return put(put(out, fore, half), rear, half, cut)

    def scatter(self, parts):
        half = self.size // 2
        cut = parts.shape[1] // 2

        def own(offset):
            return lax.dynamic_index_in_dim(parts, self.member(offset), 0, keepdims=False)

        far = own(half)
        fore = lax.ppermute(far[:cut], "dp", self.ahead)
        rear = lax.ppermute(far[cut:], "dp", self.back)
        for step in range(half - 1, 0, -1):
            mine_fore = own(step).astype(F32)
            mine_rear = own(-step).astype(F32)
            if step == half - 1:
                fore = jnp.concatenate([mine_fore[:cut] + fore.astype(F32), mine_fore[cut:]], axis=0)
                rear = jnp.concatenate([mine_rear[:cut], mine_rear[cut:] + rear.astype(F32)], axis=0)
            else:
                fore = mine_fore + fore.astype(F32)
                rear = mine_rear + rear.astype(F32)
            fore = lax.ppermute(fore.astype(BF16), "dp", self.ahead)
            rear = lax.ppermute(rear.astype(BF16), "dp", self.back)
        return own(0).astype(F32) + fore.astype(F32) + rear.astype(F32)


class Group:
    def __init__(self, size, index):
        self.size = size
        self.index = index
        self.bits = []
        bit = size // 2
        while bit:
            self.bits.append(bit)
            bit //= 2

    def swap(self, values, bit):
        return lax.ppermute(values, "blk", [(i, i ^ bit) for i in range(self.size)])

    def exchange(self, pieces):
        if self.size > 4:
            return lax.all_to_all(pieces, "blk", 0, 0, tiled=True)
        got = []
        for r in range(self.size):
            piece = lax.dynamic_index_in_dim(pieces, self.index ^ r, 0, keepdims=False)
            got.append(self.swap(piece, r) if r else piece)
        bit = 1
        while bit < self.size:
            odd = (self.index & bit) != 0
            got = [jnp.where(odd, got[r ^ bit], got[r]) for r in range(self.size)]
            bit *= 2
        return jnp.stack(got)

    def gather(self, block, bits=None):
        for bit in self.bits if bits is None else bits:
            block = jnp.concatenate([block, self.swap(block, bit)], axis=0)
        return block

    def scatter(self, parts, share):
        for bit in reversed(self.bits[1:]):
            half = parts.shape[0] // 2
            parts = parts[:half] + self.swap(parts[half:].astype(BF16), bit).astype(F32)
        top = self.bits[0]
        if share:
            return parts + self.swap(parts.astype(BF16), top)[::-1].astype(F32)
        return parts[:1] + self.swap(parts[1:].astype(BF16), top).astype(F32)


def local_plain(tokens, timestep, mod_table, w_qkv, w_out, w_up, w_down, cotangent):
    frames, patches, width = tokens.shape[1:]
    nd = lax.axis_size("dp")
    nb = lax.axis_size("blk")
    dp = lax.axis_index("dp")
    blk = lax.axis_index("blk")
    ring = Ring(nd, dp)
    group = Group(nb, blk)
    rows = nb * frames * patches
    scale = HEAD_DIM ** (-0.5)
    heads = HEADS // nb
    deep = width // nb
    ff = w_down.shape[0]
    hidden = w_up.shape[1]
    out_cols = w_out.shape[1]

    columns = w_qkv.shape[1] // HEAD_DIM
    slots = -(-columns // nb)
    offset = (columns * dp) % nb
    qkv_t = w_qkv.T.reshape(columns, HEAD_DIM, deep)
    qkv_pos = jnp.zeros((2 * slots * nb, HEAD_DIM, deep), BF16)
    qkv_pos = lax.dynamic_update_slice(qkv_pos, qkv_t, (offset, 0, 0))
    qkv_pos = qkv_pos[: slots * nb] + qkv_pos[slots * nb :]
    qkv_send = qkv_pos.reshape(slots, nb, HEAD_DIM, deep).transpose(1, 0, 2, 3)
    qkv_send = qkv_send.reshape(nb, slots * HEAD_DIM, deep)
    spread = heads // nb
    if spread:
        out_send = w_out.T.reshape(out_cols, spread, nb, HEAD_DIM).transpose(2, 0, 1, 3)
        out_send = out_send.reshape(nb, out_cols, spread * HEAD_DIM)
    up_send = w_up.T.reshape(nb, hidden // nb, deep)
    many = ff // hidden
    down_send = w_down.T.reshape(out_cols, many, nb, hidden // nb).transpose(2, 0, 1, 3)
    down_send = down_send.reshape(nb, out_cols, many * hidden // nb)
    first = group.exchange(jnp.concatenate([qkv_send, out_send], axis=2) if spread else qkv_send)
    up_got = group.exchange(up_send)
    down_got = group.exchange(down_send)
    qkv_own = first[:, :, :deep].transpose(1, 0, 2).reshape(slots * HEAD_DIM, width)
    out_own = first[:, :, deep:].transpose(1, 0, 2).reshape(out_cols, heads * HEAD_DIM) if spread else w_out.T
    up_own = up_got.transpose(1, 0, 2).reshape(hidden // nb, width)
    down_own = down_got.transpose(1, 0, 2).reshape(out_cols, nd * hidden // nb)

    token_all = group.gather(tokens)
    cot_all = group.gather(cotangent)

    picker = (timestep[:, None] == jnp.arange(mod_table.shape[0], dtype=jnp.int32)[None, :]).astype(BF16)
    table_cols = dot_nn(picker, mod_table).astype(BF16)
    piece = table_cols.shape[1]
    mods_send = jnp.broadcast_to(table_cols[:, None, :], (nd, nb, piece)).reshape(nd * nb, piece)
    mod_row = lax.all_to_all(mods_send, ("dp", "blk"), 0, 0, tiled=True).reshape(6, width).astype(F32)
    shift_a, scale_a, gate_a, shift_b, scale_b, gate_b = (mod_row[i] for i in range(6))

    first_all = ring.gather(jnp.concatenate([qkv_own, out_own], axis=1))
    up_full = ring.gather(up_own).reshape(ff, width)
    down_full = ring.gather(down_own).reshape(width, ff)
    out_full = first_all[:, :, width:].reshape(width, heads * HEAD_DIM)
    wanted = blk + nb * jnp.arange(3 * heads, dtype=jnp.int32)
    holder = wanted // columns
    place = ((wanted - columns * holder + (columns * holder) % nb) % (slots * nb)) // nb
    slot_of = holder * slots + place
    qkv_slots = first_all[:, :, :width].reshape(nd * slots, HEAD_DIM, width)
    qkv_full = jnp.take(qkv_slots, slot_of, axis=0).reshape(3 * heads * HEAD_DIM, width)

    inputs = token_all.reshape(rows, width).astype(F32)
    normed_a, root_a = norm_rows(inputs)
    hidden_a = (normed_a * (1.0 + scale_a) + shift_a).astype(BF16)
    projected = dot_nt(hidden_a, qkv_full).astype(BF16)

    def by_head(values, parts):
        split = values.reshape(nb, frames, patches, parts, heads, HEAD_DIM)
        split = split.transpose(3, 1, 4, 0, 2, 5)
        return split.reshape(parts, frames, heads, nb * patches, HEAD_DIM)

    def by_row(values):
        split = values.reshape(-1, frames, heads, nb, patches, HEAD_DIM)
        return split.transpose(3, 1, 4, 0, 2, 5).reshape(rows, -1)

    query, keys, values = by_head(projected, 3)
    scores = jnp.einsum("fhqe,fhke->fhqk", query, keys, preferred_element_type=F32) * scale
    top = jnp.max(scores, axis=-1, keepdims=True)
    weights = jnp.exp(scores - top)
    probs = weights / jnp.sum(weights, axis=-1, keepdims=True)
    probs_low = probs.astype(BF16)
    attended = jnp.einsum("fhqk,fhke->fhqe", probs_low, values, preferred_element_type=F32)
    attn_low = by_row(attended).astype(BF16)
    share = 2 * frames * patches
    own = frames * patches

    def blocks(partial_sum):
        return partial_sum.reshape(nb, own, width)

    branch_a = group.scatter(blocks(dot_nt(attn_low, out_full)), True).reshape(share, width)
    middle = inputs[:share] + gate_a * branch_a
    normed_b, root_b = norm_rows(middle)
    hidden_low = (normed_b * (1.0 + scale_b) + shift_b).astype(BF16)
    hidden_b = group.gather(hidden_low.reshape(2, own, width), group.bits[1:]).reshape(rows, width)
    pre_act = dot_nt(hidden_b, up_full)
    activated, gelu_back = jax.vjp(partial(jax.nn.gelu, approximate=True), pre_act)
    act_low = activated.astype(BF16)
    grad_in = cot_all.reshape(rows, width).astype(F32)
    d_branch_b = (gate_b * grad_in).astype(BF16)
    grad_down = dot_tn(d_branch_b, act_low).astype(BF16)
    down_sum = ring.scatter(grad_down.reshape(nd, out_cols, ff))
    d_act = dot_nn(d_branch_b, down_full)
    d_pre = gelu_back(d_act)[0].astype(BF16)
    grad_up = dot_tn(d_pre, hidden_b).astype(BF16)
    up_sum = ring.scatter(grad_up.reshape(nd, hidden // nb, width))
    d_hidden_b = group.scatter(blocks(dot_nn(d_pre, up_full)), True).reshape(share, width)
    branch_b = group.scatter(blocks(dot_nt(act_low, down_full)), False).reshape(own, width)
    output = (middle[:own] + gate_b * branch_b).reshape(tokens.shape)
    d_gate_b = jnp.sum(grad_in[:own] * branch_b, axis=0)
    d_shift_b = jnp.sum(d_hidden_b[:own], axis=0)
    d_scale_b = jnp.sum(d_hidden_b[:own] * normed_b[:own], axis=0)
    d_middle = grad_in[:share] + norm_back(d_hidden_b * (1.0 + scale_b), normed_b, root_b)
    d_gate_a = jnp.sum(d_middle[:own] * branch_a[:own], axis=0)
    d_branch_a = (gate_a * d_middle).astype(BF16).reshape(2, own, width)
    d_branch_a = group.gather(d_branch_a, group.bits[1:]).reshape(rows, width)
    grad_out = dot_tn(d_branch_a, attn_low).astype(BF16)
    d_attended = dot_nn(d_branch_a, out_full).astype(BF16)
    d_att = by_head(d_attended, 1)[0]
    delta = jnp.sum(d_att.astype(F32) * attended, axis=-1, keepdims=True)
    d_probs = jnp.einsum("fhqe,fhke->fhqk", d_att, values, preferred_element_type=F32)
    d_scores = (probs * (d_probs - delta)).astype(BF16)
    d_query = jnp.einsum("fhqk,fhke->fhqe", d_scores, keys, preferred_element_type=F32) * scale
    d_key = jnp.einsum("fhqk,fhqe->fhke", d_scores, query, preferred_element_type=F32) * scale
    d_value = jnp.einsum("fhqk,fhqe->fhke", probs_low, d_att, preferred_element_type=F32)
    d_projected = by_row(jnp.stack([d_query, d_key, d_value]).astype(BF16))
    grad_qkv = dot_tn(d_projected, hidden_a).astype(BF16).reshape(3 * heads, HEAD_DIM, width)
    grad_slots = jnp.zeros((nd * slots, HEAD_DIM, width), BF16).at[slot_of].set(grad_qkv)
    grad_first = jnp.concatenate(
        [
            grad_slots.reshape(nd, slots * HEAD_DIM, width),
            grad_out.reshape(nd, out_cols, heads * HEAD_DIM),
        ],
        axis=2,
    )
    first_sum = ring.scatter(grad_first)
    d_hidden_a = group.scatter(blocks(dot_nn(d_projected, qkv_full)), False).reshape(own, width)
    d_shift_a = jnp.sum(d_hidden_a, axis=0)
    d_scale_a = jnp.sum(d_hidden_a * normed_a[:own], axis=0)
    d_normed = norm_back(d_hidden_a * (1.0 + scale_a), normed_a[:own], root_a[:own])
    grad_tokens = (d_middle[:own] + d_normed).reshape(tokens.shape)

    d_mod = jnp.concatenate([d_shift_a, d_scale_a, d_gate_a, d_shift_b, d_scale_b, d_gate_b])
    mod_got = lax.all_to_all(d_mod.reshape(nd * nb, piece), ("dp", "blk"), 0, 0, tiled=True)
    mod_sums = jnp.sum(mod_got.reshape(nd, nb, piece), axis=1)
    grad_table = lax.dot_general(
        picker.astype(F32),
        mod_sums,
        (((0,), (0,)), ((), ())),
        precision=HIGHEST,
        preferred_element_type=F32,
    )

    up_back = group.exchange(up_sum.astype(BF16).reshape(hidden // nb, nb, deep).transpose(1, 0, 2))
    final_up = up_back.reshape(hidden, deep).T.astype(F32)
    down_back = down_sum.astype(BF16).reshape(out_cols, nb, many, hidden // nb).transpose(1, 0, 2, 3)
    down_back = group.exchange(down_back.reshape(nb, out_cols, many * hidden // nb))
    down_back = down_back.reshape(nb, out_cols, many, hidden // nb).transpose(2, 0, 3, 1)
    final_down = down_back.reshape(ff, out_cols).astype(F32)
    first_low = first_sum.astype(BF16)
    qkv_back = first_low[:, :width].reshape(slots * HEAD_DIM, nb, deep).transpose(1, 0, 2)
    out_back = first_low[:, width:]
    if spread:
        out_back = out_back.reshape(out_cols, nb, spread * HEAD_DIM).transpose(1, 0, 2)
        back = group.exchange(jnp.concatenate([qkv_back, out_back], axis=2))
        out_back = back[:, :, deep:].reshape(nb, out_cols, spread, HEAD_DIM).transpose(2, 0, 3, 1)
        final_out = out_back.reshape(deep, out_cols).astype(F32)
    else:
        back = group.exchange(qkv_back)
        final_out = out_back.T.astype(F32)
    qkv_back = back[:, :, :deep].reshape(nb, slots, HEAD_DIM, deep).transpose(1, 0, 2, 3)
    qkv_back = qkv_back.reshape(slots * nb, HEAD_DIM, deep)
    qkv_back = lax.dynamic_slice(
        jnp.concatenate([qkv_back, qkv_back], axis=0), (offset, 0, 0), (columns, HEAD_DIM, deep)
    )
    final_qkv = qkv_back.reshape(columns * HEAD_DIM, deep).T.astype(F32)
    return (output, grad_tokens, grad_table, final_qkv, final_out, final_up, final_down)


GELU_IN = 0.7978845608028654
GELU_CUBE = 0.044715


def padded_bytes(shape, kind):
    *lead, rows, lanes = shape
    return math.prod(lead) * -(-rows // 16) * 16 * -(-lanes // 128) * 128 * jnp.dtype(kind).itemsize


def run_kernel(body, outs, *args, spaces=(), scratch=(), sems=0, spare=8, flops=0, name=None):
    places = [pl.ANY if i in spaces else pltpu.VMEM for i in range(len(args))]
    held = list(outs) + list(scratch) + [(a.shape, a.dtype) for i, a in enumerate(args) if i not in spaces]
    limit = sum(padded_bytes(*h) for h in held) + (spare << 20)
    moved = sum(padded_bytes(*o) for o in outs) + sum(padded_bytes(a.shape, a.dtype) for a in args)
    return pl.pallas_call(
        body,
        out_shape=[jax.ShapeDtypeStruct(shape, t) for shape, t in outs],
        in_specs=[pl.BlockSpec(memory_space=place) for place in places],
        out_specs=[pl.BlockSpec(memory_space=pltpu.VMEM) for _ in outs],
        scratch_shapes=[pltpu.VMEM(*h) for h in scratch] + [pltpu.SemaphoreType.DMA((9,))] * sems,
        compiler_params=pltpu.CompilerParams(vmem_limit_bytes=limit),
        cost_estimate=pl.CostEstimate(flops=flops, bytes_accessed=moved, transcendentals=0),
        name=name,
    )(*args)


def after(value, *others):
    return lax.optimization_barrier((value, *others))[0]


class Gathered:
    def __init__(self, ring, chunk):
        self.ring = ring
        self.fore = self.rear = chunk
        self.got = [chunk]
        self.left = ring.size // 2

    def ready(self):
        if self.left == 1:
            cut = self.fore.shape[0] // 2
            return self.fore[:cut], self.rear[cut:]
        return self.fore, self.rear

    def send(self, fore, rear):
        self.left -= 1
        self.fore = lax.ppermute(fore, "dp", self.ring.ahead)
        self.rear = lax.ppermute(rear, "dp", self.ring.back)
        self.got += [self.fore, self.rear]


class Summed:
    def __init__(self, ring, parts):
        self.ring, self.parts = ring, parts
        self.fore, self.rear = parts[-2:]
        self.left = ring.size // 2

    def ready(self):
        whole = self.ring.size // 2
        if self.left == whole:
            return self.fore, self.rear
        mine_fore, mine_rear = self.parts[2 * self.left], self.parts[2 * self.left - 1]
        if self.left < whole - 1:
            return self.add(mine_fore, self.fore), self.add(mine_rear, self.rear)
        cut = self.fore.shape[0]
        fore = jnp.concatenate([self.add(mine_fore[:cut], self.fore), mine_fore[cut:]], axis=0)
        return fore, jnp.concatenate([mine_rear[:cut], self.add(mine_rear[cut:], self.rear)], axis=0)

    def send(self, fore, rear):
        self.left -= 1
        self.fore = lax.ppermute(fore, "dp", self.ring.ahead)
        self.rear = lax.ppermute(rear, "dp", self.ring.back)

    def add(self, mine, got):
        return (mine.astype(F32) + got.astype(F32)).astype(BF16)

    def ends(self):
        return self.parts[0], self.fore, self.rear


def beat(*rings, carry=()):
    ready = [pair for ring in rings for pair in ring.ready()]
    out = lax.optimization_barrier((*ready, *carry))
    for i, ring in enumerate(rings):
        ring.send(out[2 * i], out[2 * i + 1])
    return out[2 * len(rings) :]


NEAR_FIRST = (0, -1, 1, -2, 2, -3, 3, 4)


def member_at(offset):
    dp = lax.axis_index("dp")
    spot = jnp.where(dp % 2 == 0, dp // 2, 7 - dp // 2)
    at = (spot + offset + 8) % 8
    return jnp.where(at < 4, 2 * at, 15 - 2 * at)


def turn(values):
    return values.astype(F32).T.astype(BF16)


def pack_body(qkv, out, up, down, mods, *refs):
    heads, updown = refs[:4], refs[4:8]
    held_q, held_o, held_u, held_d = refs[8:]
    blk = lax.axis_index("blk")
    offset = (6 * lax.axis_index("dp")) % 4
    held_q[...] = jnp.zeros_like(held_q)
    for i in range(6):
        held_q[i + offset] = turn(qkv[:, 72 * i : 72 * i + 72])
    for t in range(4):
        held_o[t] = out[:, 72 * t : 72 * t + 72]
        held_u[t] = turn(up[:, 144 * t : 144 * t + 144])
        for part in range(2):
            at = 576 * part + 144 * t
            held_d[t, :, 144 * part : 144 * part + 144] = down[:, at : at + 144]
    for r in range(4):
        t = blk ^ r
        heads[r][...] = jnp.zeros((160, 384), BF16)
        heads[r][0:72, 0:288] = held_q[t]
        heads[r][72:144, 0:288] = held_q[t + 4]
        heads[r][0:144, 288:360] = held_o[t]
        heads[r][144:152, 0:216] = mods[...]
        updown[r][:, 0:288] = held_u[t]
        updown[r][:, 288:576] = held_d[t]
        updown[r][:, 576:640] = jnp.zeros((144, 64), BF16)


def join_heads_body(*refs):
    pieces, joined, held, row = refs[:4], refs[4], refs[5], refs[6]
    blk = lax.axis_index("blk")
    for r in range(4):
        held[blk ^ r] = pieces[r][...]
    joined[144:192, :] = jnp.zeros((48, 1152), BF16)
    for s in range(4):
        joined[0:144, 288 * s : 288 * s + 288] = held[s, 0:144, 0:288]
        for q in range(3):
            at = 288 * q + 72 * s
            joined[144:192, at : at + 72] = held[s, 48 * q : 48 * q + 48, 288:360]
        row[:, 216 * s : 216 * s + 216] = held[s, 144:152, 0:216].astype(F32)
    for j in range(3):
        joined[144 + 16 * j : 152 + 16 * j, 864:1152] = row[:, 288 * j : 288 * j + 288].astype(BF16)


def join_updown_body(*refs):
    pieces, joined, held = refs[:4], refs[4], refs[5]
    blk = lax.axis_index("blk")
    for r in range(4):
        held[blk ^ r] = pieces[r][...]
    for s in range(4):
        joined[0:144, 288 * s : 288 * s + 288] = held[s, :, 0:288]
        joined[144:288, 288 * s : 288 * s + 288] = held[s, :, 288:576]


def load_chunks(chunks, full, sems, first, count):
    cut = chunks[7].shape[0]
    pieces = [(k, chunk, first, first + count, 0) for k, chunk in enumerate(chunks[:7])]
    pieces.append((7, chunks[7], first, min(first + count, cut), 0))
    pieces.append((7, chunks[8], max(first, cut), first + count, cut))
    copies = []
    for i, (k, chunk, start, stop, base) in enumerate(pieces):
        if start < stop:
            at = pl.multiple_of(member_at(NEAR_FIRST[k]) * count + (start - first), math.gcd(count, max(start - first, 0)))
            source = chunk.at[pl.ds(start - base, stop - start), :]
            copies.append(pltpu.make_async_copy(source, full.at[pl.ds(at, stop - start), :], sems.at[i]))
    for copy in copies:
        copy.start()
    return copies


def split_halves(total, keep, send):
    for f in range(2):
        keep[128 * f : 128 * f + 128, :] = total[256 * f : 256 * f + 128, :]
        send[128 * f : 128 * f + 128, :] = total[256 * f + 128 : 256 * f + 256, :].astype(BF16)


def split_owners(total, own, far, near, cross):
    for i, block in enumerate((own, far, near, cross)):
        for f in range(2):
            row = 256 * f + 64 * i
            block[64 * f : 64 * f + 64, :] = total[row : row + 64, :].astype(block.dtype)


def join_halves(mine, theirs, full):
    for f in range(2):
        full[256 * f : 256 * f + 128, :] = mine[128 * f : 128 * f + 128, :]
        full[256 * f + 128 : 256 * f + 256, :] = theirs[128 * f : 128 * f + 128, :]


def attend_body(t0, t1, t2, t3, *refs):
    chunks = refs[:9]
    hidden, parts, probs, attended, low, out, mod, keep, send = refs[9:18]
    full, slots, tail, full_sems, tail_sems = refs[18:]
    tails = load_chunks(chunks, tail, tail_sems, 144, 48)
    copies = load_chunks(chunks, full, full_sems, 0, 144)
    for copy in tails:
        copy.wait()
    clip = lax.axis_index("dp")
    own = lax.broadcasted_iota(jnp.int32, (8, 288), 0) == clip
    for m in range(24):
        d, j = divmod(m, 3)
        rows = tail[48 * d + 16 * j : 48 * d + 16 * j + 8, 864:1152].astype(F32)
        row = jnp.sum(jnp.where(own, rows, 0.0), axis=0, keepdims=True)
        mod[m // 4 : m // 4 + 1, 288 * (m % 4) : 288 * (m % 4) + 288] = row
        out[48 * m : 48 * m + 48, :] = tail[48 * d : 48 * d + 48, 288 * j : 288 * j + 288]
    for i, block in enumerate((t0, t1, t2, t3)):
        for f in range(2):
            normed, _ = norm_rows(block[f].astype(F32))
            at = 256 * f + 64 * i
            hidden[at : at + 64, :] = (normed * (1.0 + mod[1:2, :]) + mod[0:1, :]).astype(BF16)
    for copy in copies:
        copy.wait()
    slots[...] = dot_nt(hidden[...], full[...]).astype(BF16)
    for e in range(4):
        at = 288 * e
        parts[3 * e] = slots[:, at : at + 72]
        parts[3 * e + 1] = slots[:, at + 72 : at + 144] + slots[:, at + 144 : at + 216]
        parts[3 * e + 2] = slots[:, at + 216 : at + 288]
    scale = HEAD_DIM ** (-0.5)
    for f in range(2):
        rows = slice(256 * f, 256 * f + 256)
        for h in range(4):
            scores = dot_nt(parts[h, rows, :], parts[4 + h, rows, :]) * scale
            weights = jnp.exp(scores - jnp.max(scores, axis=-1, keepdims=True))
            prob = weights / jnp.sum(weights, axis=-1, keepdims=True)
            probs[4 * f + h] = prob
            mixed = dot_nn(prob.astype(BF16), parts[8 + h, rows, :])
            attended[h, rows, :] = mixed
            low[rows, 72 * h : 72 * h + 72] = mixed.astype(BF16)
    split_halves(dot_nt(low[...], out[...]), keep, send)


def middle_body(keep, near, far, t0, t1, mod, hidden, normed, root, branch, middle):
    for f in range(2):
        for i, block in enumerate((t0, t1)):
            rows = slice(128 * f + 64 * i, 128 * f + 64 * i + 64)
            cross = slice(128 * f + 64 * (1 - i), 128 * f + 64 * (1 - i) + 64)
            part = keep[rows, :] + near[rows, :].astype(F32) + far[cross, :].astype(F32)
            mid = block[f].astype(F32) + mod[2:3, :] * part
            norm, inv = norm_rows(mid)
            hidden[rows, :] = (norm * (1.0 + mod[4:5, :]) + mod[3:4, :]).astype(BF16)
            normed[rows, :] = norm
            root[rows, :] = jnp.broadcast_to(inv, (64, 128))
            if i == 0:
                branch[64 * f : 64 * f + 64, :] = part
                middle[64 * f : 64 * f + 64, :] = mid


def mlp_body(mine, theirs, g0, g1, g2, g3, mod, *refs):
    chunks = refs[:9]
    hidden, act, d_branch, d_pre, keep, send = refs[9:15]
    up, down, slope, up_sems, down_sems = refs[15:]
    up_copies = load_chunks(chunks, up, up_sems, 0, 144)
    down_copies = load_chunks(chunks, down, down_sems, 144, 144)
    join_halves(mine, theirs, hidden)
    for f in range(2):
        for i, block in enumerate((g0, g1, g2, g3)):
            row = 256 * f + 64 * i
            d_branch[row : row + 64, :] = (mod[5:6, :] * block[f].astype(F32)).astype(BF16)
    for copy in up_copies:
        copy.wait()
    for at in range(0, 512, 128):
        rows = slice(at, at + 128)
        pre = dot_nt(hidden[rows, :], up[...])
        square = pre * pre
        bend = jnp.tanh(GELU_IN * (pre + GELU_CUBE * (square * pre)))
        half = 0.5 * (1.0 + bend)
        act[rows, :] = (pre * half).astype(BF16)
        inner = GELU_IN * (1.0 + (3.0 * GELU_CUBE) * square)
        slope[rows, :] = half + (0.5 * pre) * ((1.0 - bend * bend) * inner)
    for copy in down_copies:
        copy.wait()
    d_pre[...] = (dot_nn(d_branch[...], down[...]) * slope[...]).astype(BF16)
    split_halves(dot_nn(d_pre[...], up[...]), keep, send)


def grad_updown_body(d_pre, hidden, d_branch, act, *refs):
    outs, total = refs[:9], refs[9]
    total[0] = dot_tn(d_pre[...], hidden[...]).astype(BF16)
    total[1] = dot_tn(d_branch[...], act[...]).astype(BF16)
    for k in range(8):
        at = pl.multiple_of(member_at(NEAR_FIRST[k]) * 144, 144)
        if k < 7:
            outs[k][0:144, :] = total[0, pl.ds(at, 144), :]
            outs[k][144:288, :] = total[1, pl.ds(at, 144), :]
        else:
            outs[7][...] = total[0, pl.ds(at, 144), :]
            outs[8][...] = total[1, pl.ds(at, 144), :]


def branch_b_body(act, *refs):
    chunks, owners, full, sems = refs[:9], refs[9:13], refs[13], refs[14]
    for copy in load_chunks(chunks, full, sems, 144, 144):
        copy.wait()
    split_owners(dot_nt(act[...], full[...]), *owners)


def d_middle_body(keep, near, far, normed, root, g0, g1, branch, mod, d_low, d_mid, sums):
    d_shift = jnp.zeros((1, 1152), F32)
    d_scale = jnp.zeros((1, 1152), F32)
    d_gate = jnp.zeros((1, 1152), F32)
    for f in range(2):
        for i, block in enumerate((g0, g1)):
            rows = slice(128 * f + 64 * i, 128 * f + 64 * i + 64)
            cross = slice(128 * f + 64 * (1 - i), 128 * f + 64 * (1 - i) + 64)
            d_hidden = keep[rows, :] + near[rows, :].astype(F32) + far[cross, :].astype(F32)
            norm = normed[rows, :]
            back = norm_back(d_hidden * (1.0 + mod[4:5, :]), norm, root[rows, 0:1])
            mid = block[f].astype(F32) + back
            d_low[rows, :] = (mod[2:3, :] * mid).astype(BF16)
            if i == 0:
                own = slice(64 * f, 64 * f + 64)
                d_mid[own, :] = mid
                d_shift = d_shift + jnp.sum(d_hidden, axis=0, keepdims=True)
                d_scale = d_scale + jnp.sum(d_hidden * norm, axis=0, keepdims=True)
                d_gate = d_gate + jnp.sum(mid * branch[own, :], axis=0, keepdims=True)
    sums[0:1, :] = d_gate
    sums[1:2, :] = d_shift
    sums[2:3, :] = d_scale


def d_attend_body(mine, theirs, parts, probs, attended, out, d_branch, d_slots, d_att):
    join_halves(mine, theirs, d_branch)
    d_att[...] = dot_nn(d_branch[...], out[...]).astype(BF16)
    scale = HEAD_DIM ** (-0.5)

    def place(rows, m, value):
        e, k = divmod(m, 3)
        low = value.astype(BF16)
        for slot in ((0,), (1, 2), (3,))[k]:
            d_slots[rows, 288 * e + 72 * slot : 288 * e + 72 * slot + 72] = low

    for f in range(2):
        rows = slice(256 * f, 256 * f + 256)
        for h in range(4):
            d_out = d_att[rows, 72 * h : 72 * h + 72]
            delta = jnp.sum(d_out.astype(F32) * attended[h, rows, :], axis=-1, keepdims=True)
            prob = probs[4 * f + h]
            d_prob = dot_nt(d_out, parts[8 + h, rows, :])
            d_score = (prob * (d_prob - delta)).astype(BF16)
            place(rows, h, dot_nn(d_score, parts[4 + h, rows, :]) * scale)
            place(rows, 4 + h, dot_tn(d_score, parts[h, rows, :]) * scale)
            place(rows, 8 + h, dot_tn(prob.astype(BF16), d_out))


def grad_first_body(d_slots, hidden, d_branch, low, *refs):
    outs, total, below = refs[:9], refs[9], refs[10]
    total[...] = dot_tn(d_slots[...], hidden[...]).astype(BF16)
    below[...] = dot_tn(d_branch[...], low[...]).astype(BF16)
    for k in range(8):
        at = pl.multiple_of(member_at(NEAR_FIRST[k]) * 144, 144)
        if k < 7:
            outs[k][0:144, :] = total[pl.ds(at, 144), :]
            tail, row = outs[k], 144
        else:
            outs[7][...] = total[pl.ds(at, 96), :]
            outs[8][0:48, :] = total[pl.ds(at + 96, 48), :]
            tail, row = outs[8], 48
        for q in range(3):
            tail[row : row + 48, 288 * q : 288 * q + 288] = below[pl.ds(at + 48 * q, 48), :]
        tail[row : row + 48, 864:1152] = jnp.zeros((48, 288), BF16)


def d_hidden_a_body(d_slots, *refs):
    chunks, owners, full, sems = refs[:9], refs[9:13], refs[13], refs[14]
    for copy in load_chunks(chunks, full, sems, 0, 144):
        copy.wait()
    split_owners(dot_nn(d_slots[...], full[...]), *owners)


def output_body(own, far, near, cross, middle, g0, mod, output, d_gate):
    total = jnp.zeros((1, 1152), F32)
    for f in range(2):
        rows = slice(64 * f, 64 * f + 64)
        branch = own[rows, :] + near[rows, :].astype(F32)
        branch = branch + far[rows, :].astype(F32) + cross[rows, :].astype(F32)
        output[f] = middle[rows, :] + mod[5:6, :] * branch
        total = total + jnp.sum(g0[f].astype(F32) * branch, axis=0, keepdims=True)
    d_gate[...] = total


def grad_tokens_body(own, far, near, cross, t0, d_mid, mod, sums_b, d_gate_b, grad, d_mod):
    d_shift = jnp.zeros((1, 1152), F32)
    d_scale = jnp.zeros((1, 1152), F32)
    for f in range(2):
        rows = slice(64 * f, 64 * f + 64)
        norm, inv = norm_rows(t0[f].astype(F32))
        d_hidden = own[rows, :] + near[rows, :].astype(F32)
        d_hidden = d_hidden + far[rows, :].astype(F32) + cross[rows, :].astype(F32)
        grad[f] = d_mid[rows, :] + norm_back(d_hidden * (1.0 + mod[1:2, :]), norm, inv)
        d_shift = d_shift + jnp.sum(d_hidden, axis=0, keepdims=True)
        d_scale = d_scale + jnp.sum(d_hidden * norm, axis=0, keepdims=True)
    d_mod[0:1, :] = d_shift
    d_mod[1:2, :] = d_scale
    d_mod[2:5, :] = sums_b[0:3, :]
    d_mod[5:6, :] = d_gate_b[...]


def cut_updown_body(s0, s1, s2, *refs):
    pieces, held = refs[:4], refs[4]
    blk = lax.axis_index("blk")
    total = s0[...].astype(F32) + s1[...].astype(F32) + s2[...].astype(F32)
    for t in range(4):
        held[t, :, 0:288] = total[0:144, 288 * t : 288 * t + 288].astype(BF16)
        held[t, :, 288:576] = total[144:288, 288 * t : 288 * t + 288].astype(BF16)
        held[t, :, 576:640] = jnp.zeros((144, 64), BF16)
    for r in range(4):
        pieces[r][...] = held[blk ^ r]


def final_updown_body(p0, p1, p2, p3, up, down, held):
    blk = lax.axis_index("blk")
    for r, piece in enumerate((p0, p1, p2, p3)):
        held[blk ^ r] = piece[...]
    for s in range(4):
        up[:, 144 * s : 144 * s + 144] = held[s, :, 0:288].astype(F32).T
        for part in range(2):
            at = 576 * part + 144 * s
            down[:, at : at + 144] = held[s, :, 288 + 144 * part : 432 + 144 * part].astype(F32)


def cut_heads_body(s0, s1, s2, *refs):
    pieces, held = refs[:4], refs[4]
    blk = lax.axis_index("blk")
    total = s0[...].astype(F32) + s1[...].astype(F32) + s2[...].astype(F32)
    for t in range(4):
        held[t, :, 0:288] = total[0:144, 288 * t : 288 * t + 288].astype(BF16)
        for q in range(3):
            at = 288 * q + 72 * t
            held[t, 48 * q : 48 * q + 48, 288:360] = total[144:192, at : at + 72].astype(BF16)
        held[t, :, 360:384] = jnp.zeros((144, 24), BF16)
    for r in range(4):
        pieces[r][...] = held[blk ^ r]


def final_heads_body(p0, p1, p2, p3, qkv, out, held, placed):
    blk = lax.axis_index("blk")
    offset = (6 * lax.axis_index("dp")) % 4
    for r, piece in enumerate((p0, p1, p2, p3)):
        sender = blk ^ r
        placed[sender] = piece[0:72, 0:288].astype(F32)
        placed[sender + 4] = piece[72:144, 0:288].astype(F32)
        held[sender] = piece[:, 288:360].astype(F32)
    for i in range(6):
        qkv[:, 72 * i : 72 * i + 72] = placed[i + offset].T
    for s in range(4):
        out[:, 72 * s : 72 * s + 72] = held[s]


def vmem(shape, kind=BF16):
    return (shape, kind)


def local_kernels(tokens, timestep, mod_table, w_qkv, w_out, w_up, w_down, cotangent):
    nd, nb = 8, 4
    ring = Ring(nd, lax.axis_index("dp"))
    group = Group(nb, lax.axis_index("blk"))
    width = tokens.shape[3]
    own_tokens = tokens[0]
    own_cot = cotangent[0]
    full_low = ((512, 1152), BF16)
    half_low = ((256, 1152), BF16)
    half_wide = ((256, 1152), F32)
    own_wide = ((128, 1152), F32)
    owners = [own_wide] + [((128, 1152), BF16)] * 3

    def send_out(pieces):
        return [pieces[0]] + [group.swap(pieces[r], r) for r in (1, 2, 3)]

    def add_low(keep, near):
        return (keep + near.astype(F32)).astype(BF16)

    def own_sum(own, far, near, cross):
        return own, group.swap(far, 2), group.swap(near, 1), group.swap(cross, 3)

    picker = (timestep[:, None] == jnp.arange(mod_table.shape[0], dtype=jnp.int32)[None, :]).astype(BF16)
    table_cols = dot_nn(picker, mod_table).astype(BF16)
    piece = table_cols.shape[1]
    packed = run_kernel(
        pack_body,
        [((160, 384), BF16)] * 4 + [((144, 640), BF16)] * 4,
        w_qkv, w_out.T, w_up, w_down.T, table_cols,
        scratch=[vmem((8, 72, 288)), vmem((4, 144, 72)), vmem((4, 144, 288)), vmem((4, 144, 288))],
        name="pack",
    )
    (first_own,) = run_kernel(
        join_heads_body,
        [((192, 1152), BF16)],
        *send_out(packed[:4]),
        scratch=[vmem((4, 160, 384)), vmem((8, 864), F32)],
        name="join_heads",
    )
    updown_got = send_out(packed[4:])
    first = Gathered(ring, first_own)
    beat(first)
    *updown_got, near_t = beat(first, carry=(*updown_got, own_tokens))
    (updown_own,) = run_kernel(
        join_updown_body,
        [((288, 1152), BF16)],
        *updown_got,
        scratch=[vmem((4, 144, 640))],
        name="join_updown",
    )
    far_t = group.swap(near_t, 2)
    updown_own, near_t, far_t, near_c = beat(first, carry=(updown_own, own_tokens, far_t, own_cot))
    token_blocks = [own_tokens, far_t, group.swap(near_t, 1), group.swap(far_t, 1)]
    far_c = group.swap(near_c, 2)
    updown_own, far_c, near_c, *token_blocks = beat(first, carry=(updown_own, far_c, own_cot, *token_blocks))
    cot_blocks = [own_cot, far_c, group.swap(near_c, 1), group.swap(far_c, 1)]
    updown = Gathered(ring, updown_own)
    held = beat(updown, carry=(*cot_blocks, *token_blocks, *first.got))
    cot_blocks, token_blocks, first_got = held[:4], held[4:8], held[8:]
    hidden_a, parts, probs, attended, low, out_full, mod, keep_a, send_a = run_kernel(
        attend_body,
        [
            full_low,
            ((12, 512, 72), BF16),
            ((8, 256, 256), F32),
            ((4, 512, 72), F32),
            ((512, 288), BF16),
            ((1152, 288), BF16),
            ((8, 1152), F32),
            half_wide,
            half_low,
        ],
        *token_blocks, *first_got,
        spaces=range(4, 13),
        scratch=[vmem((1152, 1152)), vmem((512, 1152)), vmem((384, 1152))],
        sems=2,
        flops=4 * 10**9,
        name="attend",
    )
    keep_a, send_a = beat(updown, carry=(keep_a, send_a))
    near_a = group.swap(send_a, 1)
    low_a = add_low(keep_a, near_a)
    keep_a, near_a, low_a = beat(updown, carry=(keep_a, near_a, low_a))
    far_a = group.swap(low_a, 2)
    keep_a, near_a, far_a = beat(updown, carry=(keep_a, near_a, far_a))
    hidden_mine, normed_b, root_b, branch_a, middle = run_kernel(
        middle_body,
        [half_low, half_wide, ((256, 128), F32), own_wide, own_wide],
        keep_a, near_a, far_a, *token_blocks[:2], mod,
        name="middle",
    )
    hidden_b, act, d_branch_b, d_pre, keep_d, send_d = run_kernel(
        mlp_body,
        [full_low, full_low, full_low, full_low, half_wide, half_low],
        hidden_mine, group.swap(hidden_mine, 1), *cot_blocks, mod, *updown.got,
        spaces=range(7, 16),
        scratch=[vmem((1152, 1152)), vmem((1152, 1152)), vmem((512, 1152), F32)],
        sems=2,
        flops=6 * 10**9,
        name="mlp",
    )
    near_d = group.swap(send_d, 1)
    low_d = add_low(keep_d, near_d)
    grad_updown = run_kernel(
        grad_updown_body,
        [((288, 1152), BF16)] * 7 + [((144, 1152), BF16)] * 2,
        d_pre, hidden_b, d_branch_b, act,
        scratch=[vmem((2, 1152, 1152))],
        flops=4 * 10**9,
        name="grad_updown",
    )
    updown_sum = Summed(ring, grad_updown)
    keep_d, near_d, low_d, act = beat(updown_sum, carry=(keep_d, near_d, low_d, act))
    far_d = group.swap(low_d, 2)
    (act,) = beat(updown_sum, carry=(act,))
    branch_owners = run_kernel(
        branch_b_body,
        owners,
        act, *updown.got,
        spaces=range(1, 10),
        scratch=[vmem((1152, 1152))],
        sems=1,
        flops=2 * 10**9,
        name="branch_b",
    )
    keep_d, near_d, far_d, *branch_owners = beat(updown_sum, carry=(keep_d, near_d, far_d, *branch_owners))
    d_low, d_mid, sums_b = run_kernel(
        d_middle_body,
        [half_low, own_wide, ((3, 1152), F32)],
        keep_d, near_d, far_d, normed_b, root_b, *cot_blocks[:2], branch_a, mod,
        name="d_middle",
    )
    d_branch_a, d_slots = run_kernel(
        d_attend_body,
        [full_low, full_low],
        d_low, group.swap(d_low, 1), parts, probs, attended, out_full,
        scratch=[vmem((512, 288))],
        flops=3 * 10**9,
        name="d_attend",
    )
    grad_first = run_kernel(
        grad_first_body,
        [((192, 1152), BF16)] * 7 + [((96, 1152), BF16)] * 2,
        d_slots, hidden_a, d_branch_a, low,
        scratch=[vmem((1152, 1152)), vmem((1152, 288))],
        flops=2 * 10**9,
        name="grad_first",
    )
    first_sum = Summed(ring, grad_first)
    d_slots, *branch_owners = beat(updown_sum, first_sum, carry=(d_slots, *branch_owners))
    hidden_owners = run_kernel(
        d_hidden_a_body,
        owners,
        d_slots, *first_got,
        spaces=range(1, 10),
        scratch=[vmem((1152, 1152))],
        sems=1,
        flops=2 * 10**9,
        name="d_hidden_a",
    )
    branch_sums = own_sum(*branch_owners)
    held = beat(first_sum, carry=(*updown_sum.ends(), *hidden_owners, *branch_sums))
    updown_ends, hidden_owners, branch_sums = held[:3], held[3:7], held[7:]
    hidden_sums = own_sum(*hidden_owners)
    output, d_gate_b = run_kernel(
        output_body,
        [((2, 64, 1152), F32), ((1, 1152), F32)],
        *branch_sums, middle, own_cot, mod,
        name="output",
    )
    updown_cut = run_kernel(
        cut_updown_body, [((144, 640), BF16)] * 4, *updown_ends, scratch=[vmem((4, 144, 640))], name="cut_updown"
    )
    held = beat(first_sum, carry=(*hidden_sums, *updown_cut))
    hidden_sums, updown_cut = held[:4], held[4:]
    grad_tokens, d_mod = run_kernel(
        grad_tokens_body,
        [((2, 64, 1152), F32), ((6, 1152), F32)],
        *hidden_sums, own_tokens, d_mid, mod, sums_b, d_gate_b,
        name="grad_tokens",
    )
    updown_back = send_out(updown_cut)
    d_mod, *updown_back = beat(first_sum, carry=(d_mod, *updown_back))
    mod_got = lax.all_to_all(d_mod.reshape(nd * nb, piece), ("dp", "blk"), 0, 0, tiled=True)
    mod_sums = jnp.sum(mod_got.reshape(nd, nb, piece), axis=1)
    grad_table = lax.dot_general(
        picker.astype(F32),
        mod_sums,
        (((0,), (0,)), ((), ())),
        precision=HIGHEST,
        preferred_element_type=F32,
    )
    final_up, final_down = run_kernel(
        final_updown_body,
        [((288, 576), F32), ((144, 1152), F32)],
        *updown_back,
        scratch=[vmem((4, 144, 640))],
        name="final_updown",
    )
    heads_cut = run_kernel(
        cut_heads_body, [((144, 384), BF16)] * 4, *first_sum.ends(), scratch=[vmem((4, 144, 384))], name="cut_heads"
    )
    final_qkv, final_out = run_kernel(
        final_heads_body,
        [((288, 432), F32), ((144, 288), F32)],
        *send_out(heads_cut),
        scratch=[vmem((4, 144, 72), F32), vmem((8, 72, 288), F32)],
        name="final_heads",
    )
    return (output[None], grad_tokens[None], grad_table, final_qkv, final_out.T, final_up, final_down.T)


def local(tokens, timestep, mod_table, w_qkv, w_out, w_up, w_down, cotangent):
    sizes = (lax.axis_size("dp"), lax.axis_size("blk"), tokens.shape, w_qkv.shape, w_up.shape, w_down.shape)
    known = (8, 4, (1, 2, 64, 1152), (288, 432), (288, 576), (1152, 144))
    chosen = local_kernels if sizes == known else local_plain
    return chosen(tokens, timestep, mod_table, w_qkv, w_out, w_up, w_down, cotangent)


def solution(mesh):
    in_specs = (
        P("dp", None, "blk", None),
        P(),
        P(None, ("dp", "blk")),
        P("blk", "dp"),
        P("blk", "dp"),
        P("blk", "dp"),
        P("blk", "dp"),
        P("dp", None, "blk", None),
    )
    out_specs = (
        P("dp", None, "blk", None),
        P("dp", None, "blk", None),
        P(None, ("dp", "blk")),
        P("blk", "dp"),
        P("blk", "dp"),
        P("blk", "dp"),
        P("blk", "dp"),
    )
    return jax.shard_map(local, mesh=mesh, in_specs=in_specs, out_specs=out_specs, check_vma=False)
```

```python
import math
from functools import partial

import jax
import jax.numpy as jnp
from jax import lax
from jax.experimental import pallas as pl
from jax.experimental.pallas import tpu as pltpu
from jax.sharding import PartitionSpec as P

HEADS = 16
HEAD_DIM = 72
EPS = 1e-06
HIGHEST = lax.Precision.HIGHEST
BF16 = jnp.bfloat16
F32 = jnp.float32


def norm_rows(values):
    center = values - jnp.mean(values, axis=-1, keepdims=True)
    spread = jnp.mean(center * center, axis=-1, keepdims=True)
    root_inv = lax.rsqrt(spread + EPS)
    return (center * root_inv, root_inv)


def norm_back(d_normed, normed, root_inv):
    mean_one = jnp.mean(d_normed, axis=-1, keepdims=True)
    mean_two = jnp.mean(d_normed * normed, axis=-1, keepdims=True)
    return root_inv * (d_normed - mean_one - normed * mean_two)


def dot_nn(left, right):
    return jnp.dot(left, right, preferred_element_type=F32)


def dot_tn(left, right):
    return lax.dot_general(left, right, (((0,), (0,)), ((), ())), preferred_element_type=F32)


def dot_nt(left, right):
    return lax.dot_general(left, right, (((1,), (1,)), ((), ())), preferred_element_type=F32)


class Ring:
    def __init__(self, size, index):
        self.size = size
        self.order = list(range(0, size, 2)) + list(range(size - 1, 0, -2))
        place = [0] * size
        for spot, member in enumerate(self.order):
            place[member] = spot
        self.spot = jnp.array(place, jnp.int32)[index]
        self.table = jnp.array(self.order, jnp.int32)
        self.ahead = [(self.order[i], self.order[(i + 1) % size]) for i in range(size)]
        self.back = [(right, left) for left, right in self.ahead]

    def member(self, offset):
        return self.table[(self.spot + offset) % self.size]

    def gather(self, chunk):
        half = self.size // 2
        cut = chunk.shape[0] // 2
        out = jnp.zeros((self.size,) + chunk.shape, chunk.dtype)

        def put(out, piece, offset, row=0):
            return lax.dynamic_update_slice(out, piece[None], (self.member(offset), row, 0))

        out = put(out, chunk, 0)
        fore = rear = chunk
        for step in range(1, half):
            fore = lax.ppermute(fore, "dp", self.ahead)
            rear = lax.ppermute(rear, "dp", self.back)
            out = put(put(out, fore, -step), rear, step)
        fore = lax.ppermute(fore[:cut], "dp", self.ahead)
        rear = lax.ppermute(rear[cut:], "dp", self.back)
        return put(put(out, fore, half), rear, half, cut)

    def scatter(self, parts):
        half = self.size // 2
        cut = parts.shape[1] // 2

        def own(offset):
            return lax.dynamic_index_in_dim(parts, self.member(offset), 0, keepdims=False)

        far = own(half)
        fore = lax.ppermute(far[:cut], "dp", self.ahead)
        rear = lax.ppermute(far[cut:], "dp", self.back)
        for step in range(half - 1, 0, -1):
            mine_fore = own(step).astype(F32)
            mine_rear = own(-step).astype(F32)
            if step == half - 1:
                fore = jnp.concatenate([mine_fore[:cut] + fore.astype(F32), mine_fore[cut:]], axis=0)
                rear = jnp.concatenate([mine_rear[:cut], mine_rear[cut:] + rear.astype(F32)], axis=0)
            else:
                fore = mine_fore + fore.astype(F32)
                rear = mine_rear + rear.astype(F32)
            fore = lax.ppermute(fore.astype(BF16), "dp", self.ahead)
            rear = lax.ppermute(rear.astype(BF16), "dp", self.back)
        return own(0).astype(F32) + fore.astype(F32) + rear.astype(F32)


class Group:
    def __init__(self, size, index):
        self.size = size
        self.index = index
        self.bits = []
        bit = size // 2
        while bit:
            self.bits.append(bit)
            bit //= 2

    def swap(self, values, bit):
        return lax.ppermute(values, "blk", [(i, i ^ bit) for i in range(self.size)])

    def exchange(self, pieces):
        if self.size > 4:
            return lax.all_to_all(pieces, "blk", 0, 0, tiled=True)
        got = []
        for r in range(self.size):
            piece = lax.dynamic_index_in_dim(pieces, self.index ^ r, 0, keepdims=False)
            got.append(self.swap(piece, r) if r else piece)
        bit = 1
        while bit < self.size:
            odd = (self.index & bit) != 0
            got = [jnp.where(odd, got[r ^ bit], got[r]) for r in range(self.size)]
            bit *= 2
        return jnp.stack(got)

    def gather(self, block, bits=None):
        for bit in self.bits if bits is None else bits:
            block = jnp.concatenate([block, self.swap(block, bit)], axis=0)
        return block

    def scatter(self, parts, share):
        for bit in reversed(self.bits[1:]):
            half = parts.shape[0] // 2
            parts = parts[:half] + self.swap(parts[half:].astype(BF16), bit).astype(F32)
        top = self.bits[0]
        if share:
            return parts + self.swap(parts.astype(BF16), top)[::-1].astype(F32)
        return parts[:1] + self.swap(parts[1:].astype(BF16), top).astype(F32)


def local_plain(tokens, timestep, mod_table, w_qkv, w_out, w_up, w_down, cotangent):
    frames, patches, width = tokens.shape[1:]
    nd = lax.axis_size("dp")
    nb = lax.axis_size("blk")
    dp = lax.axis_index("dp")
    blk = lax.axis_index("blk")
    ring = Ring(nd, dp)
    group = Group(nb, blk)
    rows = nb * frames * patches
    scale = HEAD_DIM ** (-0.5)
    heads = HEADS // nb
    deep = width // nb
    ff = w_down.shape[0]
    hidden = w_up.shape[1]
    out_cols = w_out.shape[1]

    columns = w_qkv.shape[1] // HEAD_DIM
    slots = -(-columns // nb)
    offset = (columns * dp) % nb
    qkv_t = w_qkv.T.reshape(columns, HEAD_DIM, deep)
    qkv_pos = jnp.zeros((2 * slots * nb, HEAD_DIM, deep), BF16)
    qkv_pos = lax.dynamic_update_slice(qkv_pos, qkv_t, (offset, 0, 0))
    qkv_pos = qkv_pos[: slots * nb] + qkv_pos[slots * nb :]
    qkv_send = qkv_pos.reshape(slots, nb, HEAD_DIM, deep).transpose(1, 0, 2, 3)
    qkv_send = qkv_send.reshape(nb, slots * HEAD_DIM, deep)
    spread = heads // nb
    if spread:
        out_send = w_out.T.reshape(out_cols, spread, nb, HEAD_DIM).transpose(2, 0, 1, 3)
        out_send = out_send.reshape(nb, out_cols, spread * HEAD_DIM)
    up_send = w_up.T.reshape(nb, hidden // nb, deep)
    many = ff // hidden
    down_send = w_down.T.reshape(out_cols, many, nb, hidden // nb).transpose(2, 0, 1, 3)
    down_send = down_send.reshape(nb, out_cols, many * hidden // nb)
    first = group.exchange(jnp.concatenate([qkv_send, out_send], axis=2) if spread else qkv_send)
    up_got = group.exchange(up_send)
    down_got = group.exchange(down_send)
    qkv_own = first[:, :, :deep].transpose(1, 0, 2).reshape(slots * HEAD_DIM, width)
    out_own = first[:, :, deep:].transpose(1, 0, 2).reshape(out_cols, heads * HEAD_DIM) if spread else w_out.T
    up_own = up_got.transpose(1, 0, 2).reshape(hidden // nb, width)
    down_own = down_got.transpose(1, 0, 2).reshape(out_cols, nd * hidden // nb)

    token_all = group.gather(tokens)
    cot_all = group.gather(cotangent)

    picker = (timestep[:, None] == jnp.arange(mod_table.shape[0], dtype=jnp.int32)[None, :]).astype(BF16)
    table_cols = dot_nn(picker, mod_table).astype(BF16)
    piece = table_cols.shape[1]
    mods_send = jnp.broadcast_to(table_cols[:, None, :], (nd, nb, piece)).reshape(nd * nb, piece)
    mod_row = lax.all_to_all(mods_send, ("dp", "blk"), 0, 0, tiled=True).reshape(6, width).astype(F32)
    shift_a, scale_a, gate_a, shift_b, scale_b, gate_b = (mod_row[i] for i in range(6))

    first_all = ring.gather(jnp.concatenate([qkv_own, out_own], axis=1))
    up_full = ring.gather(up_own).reshape(ff, width)
    down_full = ring.gather(down_own).reshape(width, ff)
    out_full = first_all[:, :, width:].reshape(width, heads * HEAD_DIM)
    wanted = blk + nb * jnp.arange(3 * heads, dtype=jnp.int32)
    holder = wanted // columns
    place = ((wanted - columns * holder + (columns * holder) % nb) % (slots * nb)) // nb
    slot_of = holder * slots + place
    qkv_slots = first_all[:, :, :width].reshape(nd * slots, HEAD_DIM, width)
    qkv_full = jnp.take(qkv_slots, slot_of, axis=0).reshape(3 * heads * HEAD_DIM, width)

    inputs = token_all.reshape(rows, width).astype(F32)
    normed_a, root_a = norm_rows(inputs)
    hidden_a = (normed_a * (1.0 + scale_a) + shift_a).astype(BF16)
    projected = dot_nt(hidden_a, qkv_full).astype(BF16)

    def by_head(values, parts):
        split = values.reshape(nb, frames, patches, parts, heads, HEAD_DIM)
        split = split.transpose(3, 1, 4, 0, 2, 5)
        return split.reshape(parts, frames, heads, nb * patches, HEAD_DIM)

    def by_row(values):
        split = values.reshape(-1, frames, heads, nb, patches, HEAD_DIM)
        return split.transpose(3, 1, 4, 0, 2, 5).reshape(rows, -1)

    query, keys, values = by_head(projected, 3)
    scores = jnp.einsum("fhqe,fhke->fhqk", query, keys, preferred_element_type=F32) * scale
    top = jnp.max(scores, axis=-1, keepdims=True)
    weights = jnp.exp(scores - top)
    probs = weights / jnp.sum(weights, axis=-1, keepdims=True)
    probs_low = probs.astype(BF16)
    attended = jnp.einsum("fhqk,fhke->fhqe", probs_low, values, preferred_element_type=F32)
    attn_low = by_row(attended).astype(BF16)
    share = 2 * frames * patches
    own = frames * patches

    def blocks(partial_sum):
        return partial_sum.reshape(nb, own, width)

    branch_a = group.scatter(blocks(dot_nt(attn_low, out_full)), True).reshape(share, width)
    middle = inputs[:share] + gate_a * branch_a
    normed_b, root_b = norm_rows(middle)
    hidden_low = (normed_b * (1.0 + scale_b) + shift_b).astype(BF16)
    hidden_b = group.gather(hidden_low.reshape(2, own, width), group.bits[1:]).reshape(rows, width)
    pre_act = dot_nt(hidden_b, up_full)
    activated, gelu_back = jax.vjp(partial(jax.nn.gelu, approximate=True), pre_act)
    act_low = activated.astype(BF16)
    grad_in = cot_all.reshape(rows, width).astype(F32)
    d_branch_b = (gate_b * grad_in).astype(BF16)
    grad_down = dot_tn(d_branch_b, act_low).astype(BF16)
    down_sum = ring.scatter(grad_down.reshape(nd, out_cols, ff))
    d_act = dot_nn(d_branch_b, down_full)
    d_pre = gelu_back(d_act)[0].astype(BF16)
    grad_up = dot_tn(d_pre, hidden_b).astype(BF16)
    up_sum = ring.scatter(grad_up.reshape(nd, hidden // nb, width))
    d_hidden_b = group.scatter(blocks(dot_nn(d_pre, up_full)), True).reshape(share, width)
    branch_b = group.scatter(blocks(dot_nt(act_low, down_full)), False).reshape(own, width)
    output = (middle[:own] + gate_b * branch_b).reshape(tokens.shape)
    d_gate_b = jnp.sum(grad_in[:own] * branch_b, axis=0)
    d_shift_b = jnp.sum(d_hidden_b[:own], axis=0)
    d_scale_b = jnp.sum(d_hidden_b[:own] * normed_b[:own], axis=0)
    d_middle = grad_in[:share] + norm_back(d_hidden_b * (1.0 + scale_b), normed_b, root_b)
    d_gate_a = jnp.sum(d_middle[:own] * branch_a[:own], axis=0)
    d_branch_a = (gate_a * d_middle).astype(BF16).reshape(2, own, width)
    d_branch_a = group.gather(d_branch_a, group.bits[1:]).reshape(rows, width)
    grad_out = dot_tn(d_branch_a, attn_low).astype(BF16)
    d_attended = dot_nn(d_branch_a, out_full).astype(BF16)
    d_att = by_head(d_attended, 1)[0]
    delta = jnp.sum(d_att.astype(F32) * attended, axis=-1, keepdims=True)
    d_probs = jnp.einsum("fhqe,fhke->fhqk", d_att, values, preferred_element_type=F32)
    d_scores = (probs * (d_probs - delta)).astype(BF16)
    d_query = jnp.einsum("fhqk,fhke->fhqe", d_scores, keys, preferred_element_type=F32) * scale
    d_key = jnp.einsum("fhqk,fhqe->fhke", d_scores, query, preferred_element_type=F32) * scale
    d_value = jnp.einsum("fhqk,fhqe->fhke", probs_low, d_att, preferred_element_type=F32)
    d_projected = by_row(jnp.stack([d_query, d_key, d_value]).astype(BF16))
    grad_qkv = dot_tn(d_projected, hidden_a).astype(BF16).reshape(3 * heads, HEAD_DIM, width)
    grad_slots = jnp.zeros((nd * slots, HEAD_DIM, width), BF16).at[slot_of].set(grad_qkv)
    grad_first = jnp.concatenate(
        [
            grad_slots.reshape(nd, slots * HEAD_DIM, width),
            grad_out.reshape(nd, out_cols, heads * HEAD_DIM),
        ],
        axis=2,
    )
    first_sum = ring.scatter(grad_first)
    d_hidden_a = group.scatter(blocks(dot_nn(d_projected, qkv_full)), False).reshape(own, width)
    d_shift_a = jnp.sum(d_hidden_a, axis=0)
    d_scale_a = jnp.sum(d_hidden_a * normed_a[:own], axis=0)
    d_normed = norm_back(d_hidden_a * (1.0 + scale_a), normed_a[:own], root_a[:own])
    grad_tokens = (d_middle[:own] + d_normed).reshape(tokens.shape)

    d_mod = jnp.concatenate([d_shift_a, d_scale_a, d_gate_a, d_shift_b, d_scale_b, d_gate_b])
    mod_got = lax.all_to_all(d_mod.reshape(nd * nb, piece), ("dp", "blk"), 0, 0, tiled=True)
    mod_sums = jnp.sum(mod_got.reshape(nd, nb, piece), axis=1)
    grad_table = lax.dot_general(
        picker.astype(F32),
        mod_sums,
        (((0,), (0,)), ((), ())),
        precision=HIGHEST,
        preferred_element_type=F32,
    )

    up_back = group.exchange(up_sum.astype(BF16).reshape(hidden // nb, nb, deep).transpose(1, 0, 2))
    final_up = up_back.reshape(hidden, deep).T.astype(F32)
    down_back = down_sum.astype(BF16).reshape(out_cols, nb, many, hidden // nb).transpose(1, 0, 2, 3)
    down_back = group.exchange(down_back.reshape(nb, out_cols, many * hidden // nb))
    down_back = down_back.reshape(nb, out_cols, many, hidden // nb).transpose(2, 0, 3, 1)
    final_down = down_back.reshape(ff, out_cols).astype(F32)
    first_low = first_sum.astype(BF16)
    qkv_back = first_low[:, :width].reshape(slots * HEAD_DIM, nb, deep).transpose(1, 0, 2)
    out_back = first_low[:, width:]
    if spread:
        out_back = out_back.reshape(out_cols, nb, spread * HEAD_DIM).transpose(1, 0, 2)
        back = group.exchange(jnp.concatenate([qkv_back, out_back], axis=2))
        out_back = back[:, :, deep:].reshape(nb, out_cols, spread, HEAD_DIM).transpose(2, 0, 3, 1)
        final_out = out_back.reshape(deep, out_cols).astype(F32)
    else:
        back = group.exchange(qkv_back)
        final_out = out_back.T.astype(F32)
    qkv_back = back[:, :, :deep].reshape(nb, slots, HEAD_DIM, deep).transpose(1, 0, 2, 3)
    qkv_back = qkv_back.reshape(slots * nb, HEAD_DIM, deep)
    qkv_back = lax.dynamic_slice(
        jnp.concatenate([qkv_back, qkv_back], axis=0), (offset, 0, 0), (columns, HEAD_DIM, deep)
    )
    final_qkv = qkv_back.reshape(columns * HEAD_DIM, deep).T.astype(F32)
    return (output, grad_tokens, grad_table, final_qkv, final_out, final_up, final_down)


GELU_IN = 0.7978845608028654
GELU_CUBE = 0.044715


def padded_bytes(shape, kind):
    *lead, rows, lanes = shape
    return math.prod(lead) * -(-rows // 16) * 16 * -(-lanes // 128) * 128 * jnp.dtype(kind).itemsize


def run_kernel(body, outs, *args, spaces=(), scratch=(), sems=0, spare=8, flops=0, name=None):
    places = [pl.ANY if i in spaces else pltpu.VMEM for i in range(len(args))]
    held = list(outs) + list(scratch) + [(a.shape, a.dtype) for i, a in enumerate(args) if i not in spaces]
    limit = sum(padded_bytes(*h) for h in held) + (spare << 20)
    moved = sum(padded_bytes(*o) for o in outs) + sum(padded_bytes(a.shape, a.dtype) for a in args)
    return pl.pallas_call(
        body,
        out_shape=[jax.ShapeDtypeStruct(shape, t) for shape, t in outs],
        in_specs=[pl.BlockSpec(memory_space=place) for place in places],
        out_specs=[pl.BlockSpec(memory_space=pltpu.VMEM) for _ in outs],
        scratch_shapes=[pltpu.VMEM(*h) for h in scratch] + [pltpu.SemaphoreType.DMA((9,))] * sems,
        compiler_params=pltpu.CompilerParams(vmem_limit_bytes=limit),
        cost_estimate=pl.CostEstimate(flops=flops, bytes_accessed=moved, transcendentals=0),
        name=name,
    )(*args)


def after(value, *others):
    return lax.optimization_barrier((value, *others))[0]


def step(ring, fore, rear, *carry):
    (fore, rear), carry = lax.optimization_barrier(((fore, rear), carry))
    return lax.ppermute(fore, "dp", ring.ahead), lax.ppermute(rear, "dp", ring.back), carry


def sum_low(mine, got):
    return (mine.astype(F32) + got.astype(F32)).astype(BF16)


def stack(*blocks):
    return jnp.concatenate(blocks, axis=0)


NEAR_FIRST = (0, -1, 1, -2, 2, -3, 3, 4)


def member_at(offset):
    dp = lax.axis_index("dp")
    spot = jnp.where(dp % 2 == 0, dp // 2, 7 - dp // 2)
    at = (spot + offset + 8) % 8
    return jnp.where(at < 4, 2 * at, 15 - 2 * at)


def turn(values):
    return values.astype(F32).T.astype(BF16)


def pack_heads_body(qkv, out, mods, *refs):
    heads, held_q, held_o = refs[:4], refs[4], refs[5]
    blk = lax.axis_index("blk")
    offset = (6 * lax.axis_index("dp")) % 4
    held_q[...] = jnp.zeros_like(held_q)
    for i in range(6):
        held_q[i + offset] = turn(qkv[:, 72 * i : 72 * i + 72])
    for t in range(4):
        held_o[t] = out[:, 72 * t : 72 * t + 72]
    for r in range(4):
        t = blk ^ r
        heads[r][...] = jnp.zeros((160, 384), BF16)
        heads[r][0:72, 0:288] = held_q[t]
        heads[r][72:144, 0:288] = held_q[t + 4]
        heads[r][0:144, 288:360] = held_o[t]
        heads[r][144:152, 0:216] = mods[...]


def pack_updown_body(up, down, *refs):
    updown, held_u, held_d = refs[:4], refs[4], refs[5]
    blk = lax.axis_index("blk")
    for t in range(4):
        held_u[t] = turn(up[:, 144 * t : 144 * t + 144])
        for part in range(2):
            at = 576 * part + 144 * t
            held_d[t, :, 144 * part : 144 * part + 144] = down[:, at : at + 144]
    for r in range(4):
        t = blk ^ r
        updown[r][:, 0:288] = held_u[t]
        updown[r][:, 288:576] = held_d[t]
        updown[r][:, 576:640] = jnp.zeros((144, 64), BF16)


def join_heads_body(*refs):
    pieces, joined, held, row = refs[:4], refs[4], refs[5], refs[6]
    blk = lax.axis_index("blk")
    for r in range(4):
        held[blk ^ r] = pieces[r][...]
    joined[144:192, :] = jnp.zeros((48, 1152), BF16)
    for s in range(4):
        joined[0:144, 288 * s : 288 * s + 288] = held[s, 0:144, 0:288]
        for q in range(3):
            at = 288 * q + 72 * s
            joined[144:192, at : at + 72] = held[s, 48 * q : 48 * q + 48, 288:360]
        row[:, 216 * s : 216 * s + 216] = held[s, 144:152, 0:216].astype(F32)
    for j in range(3):
        joined[144 + 16 * j : 152 + 16 * j, 864:1152] = row[:, 288 * j : 288 * j + 288].astype(BF16)


def join_updown_body(*refs):
    pieces, up, down, held = refs[:4], refs[4], refs[5], refs[6]
    blk = lax.axis_index("blk")
    for r in range(4):
        held[blk ^ r] = pieces[r][...]
    for s in range(4):
        up[:, 288 * s : 288 * s + 288] = held[s, :, 0:288]
        down[:, 288 * s : 288 * s + 288] = held[s, :, 288:576]


FIRST_PLACES = (
    (0, 0, 0, 192, 0),
    (-1, 1, 0, 192, 0),
    (1, 2, 0, 192, 0),
    (-2, 3, 0, 192, 0),
    (2, 4, 0, 192, 0),
    (-3, 5, 0, 192, 0),
    (3, 6, 0, 192, 0),
    (4, 7, 0, 96, 0),
    (4, 8, 0, 96, 96),
)
UP_PLACES = (
    (0, 0, 0, 144, 0),
    (-1, 1, 96, 144, 0),
    (1, 2, 96, 144, 0),
    (-2, 3, 0, 144, 0),
    (2, 4, 0, 144, 0),
    (-3, 5, 0, 144, 0),
    (3, 6, 0, 144, 0),
    (4, 7, 0, 80, 0),
    (4, 8, 0, 64, 80),
)
DOWN_PLACES = (
    (0, 0, 0, 144, 0),
    (-1, 1, 144, 144, 0),
    (1, 2, 144, 144, 0),
    (-2, 3, 144, 144, 0),
    (2, 4, 144, 144, 0),
    (-3, 5, 80, 144, 0),
    (3, 6, 64, 144, 0),
    (4, 7, 0, 80, 0),
    (4, 8, 0, 64, 80),
)


def load_chunks(arrays, places, full, sems, first=0, count=144):
    copies = []
    for offset, index, start, rows, row in places:
        low, high = max(first, row), min(first + count, row + rows)
        if low < high:
            skip = low - first
            at = pl.multiple_of(member_at(offset) * count + skip, math.gcd(count, skip))
            source = arrays[index].at[pl.ds(start + low - row, high - low), :]
            target = full.at[pl.ds(at, high - low), :]
            copies.append(pltpu.make_async_copy(source, target, sems.at[len(copies)]))
    for copy in copies:
        copy.start()
    return copies


def split_halves(total, keep, send):
    for f in range(2):
        keep[128 * f : 128 * f + 128, :] = total[256 * f : 256 * f + 128, :]
        send[128 * f : 128 * f + 128, :] = total[256 * f + 128 : 256 * f + 256, :].astype(BF16)


def join_halves(mine, theirs, full):
    for f in range(2):
        full[256 * f : 256 * f + 128, :] = mine[128 * f : 128 * f + 128, :]
        full[256 * f + 128 : 256 * f + 256, :] = theirs[128 * f : 128 * f + 128, :]


def attend_body(t0, t1, t2, t3, *refs):
    chunks = refs[:9]
    hidden, parts, probs, attended, low, out, mod, keep, send = refs[9:18]
    full, slots, tail, full_sems, tail_sems = refs[18:]
    tails = load_chunks(chunks, FIRST_PLACES, tail, tail_sems, 144, 48)
    copies = load_chunks(chunks, FIRST_PLACES, full, full_sems)
    for copy in tails:
        copy.wait()
    clip = lax.axis_index("dp")
    own = lax.broadcasted_iota(jnp.int32, (8, 288), 0) == clip
    for m in range(24):
        d, j = divmod(m, 3)
        rows = tail[48 * d + 16 * j : 48 * d + 16 * j + 8, 864:1152].astype(F32)
        row = jnp.sum(jnp.where(own, rows, 0.0), axis=0, keepdims=True)
        mod[m // 4 : m // 4 + 1, 288 * (m % 4) : 288 * (m % 4) + 288] = row
        out[48 * m : 48 * m + 48, :] = tail[48 * d : 48 * d + 48, 288 * j : 288 * j + 288]
    for i, block in enumerate((t0, t1, t2, t3)):
        for f in range(2):
            normed, _ = norm_rows(block[f].astype(F32))
            at = 256 * f + 64 * i
            hidden[at : at + 64, :] = (normed * (1.0 + mod[1:2, :]) + mod[0:1, :]).astype(BF16)
    for copy in copies:
        copy.wait()
    slots[...] = dot_nt(hidden[...], full[...]).astype(BF16)
    for e in range(4):
        at = 288 * e
        parts[3 * e] = slots[:, at : at + 72]
        parts[3 * e + 1] = slots[:, at + 72 : at + 144] + slots[:, at + 144 : at + 216]
        parts[3 * e + 2] = slots[:, at + 216 : at + 288]
    scale = HEAD_DIM ** (-0.5)
    for f in range(2):
        rows = slice(256 * f, 256 * f + 256)
        for h in range(4):
            scores = dot_nt(parts[h, rows, :], parts[4 + h, rows, :]) * scale
            weights = jnp.exp(scores - jnp.max(scores, axis=-1, keepdims=True))
            prob = weights / jnp.sum(weights, axis=-1, keepdims=True)
            probs[4 * f + h] = prob
            mixed = dot_nn(prob.astype(BF16), parts[8 + h, rows, :])
            attended[h, rows, :] = mixed
            low[rows, 72 * h : 72 * h + 72] = mixed.astype(BF16)
    split_halves(dot_nt(low[...], out[...]), keep, send)


def middle_body(keep, near, far, t0, t1, mod, hidden, normed, root, branch, middle):
    for f in range(2):
        for i, block in enumerate((t0, t1)):
            rows = slice(128 * f + 64 * i, 128 * f + 64 * i + 64)
            cross = slice(128 * f + 64 * (1 - i), 128 * f + 64 * (1 - i) + 64)
            part = keep[rows, :] + near[rows, :].astype(F32) + far[cross, :].astype(F32)
            mid = block[f].astype(F32) + mod[2:3, :] * part
            norm, inv = norm_rows(mid)
            hidden[rows, :] = (norm * (1.0 + mod[4:5, :]) + mod[3:4, :]).astype(BF16)
            normed[rows, :] = norm
            root[rows, :] = jnp.broadcast_to(inv, (64, 128))
            if i == 0:
                branch[64 * f : 64 * f + 64, :] = part
                middle[64 * f : 64 * f + 64, :] = mid


def write_parts(total, outs):
    cut = outs[7].shape[0]
    for k in range(8):
        at = pl.multiple_of(member_at(NEAR_FIRST[k]) * 144, 144)
        if k < 7:
            outs[k][...] = total[pl.ds(at, 144), :]
        else:
            outs[7][...] = total[pl.ds(at, cut), :]
            outs[8][...] = total[pl.ds(at + cut, 144 - cut), :]


def up_body(mine, theirs, g0, g1, g2, g3, mod, *refs):
    chunks = refs[:9]
    hidden, act, slope, d_branch = refs[9:13]
    parts = refs[13:22]
    up, total, sems = refs[22:]
    copies = load_chunks(chunks, UP_PLACES, up, sems)
    join_halves(mine, theirs, hidden)
    for f in range(2):
        for i, block in enumerate((g0, g1, g2, g3)):
            row = 256 * f + 64 * i
            d_branch[row : row + 64, :] = (mod[5:6, :] * block[f].astype(F32)).astype(BF16)
    for copy in copies:
        copy.wait()
    for at in range(0, 512, 128):
        rows = slice(at, at + 128)
        pre = dot_nt(hidden[rows, :], up[...])
        square = pre * pre
        bend = jnp.tanh(GELU_IN * (pre + GELU_CUBE * (square * pre)))
        half = 0.5 * (1.0 + bend)
        act[rows, :] = (pre * half).astype(BF16)
        inner = GELU_IN * (1.0 + (3.0 * GELU_CUBE) * square)
        slope[rows, :] = half + (0.5 * pre) * ((1.0 - bend * bend) * inner)
    total[...] = dot_tn(d_branch[...], act[...]).astype(BF16)
    write_parts(total, parts)


def down_body(d_branch, slope, *refs):
    downs, ups = refs[:9], refs[9:18]
    d_pre, keep, send = refs[18:21]
    down, up, down_sems, up_sems = refs[21:]
    down_copies = load_chunks(downs, DOWN_PLACES, down, down_sems)
    up_copies = load_chunks(ups, UP_PLACES, up, up_sems)
    for copy in down_copies:
        copy.wait()
    d_pre[...] = (dot_nn(d_branch[...], down[...]) * slope[...]).astype(BF16)
    for copy in up_copies:
        copy.wait()
    split_halves(dot_nn(d_pre[...], up[...]), keep, send)


def grad_body(left, right, *refs):
    parts, total = refs[:9], refs[9]
    total[...] = dot_tn(left[...], right[...]).astype(BF16)
    write_parts(total, parts)


def branch_b_body(act, g0, g1, g2, g3, *refs):
    chunks = refs[:9]
    keep, send, d_gate, full, total, sems = refs[9:]
    for copy in load_chunks(chunks, DOWN_PLACES, full, sems):
        copy.wait()
    total[...] = dot_nt(act[...], full[...])
    split_halves(total, keep, send)
    gate = jnp.zeros((1, 1152), F32)
    for f in range(2):
        for i, block in enumerate((g0, g1, g2, g3)):
            row = 256 * f + 64 * i
            gate = gate + jnp.sum(block[f].astype(F32) * total[row : row + 64, :], axis=0, keepdims=True)
    d_gate[...] = gate


def d_middle_body(keep, near, far, normed, root, g0, g1, branch, mod, d_low, d_mid, sums):
    d_shift = jnp.zeros((1, 1152), F32)
    d_scale = jnp.zeros((1, 1152), F32)
    d_gate = jnp.zeros((1, 1152), F32)
    for f in range(2):
        for i, block in enumerate((g0, g1)):
            rows = slice(128 * f + 64 * i, 128 * f + 64 * i + 64)
            cross = slice(128 * f + 64 * (1 - i), 128 * f + 64 * (1 - i) + 64)
            d_hidden = keep[rows, :] + near[rows, :].astype(F32) + far[cross, :].astype(F32)
            norm = normed[rows, :]
            back = norm_back(d_hidden * (1.0 + mod[4:5, :]), norm, root[rows, 0:1])
            mid = block[f].astype(F32) + back
            d_low[rows, :] = (mod[2:3, :] * mid).astype(BF16)
            if i == 0:
                own = slice(64 * f, 64 * f + 64)
                d_mid[own, :] = mid
                d_shift = d_shift + jnp.sum(d_hidden, axis=0, keepdims=True)
                d_scale = d_scale + jnp.sum(d_hidden * norm, axis=0, keepdims=True)
                d_gate = d_gate + jnp.sum(mid * branch[own, :], axis=0, keepdims=True)
    sums[0:1, :] = d_gate
    sums[1:2, :] = d_shift
    sums[2:3, :] = d_scale


def d_attend_body(mine, theirs, parts, probs, attended, out, d_branch, d_slots, d_att):
    join_halves(mine, theirs, d_branch)
    d_att[...] = dot_nn(d_branch[...], out[...]).astype(BF16)
    scale = HEAD_DIM ** (-0.5)

    def place(rows, m, value):
        e, k = divmod(m, 3)
        low = value.astype(BF16)
        for slot in ((0,), (1, 2), (3,))[k]:
            d_slots[rows, 288 * e + 72 * slot : 288 * e + 72 * slot + 72] = low

    for f in range(2):
        rows = slice(256 * f, 256 * f + 256)
        for h in range(4):
            d_out = d_att[rows, 72 * h : 72 * h + 72]
            delta = jnp.sum(d_out.astype(F32) * attended[h, rows, :], axis=-1, keepdims=True)
            prob = probs[4 * f + h]
            d_prob = dot_nt(d_out, parts[8 + h, rows, :])
            d_score = (prob * (d_prob - delta)).astype(BF16)
            place(rows, h, dot_nn(d_score, parts[4 + h, rows, :]) * scale)
            place(rows, 4 + h, dot_tn(d_score, parts[h, rows, :]) * scale)
            place(rows, 8 + h, dot_tn(prob.astype(BF16), d_out))


def grad_first_body(d_slots, hidden, d_branch, low, *refs):
    outs, total, below = refs[:9], refs[9], refs[10]
    total[...] = dot_tn(d_slots[...], hidden[...]).astype(BF16)
    below[...] = dot_tn(d_branch[...], low[...]).astype(BF16)
    for k in range(8):
        at = pl.multiple_of(member_at(NEAR_FIRST[k]) * 144, 144)
        if k < 7:
            outs[k][0:144, :] = total[pl.ds(at, 144), :]
            tail, row = outs[k], 144
        else:
            outs[7][...] = total[pl.ds(at, 96), :]
            outs[8][0:48, :] = total[pl.ds(at + 96, 48), :]
            tail, row = outs[8], 48
        for q in range(3):
            tail[row : row + 48, 288 * q : 288 * q + 288] = below[pl.ds(at + 48 * q, 48), :]
        tail[row : row + 48, 864:1152] = jnp.zeros((48, 288), BF16)


def d_hidden_a_body(d_slots, t0, t1, t2, t3, sums_b, d_gate_b, *refs):
    chunks = refs[:9]
    keep, send = refs[9:11]
    shares = refs[11:15]
    full, total, flat, d_mod, held, sems = refs[15:]
    for copy in load_chunks(chunks, FIRST_PLACES, full, sems):
        copy.wait()
    total[...] = dot_nn(d_slots[...], full[...])
    split_halves(total, keep, send)
    d_shift = jnp.zeros((1, 1152), F32)
    d_scale = jnp.zeros((1, 1152), F32)
    for f in range(2):
        for i, block in enumerate((t0, t1, t2, t3)):
            row = 256 * f + 64 * i
            norm, _ = norm_rows(block[f].astype(F32))
            part = total[row : row + 64, :]
            d_shift = d_shift + jnp.sum(part, axis=0, keepdims=True)
            d_scale = d_scale + jnp.sum(part * norm, axis=0, keepdims=True)
    d_mod[0:1, :] = d_shift
    d_mod[1:2, :] = d_scale
    d_mod[2:5, :] = sums_b[0:3, :]
    d_mod[5:6, :] = d_gate_b[...]
    for m in range(24):
        d, j = divmod(m, 3)
        flat[d : d + 1, 288 * j : 288 * j + 288] = d_mod[m // 4 : m // 4 + 1, 288 * (m % 4) : 288 * (m % 4) + 288]
    blk = lax.axis_index("blk")
    for t in range(4):
        held[t] = flat[:, 216 * t : 216 * t + 216]
    for r in range(4):
        shares[r][...] = held[blk ^ r]


def mod_parts_body(s0, s1, s2, s3, *refs):
    outs, total = refs[:8], refs[8]
    total[...] = s0[...] + s1[...] + s2[...] + s3[...]
    mine = lax.broadcasted_iota(jnp.int32, (8, 216), 0) == lax.axis_index("dp")
    for k, out in enumerate(outs):
        row = total[pl.ds(member_at(NEAR_FIRST[k]), 1), :]
        out[...] = jnp.zeros((8, 1152), BF16)
        out[:, 0:216] = jnp.where(mine, row, 0.0).astype(BF16)


def own_half_body(keep, near, own, cross):
    for f in range(2):
        for i, block in enumerate((own, cross)):
            rows = slice(128 * f + 64 * i, 128 * f + 64 * i + 64)
            part = keep[rows, :] + near[rows, :].astype(F32)
            block[64 * f : 64 * f + 64, :] = part.astype(block.dtype)


def output_body(own, far, middle, mod, output):
    for f in range(2):
        rows = slice(64 * f, 64 * f + 64)
        output[f] = middle[rows, :] + mod[5:6, :] * (own[rows, :] + far[rows, :].astype(F32))


def grad_tokens_body(own, far, t0, d_mid, mod, grad):
    for f in range(2):
        rows = slice(64 * f, 64 * f + 64)
        norm, inv = norm_rows(t0[f].astype(F32))
        d_hidden = own[rows, :] + far[rows, :].astype(F32)
        grad[f] = d_mid[rows, :] + norm_back(d_hidden * (1.0 + mod[1:2, :]), norm, inv)


def cut_updown_body(u0, u1, u2, d0, d1, d2, *refs):
    pieces, held = refs[:4], refs[4]
    blk = lax.axis_index("blk")
    up = u0[...].astype(F32) + u1[0:144, :].astype(F32) + u2[0:144, :].astype(F32)
    down = d0[...].astype(F32) + d1[144:288, :].astype(F32) + d2[144:288, :].astype(F32)
    for t in range(4):
        held[t, :, 0:288] = up[:, 288 * t : 288 * t + 288].astype(BF16)
        held[t, :, 288:576] = down[:, 288 * t : 288 * t + 288].astype(BF16)
        held[t, :, 576:640] = jnp.zeros((144, 64), BF16)
    for r in range(4):
        pieces[r][...] = held[blk ^ r]


def final_updown_body(p0, p1, p2, p3, up, down, held):
    blk = lax.axis_index("blk")
    for r, piece in enumerate((p0, p1, p2, p3)):
        held[blk ^ r] = piece[...]
    for s in range(4):
        up[:, 144 * s : 144 * s + 144] = held[s, :, 0:288].astype(F32).T
        for part in range(2):
            at = 576 * part + 144 * s
            down[:, at : at + 144] = held[s, :, 288 + 144 * part : 432 + 144 * part].astype(F32)


def cut_heads_body(s0, s1, s2, *refs):
    pieces, held = refs[:4], refs[4]
    blk = lax.axis_index("blk")
    total = s0[...].astype(F32) + s1[0:192, :].astype(F32) + s2[0:192, :].astype(F32)
    for t in range(4):
        held[t, :, 0:288] = total[0:144, 288 * t : 288 * t + 288].astype(BF16)
        for q in range(3):
            at = 288 * q + 72 * t
            held[t, 48 * q : 48 * q + 48, 288:360] = total[144:192, at : at + 72].astype(BF16)
        held[t, :, 360:384] = jnp.zeros((144, 24), BF16)
    for r in range(4):
        pieces[r][...] = held[blk ^ r]


def final_heads_body(p0, p1, p2, p3, qkv, out, held, placed):
    blk = lax.axis_index("blk")
    offset = (6 * lax.axis_index("dp")) % 4
    for r, piece in enumerate((p0, p1, p2, p3)):
        sender = blk ^ r
        placed[sender] = piece[0:72, 0:288].astype(F32)
        placed[sender + 4] = piece[72:144, 0:288].astype(F32)
        held[sender] = piece[:, 288:360].astype(F32)
    for i in range(6):
        qkv[:, 72 * i : 72 * i + 72] = placed[i + offset].T
    for s in range(4):
        out[:, 72 * s : 72 * s + 72] = held[s]


def vmem(shape, kind=BF16):
    return (shape, kind)


def local_kernels(tokens, timestep, mod_table, w_qkv, w_out, w_up, w_down, cotangent):
    nd, nb = 8, 4
    ring = Ring(nd, lax.axis_index("dp"))
    group = Group(nb, lax.axis_index("blk"))
    width = tokens.shape[3]
    own_tokens = tokens[0]
    own_cot = cotangent[0]
    full_low = ((512, 1152), BF16)
    chunk_low = ((144, 1152), BF16)
    part_low = [chunk_low] * 7 + [((80, 1152), BF16), ((64, 1152), BF16)]
    half_low = ((256, 1152), BF16)
    half_wide = ((256, 1152), F32)
    own_wide = ((128, 1152), F32)

    def send_out(pieces):
        return [pieces[0]] + [group.swap(pieces[r], r) for r in (1, 2, 3)]

    def add_low(keep, near):
        return (keep + near.astype(F32)).astype(BF16)

    def own_half(keep, near, name):
        return run_kernel(own_half_body, [own_wide, ((128, 1152), BF16)], keep, near, name=name)

    picker = (timestep[:, None] == jnp.arange(mod_table.shape[0], dtype=jnp.int32)[None, :]).astype(BF16)
    table_cols = dot_nn(picker, mod_table).astype(BF16)
    heads_cut = run_kernel(
        pack_heads_body,
        [((160, 384), BF16)] * 4,
        w_qkv, w_out.T, table_cols,
        scratch=[vmem((8, 72, 288)), vmem((4, 144, 72))],
        name="pack_heads",
    )
    heads_got = send_out(heads_cut)
    (first_own,) = run_kernel(
        join_heads_body,
        [((192, 1152), BF16)],
        *heads_got,
        scratch=[vmem((4, 160, 384)), vmem((8, 864), F32)],
        name="join_heads",
    )
    updown_cut = run_kernel(
        pack_updown_body,
        [((144, 640), BF16)] * 4,
        *after((w_up, w_down.T), heads_got[1]),
        scratch=[vmem((4, 144, 288)), vmem((4, 144, 288))],
        name="pack_updown",
    )
    updown_got = send_out(updown_cut)
    fore1, rear1, _ = step(ring, first_own, first_own)
    fore2, rear2, held = step(ring, fore1, rear1, own_tokens, *updown_got)
    far_t = group.swap(held[0], 2)
    up_own, down_own = run_kernel(
        join_updown_body, [chunk_low] * 2, *held[1:], scratch=[vmem((4, 144, 640))], name="join_updown"
    )
    fore3, rear3, held = step(ring, fore2, rear2, up_own, down_own, far_t, own_tokens, own_cot)
    up_own, down_own, far_t, own_t, own_c = held
    token_blocks = [own_tokens, far_t, group.swap(own_t, 1), group.swap(far_t, 1)]
    far_c = group.swap(own_c, 2)
    fore4, rear4, held = step(
        ring, stack(fore3[:96], up_own), stack(rear3[96:], up_own), far_c, own_cot, *token_blocks
    )
    far_c, own_c, *token_blocks = held
    cot_blocks = [own_cot, far_c, group.swap(own_c, 1), group.swap(far_c, 1)]
    first_got = [first_own, fore1, rear1, fore2, rear2, fore3, rear3, fore4, rear4]
    fore5, rear5, held = step(
        ring, stack(fore4[96:], down_own), stack(rear4[96:], down_own), *cot_blocks, *token_blocks, *first_got
    )
    cot_blocks, token_blocks, first_got = held[:4], held[4:8], held[8:]
    hidden_a, parts, probs, attended, low, out_full, mod, keep_a, send_a = run_kernel(
        attend_body,
        [
            full_low,
            ((12, 512, 72), BF16),
            ((8, 256, 256), F32),
            ((4, 512, 72), F32),
            ((512, 288), BF16),
            ((1152, 288), BF16),
            ((8, 1152), F32),
            half_wide,
            half_low,
        ],
        *token_blocks, *first_got,
        spaces=range(4, 13),
        scratch=[vmem((1152, 1152)), vmem((512, 1152)), vmem((384, 1152))],
        sems=2,
        flops=4 * 10**9,
        name="attend",
    )
    fore6, rear6, (keep_a, send_a) = step(ring, fore5, rear5, keep_a, send_a)
    near_a = group.swap(send_a, 1)
    far_a = group.swap(add_low(keep_a, near_a), 2)
    fore7, rear7, (keep_a, near_a, far_a) = step(
        ring, stack(fore6[:80], fore6[144:]), rear6[80:], keep_a, near_a, far_a
    )
    hidden_mine, normed_b, root_b, branch_a, middle = run_kernel(
        middle_body,
        [half_low, half_wide, ((256, 128), F32), own_wide, own_wide],
        keep_a, near_a, far_a, *token_blocks[:2], mod,
        name="middle",
    )
    hidden_theirs = group.swap(hidden_mine, 1)
    fore8, rear8, (hidden_mine, hidden_theirs) = step(ring, fore7[80:160], rear7[144:], hidden_mine, hidden_theirs)
    up_got = [up_own, fore4, rear4, fore5, rear5, fore6, rear6, fore7, rear7]
    down_got = [down_own, fore5, rear5, fore6, rear6, fore7, rear7, fore8, rear8]
    hidden_b, act, slope, d_branch_b, *grad_down = run_kernel(
        up_body,
        [full_low, full_low, ((512, 1152), F32), full_low] + part_low,
        hidden_mine, hidden_theirs, *cot_blocks, mod, *up_got,
        spaces=range(7, 16),
        scratch=[vmem((1152, 1152)), vmem((1152, 1152))],
        sems=1,
        flops=4 * 10**9,
        name="up",
    )
    fore1, rear1, held = step(ring, *grad_down[7:], d_branch_b, slope, *down_got)
    d_branch_b, slope, down_got = held[0], held[1], held[2:]
    d_pre, keep_d, send_d = run_kernel(
        down_body,
        [full_low, half_wide, half_low],
        d_branch_b, slope, *down_got, *up_got,
        spaces=range(2, 20),
        scratch=[vmem((1152, 1152)), vmem((1152, 1152))],
        sems=2,
        flops=4 * 10**9,
        name="down",
    )
    near_d = group.swap(send_d, 1)
    low_d = add_low(keep_d, near_d)
    grad_up = run_kernel(
        grad_body,
        part_low,
        d_pre, hidden_b,
        scratch=[vmem((1152, 1152))],
        flops=2 * 10**9,
        name="grad_up",
    )
    fore2, rear2, (keep_d, near_d, low_d, act) = step(
        ring,
        stack(grad_up[7], sum_low(grad_down[6][:80], fore1), grad_down[6][80:]),
        stack(grad_up[8], grad_down[5][:80], sum_low(grad_down[5][80:], rear1)),
        keep_d, near_d, low_d, act,
    )
    far_d = group.swap(low_d, 2)
    fore3, rear3, (act,) = step(
        ring,
        stack(sum_low(grad_up[6][:80], fore2[:80]), grad_up[6][80:], sum_low(grad_down[4], fore2[80:])),
        stack(grad_up[5][:80], sum_low(grad_up[5][80:], rear2[:64]), sum_low(grad_down[3], rear2[64:])),
        act,
    )
    keep_b, send_b, d_gate_b = run_kernel(
        branch_b_body,
        [half_wide, half_low, ((1, 1152), F32)],
        act, *cot_blocks, *down_got,
        spaces=range(5, 14),
        scratch=[vmem((1152, 1152)), vmem((512, 1152), F32)],
        sems=1,
        flops=2 * 10**9,
        name="branch_b",
    )
    near_b = group.swap(send_b, 1)
    fore4, rear4, held = step(
        ring,
        stack(sum_low(grad_up[4], fore3[:144]), sum_low(grad_down[2], fore3[144:])),
        stack(sum_low(grad_up[3], rear3[:144]), sum_low(grad_down[1], rear3[144:])),
        keep_d, near_d, far_d, keep_b, near_b,
    )
    keep_d, near_d, far_d, keep_b, near_b = held
    own_b, cross_b = own_half(keep_b, near_b, "own_b")
    far_b = group.swap(cross_b, 2)
    d_low, d_mid, sums_b = run_kernel(
        d_middle_body,
        [half_low, own_wide, ((3, 1152), F32)],
        keep_d, near_d, far_d, normed_b, root_b, *cot_blocks[:2], branch_a, mod,
        name="d_middle",
    )
    d_branch_a, d_slots = run_kernel(
        d_attend_body,
        [full_low, full_low],
        d_low, group.swap(d_low, 1), parts, probs, attended, out_full,
        scratch=[vmem((512, 288))],
        flops=3 * 10**9,
        name="d_attend",
    )
    grad_first = run_kernel(
        grad_first_body,
        [((192, 1152), BF16)] * 7 + [((96, 1152), BF16)] * 2,
        d_slots, hidden_a, d_branch_a, low,
        scratch=[vmem((1152, 1152)), vmem((1152, 288))],
        flops=2 * 10**9,
        name="grad_first",
    )
    fore5, rear5, (d_slots, own_b, far_b) = step(
        ring,
        stack(sum_low(grad_up[2], fore4[:144]), grad_first[7]),
        stack(sum_low(grad_up[1], rear4[:144]), grad_first[8]),
        d_slots, own_b, far_b,
    )
    keep_h, send_h, *d_mod = run_kernel(
        d_hidden_a_body,
        [half_wide, half_low] + [((8, 216), F32)] * 4,
        d_slots, *token_blocks, sums_b, d_gate_b, *first_got,
        spaces=range(7, 16),
        scratch=[
            vmem((1152, 1152)),
            vmem((512, 1152), F32),
            vmem((8, 864), F32),
            vmem((6, 1152), F32),
            vmem((4, 8, 216), F32),
        ],
        sems=1,
        flops=2 * 10**9,
        name="d_hidden_a",
    )
    mods = run_kernel(
        mod_parts_body,
        [((8, 1152), BF16)] * 8,
        *send_out(d_mod),
        scratch=[vmem((8, 216), F32)],
        spare=1,
        name="mod_parts",
    )
    near_h = group.swap(send_h, 1)
    fore6, rear6, held = step(
        ring,
        stack(sum_low(grad_first[6][:96], fore5[144:]), grad_first[6][96:], mods[7]),
        stack(grad_first[5][:96], sum_low(grad_first[5][96:], rear5[144:])),
        keep_h, near_h, fore4, rear4, fore5, rear5,
    )
    keep_h, near_h, *up_down = held
    own_h, cross_h = own_half(keep_h, near_h, "own_h")
    far_h = group.swap(cross_h, 2)
    updown_cut = run_kernel(
        cut_updown_body,
        [((144, 640), BF16)] * 4,
        grad_up[0], *up_down[2:], grad_down[0], *up_down[:2],
        scratch=[vmem((4, 144, 640))],
        name="cut_updown",
    )
    fore7, rear7, held = step(
        ring,
        stack(sum_low(grad_first[4], fore6[:192]), sum_low(mods[6], fore6[192:])),
        stack(sum_low(grad_first[3], rear6), mods[5]),
        own_h, far_h, own_b, far_b, *updown_cut,
    )
    own_h, far_h, own_b, far_b, *updown_cut = held
    updown_back = send_out(updown_cut)
    (output,) = run_kernel(
        output_body, [((2, 64, 1152), F32)], own_b, far_b, middle, mod, name="output"
    )
    (grad_tokens,) = run_kernel(
        grad_tokens_body, [((2, 64, 1152), F32)], own_h, far_h, own_tokens, d_mid, mod, name="grad_tokens"
    )
    fore8, rear8, (output, grad_tokens, *updown_back) = step(
        ring,
        stack(sum_low(grad_first[2], fore7[:192]), sum_low(mods[4], fore7[192:])),
        stack(sum_low(grad_first[1], rear7[:192]), sum_low(mods[3], rear7[192:])),
        output, grad_tokens, *updown_back,
    )
    final_up, final_down = run_kernel(
        final_updown_body,
        [((288, 576), F32), ((144, 1152), F32)],
        *updown_back,
        scratch=[vmem((4, 144, 640))],
        name="final_updown",
    )
    fore9, rear9, (final_up, final_down) = step(
        ring, sum_low(mods[2], fore8[192:]), sum_low(mods[1], rear8[192:]), final_up, final_down
    )
    mod_sums = (mods[0].astype(F32) + fore9.astype(F32) + rear9.astype(F32))[:, :216]
    grad_table = lax.dot_general(
        picker.astype(F32),
        mod_sums,
        (((0,), (0,)), ((), ())),
        precision=HIGHEST,
        preferred_element_type=F32,
    )
    heads_cut = run_kernel(
        cut_heads_body, [((144, 384), BF16)] * 4, grad_first[0], fore8, rear8, scratch=[vmem((4, 144, 384))], name="cut_heads"
    )
    final_qkv, final_out = run_kernel(
        final_heads_body,
        [((288, 432), F32), ((144, 288), F32)],
        *send_out(heads_cut),
        scratch=[vmem((4, 144, 72), F32), vmem((8, 72, 288), F32)],
        name="final_heads",
    )
    return (output[None], grad_tokens[None], grad_table, final_qkv, final_out.T, final_up, final_down.T)


def local(tokens, timestep, mod_table, w_qkv, w_out, w_up, w_down, cotangent):
    sizes = (lax.axis_size("dp"), lax.axis_size("blk"), tokens.shape, w_qkv.shape, w_up.shape, w_down.shape)
    known = (8, 4, (1, 2, 64, 1152), (288, 432), (288, 576), (1152, 144))
    chosen = local_kernels if sizes == known else local_plain
    return chosen(tokens, timestep, mod_table, w_qkv, w_out, w_up, w_down, cotangent)


def solution(mesh):
    in_specs = (
        P("dp", None, "blk", None),
        P(),
        P(None, ("dp", "blk")),
        P("blk", "dp"),
        P("blk", "dp"),
        P("blk", "dp"),
        P("blk", "dp"),
        P("dp", None, "blk", None),
    )
    out_specs = (
        P("dp", None, "blk", None),
        P("dp", None, "blk", None),
        P(None, ("dp", "blk")),
        P("blk", "dp"),
        P("blk", "dp"),
        P("blk", "dp"),
        P("blk", "dp"),
    )
    return jax.shard_map(local, mesh=mesh, in_specs=in_specs, out_specs=out_specs, check_vma=False)
```

```python
import math
from functools import partial

import jax
import jax.numpy as jnp
from jax import lax
from jax.experimental import pallas as pl
from jax.experimental.pallas import tpu as pltpu
from jax.sharding import PartitionSpec as P

HEADS = 16
HEAD_DIM = 72
EPS = 1e-06
HIGHEST = lax.Precision.HIGHEST
BF16 = jnp.bfloat16
F32 = jnp.float32


def norm_rows(values):
    center = values - jnp.mean(values, axis=-1, keepdims=True)
    spread = jnp.mean(center * center, axis=-1, keepdims=True)
    root_inv = lax.rsqrt(spread + EPS)
    return (center * root_inv, root_inv)


def norm_back(d_normed, normed, root_inv):
    mean_one = jnp.mean(d_normed, axis=-1, keepdims=True)
    mean_two = jnp.mean(d_normed * normed, axis=-1, keepdims=True)
    return root_inv * (d_normed - mean_one - normed * mean_two)


def dot_nn(left, right):
    return jnp.dot(left, right, preferred_element_type=F32)


def dot_tn(left, right):
    return lax.dot_general(left, right, (((0,), (0,)), ((), ())), preferred_element_type=F32)


def dot_nt(left, right):
    return lax.dot_general(left, right, (((1,), (1,)), ((), ())), preferred_element_type=F32)


class Ring:
    def __init__(self, size, index):
        self.size = size
        self.order = list(range(0, size, 2)) + list(range(size - 1, 0, -2))
        place = [0] * size
        for spot, member in enumerate(self.order):
            place[member] = spot
        self.spot = jnp.array(place, jnp.int32)[index]
        self.table = jnp.array(self.order, jnp.int32)
        self.ahead = [(self.order[i], self.order[(i + 1) % size]) for i in range(size)]
        self.back = [(right, left) for left, right in self.ahead]

    def member(self, offset):
        return self.table[(self.spot + offset) % self.size]

    def gather(self, chunk):
        half = self.size // 2
        cut = chunk.shape[0] // 2
        out = jnp.zeros((self.size,) + chunk.shape, chunk.dtype)

        def put(out, piece, offset, row=0):
            return lax.dynamic_update_slice(out, piece[None], (self.member(offset), row, 0))

        out = put(out, chunk, 0)
        fore = rear = chunk
        for step in range(1, half):
            fore = lax.ppermute(fore, "dp", self.ahead)
            rear = lax.ppermute(rear, "dp", self.back)
            out = put(put(out, fore, -step), rear, step)
        fore = lax.ppermute(fore[:cut], "dp", self.ahead)
        rear = lax.ppermute(rear[cut:], "dp", self.back)
        return put(put(out, fore, half), rear, half, cut)

    def scatter(self, parts):
        half = self.size // 2
        cut = parts.shape[1] // 2

        def own(offset):
            return lax.dynamic_index_in_dim(parts, self.member(offset), 0, keepdims=False)

        far = own(half)
        fore = lax.ppermute(far[:cut], "dp", self.ahead)
        rear = lax.ppermute(far[cut:], "dp", self.back)
        for step in range(half - 1, 0, -1):
            mine_fore = own(step).astype(F32)
            mine_rear = own(-step).astype(F32)
            if step == half - 1:
                fore = jnp.concatenate([mine_fore[:cut] + fore.astype(F32), mine_fore[cut:]], axis=0)
                rear = jnp.concatenate([mine_rear[:cut], mine_rear[cut:] + rear.astype(F32)], axis=0)
            else:
                fore = mine_fore + fore.astype(F32)
                rear = mine_rear + rear.astype(F32)
            fore = lax.ppermute(fore.astype(BF16), "dp", self.ahead)
            rear = lax.ppermute(rear.astype(BF16), "dp", self.back)
        return own(0).astype(F32) + fore.astype(F32) + rear.astype(F32)


class Group:
    def __init__(self, size, index):
        self.size = size
        self.index = index
        self.bits = []
        bit = size // 2
        while bit:
            self.bits.append(bit)
            bit //= 2

    def swap(self, values, bit):
        return lax.ppermute(values, "blk", [(i, i ^ bit) for i in range(self.size)])

    def exchange(self, pieces):
        if self.size > 4:
            return lax.all_to_all(pieces, "blk", 0, 0, tiled=True)
        got = []
        for r in range(self.size):
            piece = lax.dynamic_index_in_dim(pieces, self.index ^ r, 0, keepdims=False)
            got.append(self.swap(piece, r) if r else piece)
        bit = 1
        while bit < self.size:
            odd = (self.index & bit) != 0
            got = [jnp.where(odd, got[r ^ bit], got[r]) for r in range(self.size)]
            bit *= 2
        return jnp.stack(got)

    def gather(self, block, bits=None):
        for bit in self.bits if bits is None else bits:
            block = jnp.concatenate([block, self.swap(block, bit)], axis=0)
        return block

    def scatter(self, parts, share):
        for bit in reversed(self.bits[1:]):
            half = parts.shape[0] // 2
            parts = parts[:half] + self.swap(parts[half:].astype(BF16), bit).astype(F32)
        top = self.bits[0]
        if share:
            return parts + self.swap(parts.astype(BF16), top)[::-1].astype(F32)
        return parts[:1] + self.swap(parts[1:].astype(BF16), top).astype(F32)


def local_plain(tokens, timestep, mod_table, w_qkv, w_out, w_up, w_down, cotangent):
    frames, patches, width = tokens.shape[1:]
    nd = lax.axis_size("dp")
    nb = lax.axis_size("blk")
    dp = lax.axis_index("dp")
    blk = lax.axis_index("blk")
    ring = Ring(nd, dp)
    group = Group(nb, blk)
    rows = nb * frames * patches
    scale = HEAD_DIM ** (-0.5)
    heads = HEADS // nb
    deep = width // nb
    ff = w_down.shape[0]
    hidden = w_up.shape[1]
    out_cols = w_out.shape[1]

    columns = w_qkv.shape[1] // HEAD_DIM
    slots = -(-columns // nb)
    offset = (columns * dp) % nb
    qkv_t = w_qkv.T.reshape(columns, HEAD_DIM, deep)
    qkv_pos = jnp.zeros((2 * slots * nb, HEAD_DIM, deep), BF16)
    qkv_pos = lax.dynamic_update_slice(qkv_pos, qkv_t, (offset, 0, 0))
    qkv_pos = qkv_pos[: slots * nb] + qkv_pos[slots * nb :]
    qkv_send = qkv_pos.reshape(slots, nb, HEAD_DIM, deep).transpose(1, 0, 2, 3)
    qkv_send = qkv_send.reshape(nb, slots * HEAD_DIM, deep)
    spread = heads // nb
    if spread:
        out_send = w_out.T.reshape(out_cols, spread, nb, HEAD_DIM).transpose(2, 0, 1, 3)
        out_send = out_send.reshape(nb, out_cols, spread * HEAD_DIM)
    up_send = w_up.T.reshape(nb, hidden // nb, deep)
    many = ff // hidden
    down_send = w_down.T.reshape(out_cols, many, nb, hidden // nb).transpose(2, 0, 1, 3)
    down_send = down_send.reshape(nb, out_cols, many * hidden // nb)
    first = group.exchange(jnp.concatenate([qkv_send, out_send], axis=2) if spread else qkv_send)
    up_got = group.exchange(up_send)
    down_got = group.exchange(down_send)
    qkv_own = first[:, :, :deep].transpose(1, 0, 2).reshape(slots * HEAD_DIM, width)
    out_own = first[:, :, deep:].transpose(1, 0, 2).reshape(out_cols, heads * HEAD_DIM) if spread else w_out.T
    up_own = up_got.transpose(1, 0, 2).reshape(hidden // nb, width)
    down_own = down_got.transpose(1, 0, 2).reshape(out_cols, nd * hidden // nb)

    token_all = group.gather(tokens)
    cot_all = group.gather(cotangent)

    picker = (timestep[:, None] == jnp.arange(mod_table.shape[0], dtype=jnp.int32)[None, :]).astype(BF16)
    table_cols = dot_nn(picker, mod_table).astype(BF16)
    piece = table_cols.shape[1]
    mods_send = jnp.broadcast_to(table_cols[:, None, :], (nd, nb, piece)).reshape(nd * nb, piece)
    mod_row = lax.all_to_all(mods_send, ("dp", "blk"), 0, 0, tiled=True).reshape(6, width).astype(F32)
    shift_a, scale_a, gate_a, shift_b, scale_b, gate_b = (mod_row[i] for i in range(6))

    first_all = ring.gather(jnp.concatenate([qkv_own, out_own], axis=1))
    up_full = ring.gather(up_own).reshape(ff, width)
    down_full = ring.gather(down_own).reshape(width, ff)
    out_full = first_all[:, :, width:].reshape(width, heads * HEAD_DIM)
    wanted = blk + nb * jnp.arange(3 * heads, dtype=jnp.int32)
    holder = wanted // columns
    place = ((wanted - columns * holder + (columns * holder) % nb) % (slots * nb)) // nb
    slot_of = holder * slots + place
    qkv_slots = first_all[:, :, :width].reshape(nd * slots, HEAD_DIM, width)
    qkv_full = jnp.take(qkv_slots, slot_of, axis=0).reshape(3 * heads * HEAD_DIM, width)

    inputs = token_all.reshape(rows, width).astype(F32)
    normed_a, root_a = norm_rows(inputs)
    hidden_a = (normed_a * (1.0 + scale_a) + shift_a).astype(BF16)
    projected = dot_nt(hidden_a, qkv_full).astype(BF16)

    def by_head(values, parts):
        split = values.reshape(nb, frames, patches, parts, heads, HEAD_DIM)
        split = split.transpose(3, 1, 4, 0, 2, 5)
        return split.reshape(parts, frames, heads, nb * patches, HEAD_DIM)

    def by_row(values):
        split = values.reshape(-1, frames, heads, nb, patches, HEAD_DIM)
        return split.transpose(3, 1, 4, 0, 2, 5).reshape(rows, -1)

    query, keys, values = by_head(projected, 3)
    scores = jnp.einsum("fhqe,fhke->fhqk", query, keys, preferred_element_type=F32) * scale
    top = jnp.max(scores, axis=-1, keepdims=True)
    weights = jnp.exp(scores - top)
    probs = weights / jnp.sum(weights, axis=-1, keepdims=True)
    probs_low = probs.astype(BF16)
    attended = jnp.einsum("fhqk,fhke->fhqe", probs_low, values, preferred_element_type=F32)
    attn_low = by_row(attended).astype(BF16)
    share = 2 * frames * patches
    own = frames * patches

    def blocks(partial_sum):
        return partial_sum.reshape(nb, own, width)

    branch_a = group.scatter(blocks(dot_nt(attn_low, out_full)), True).reshape(share, width)
    middle = inputs[:share] + gate_a * branch_a
    normed_b, root_b = norm_rows(middle)
    hidden_low = (normed_b * (1.0 + scale_b) + shift_b).astype(BF16)
    hidden_b = group.gather(hidden_low.reshape(2, own, width), group.bits[1:]).reshape(rows, width)
    pre_act = dot_nt(hidden_b, up_full)
    activated, gelu_back = jax.vjp(partial(jax.nn.gelu, approximate=True), pre_act)
    act_low = activated.astype(BF16)
    grad_in = cot_all.reshape(rows, width).astype(F32)
    d_branch_b = (gate_b * grad_in).astype(BF16)
    grad_down = dot_tn(d_branch_b, act_low).astype(BF16)
    down_sum = ring.scatter(grad_down.reshape(nd, out_cols, ff))
    d_act = dot_nn(d_branch_b, down_full)
    d_pre = gelu_back(d_act)[0].astype(BF16)
    grad_up = dot_tn(d_pre, hidden_b).astype(BF16)
    up_sum = ring.scatter(grad_up.reshape(nd, hidden // nb, width))
    d_hidden_b = group.scatter(blocks(dot_nn(d_pre, up_full)), True).reshape(share, width)
    branch_b = group.scatter(blocks(dot_nt(act_low, down_full)), False).reshape(own, width)
    output = (middle[:own] + gate_b * branch_b).reshape(tokens.shape)
    d_gate_b = jnp.sum(grad_in[:own] * branch_b, axis=0)
    d_shift_b = jnp.sum(d_hidden_b[:own], axis=0)
    d_scale_b = jnp.sum(d_hidden_b[:own] * normed_b[:own], axis=0)
    d_middle = grad_in[:share] + norm_back(d_hidden_b * (1.0 + scale_b), normed_b, root_b)
    d_gate_a = jnp.sum(d_middle[:own] * branch_a[:own], axis=0)
    d_branch_a = (gate_a * d_middle).astype(BF16).reshape(2, own, width)
    d_branch_a = group.gather(d_branch_a, group.bits[1:]).reshape(rows, width)
    grad_out = dot_tn(d_branch_a, attn_low).astype(BF16)
    d_attended = dot_nn(d_branch_a, out_full).astype(BF16)
    d_att = by_head(d_attended, 1)[0]
    delta = jnp.sum(d_att.astype(F32) * attended, axis=-1, keepdims=True)
    d_probs = jnp.einsum("fhqe,fhke->fhqk", d_att, values, preferred_element_type=F32)
    d_scores = (probs * (d_probs - delta)).astype(BF16)
    d_query = jnp.einsum("fhqk,fhke->fhqe", d_scores, keys, preferred_element_type=F32) * scale
    d_key = jnp.einsum("fhqk,fhqe->fhke", d_scores, query, preferred_element_type=F32) * scale
    d_value = jnp.einsum("fhqk,fhqe->fhke", probs_low, d_att, preferred_element_type=F32)
    d_projected = by_row(jnp.stack([d_query, d_key, d_value]).astype(BF16))
    grad_qkv = dot_tn(d_projected, hidden_a).astype(BF16).reshape(3 * heads, HEAD_DIM, width)
    grad_slots = jnp.zeros((nd * slots, HEAD_DIM, width), BF16).at[slot_of].set(grad_qkv)
    grad_first = jnp.concatenate(
        [
            grad_slots.reshape(nd, slots * HEAD_DIM, width),
            grad_out.reshape(nd, out_cols, heads * HEAD_DIM),
        ],
        axis=2,
    )
    first_sum = ring.scatter(grad_first)
    d_hidden_a = group.scatter(blocks(dot_nn(d_projected, qkv_full)), False).reshape(own, width)
    d_shift_a = jnp.sum(d_hidden_a, axis=0)
    d_scale_a = jnp.sum(d_hidden_a * normed_a[:own], axis=0)
    d_normed = norm_back(d_hidden_a * (1.0 + scale_a), normed_a[:own], root_a[:own])
    grad_tokens = (d_middle[:own] + d_normed).reshape(tokens.shape)

    d_mod = jnp.concatenate([d_shift_a, d_scale_a, d_gate_a, d_shift_b, d_scale_b, d_gate_b])
    mod_got = lax.all_to_all(d_mod.reshape(nd * nb, piece), ("dp", "blk"), 0, 0, tiled=True)
    mod_sums = jnp.sum(mod_got.reshape(nd, nb, piece), axis=1)
    grad_table = lax.dot_general(
        picker.astype(F32),
        mod_sums,
        (((0,), (0,)), ((), ())),
        precision=HIGHEST,
        preferred_element_type=F32,
    )

    up_back = group.exchange(up_sum.astype(BF16).reshape(hidden // nb, nb, deep).transpose(1, 0, 2))
    final_up = up_back.reshape(hidden, deep).T.astype(F32)
    down_back = down_sum.astype(BF16).reshape(out_cols, nb, many, hidden // nb).transpose(1, 0, 2, 3)
    down_back = group.exchange(down_back.reshape(nb, out_cols, many * hidden // nb))
    down_back = down_back.reshape(nb, out_cols, many, hidden // nb).transpose(2, 0, 3, 1)
    final_down = down_back.reshape(ff, out_cols).astype(F32)
    first_low = first_sum.astype(BF16)
    qkv_back = first_low[:, :width].reshape(slots * HEAD_DIM, nb, deep).transpose(1, 0, 2)
    out_back = first_low[:, width:]
    if spread:
        out_back = out_back.reshape(out_cols, nb, spread * HEAD_DIM).transpose(1, 0, 2)
        back = group.exchange(jnp.concatenate([qkv_back, out_back], axis=2))
        out_back = back[:, :, deep:].reshape(nb, out_cols, spread, HEAD_DIM).transpose(2, 0, 3, 1)
        final_out = out_back.reshape(deep, out_cols).astype(F32)
    else:
        back = group.exchange(qkv_back)
        final_out = out_back.T.astype(F32)
    qkv_back = back[:, :, :deep].reshape(nb, slots, HEAD_DIM, deep).transpose(1, 0, 2, 3)
    qkv_back = qkv_back.reshape(slots * nb, HEAD_DIM, deep)
    qkv_back = lax.dynamic_slice(
        jnp.concatenate([qkv_back, qkv_back], axis=0), (offset, 0, 0), (columns, HEAD_DIM, deep)
    )
    final_qkv = qkv_back.reshape(columns * HEAD_DIM, deep).T.astype(F32)
    return (output, grad_tokens, grad_table, final_qkv, final_out, final_up, final_down)


GELU_IN = 0.7978845608028654
GELU_CUBE = 0.044715


def padded_bytes(shape, kind):
    *lead, rows, lanes = shape
    return math.prod(lead) * -(-rows // 16) * 16 * -(-lanes // 128) * 128 * jnp.dtype(kind).itemsize


def run_kernel(body, outs, *args, scratch=(), spare=8, flops=0, name=None):
    held = list(outs) + list(scratch) + [(a.shape, a.dtype) for a in args]
    limit = sum(padded_bytes(*h) for h in held) + (spare << 20)
    moved = sum(padded_bytes(*o) for o in outs) + sum(padded_bytes(a.shape, a.dtype) for a in args)
    return pl.pallas_call(
        body,
        out_shape=[jax.ShapeDtypeStruct(shape, t) for shape, t in outs],
        in_specs=[pl.BlockSpec(memory_space=pltpu.VMEM) for _ in args],
        out_specs=[pl.BlockSpec(memory_space=pltpu.VMEM) for _ in outs],
        scratch_shapes=[pltpu.VMEM(*h) for h in scratch],
        compiler_params=pltpu.CompilerParams(vmem_limit_bytes=limit),
        cost_estimate=pl.CostEstimate(flops=flops, bytes_accessed=moved, transcendentals=0),
        name=name,
    )(*args)


def after(value, *others):
    return lax.optimization_barrier((value, *others))[0]


def step(ring, fore, rear, *carry):
    (fore, rear), carry = lax.optimization_barrier(((fore, rear), carry))
    return lax.ppermute(fore, "dp", ring.ahead), lax.ppermute(rear, "dp", ring.back), carry


def sum_low(mine, got):
    return (mine.astype(F32) + got.astype(F32)).astype(BF16)


def stack(*blocks):
    return jnp.concatenate(blocks, axis=0)


NEAR_FIRST = (0, -1, 1, -2, 2, -3, 3, 4)


def member_at(offset):
    dp = lax.axis_index("dp")
    spot = jnp.where(dp % 2 == 0, dp // 2, 7 - dp // 2)
    at = (spot + offset + 8) % 8
    return jnp.where(at < 4, 2 * at, 15 - 2 * at)


def kind_of(device):
    return (device >> 1) | ((device & 1) << 1)


def columns_of(device):
    odd = lax.axis_index("dp") & 1
    return kind_of(device) + 2 * odd, (device >> 1) + 4 - 4 * odd


def turn(values):
    return values.astype(F32).T.astype(BF16)


def pack_heads_body(qkv, out, mods, *refs):
    heads, held_q, held_o = refs[:4], refs[4], refs[5]
    blk = lax.axis_index("blk")
    for i in range(6):
        for half in range(2):
            at = 72 * i + 36 * half
            held_q[half, i] = turn(qkv[:, at : at + 36])
    for t in range(4):
        held_o[t] = out[:, 72 * kind_of(t) : 72 * kind_of(t) + 72]
    for r in range(4):
        t = blk ^ r
        alone, shared = columns_of(t)
        heads[r][...] = jnp.zeros((144, 384), BF16)
        heads[r][0:36, 0:288] = held_q[0, alone]
        heads[r][36:72, 0:288] = held_q[1, alone]
        heads[r][72:108, 0:288] = held_q[t & 1, shared]
        heads[r][112:120, 0:216] = mods[...]
        heads[r][:, 288:360] = held_o[t]


def pack_updown_body(up, down, *refs):
    updown, held_u, held_d = refs[:4], refs[4], refs[5]
    blk = lax.axis_index("blk")
    for t in range(4):
        held_u[t] = turn(up[:, 144 * t : 144 * t + 144])
        for part in range(2):
            at = 576 * part + 144 * t
            held_d[t, :, 144 * part : 144 * part + 144] = down[:, at : at + 144]
    for r in range(4):
        t = blk ^ r
        updown[r][:, 0:288] = held_u[t]
        updown[r][:, 288:576] = held_d[t]
        updown[r][:, 576:640] = jnp.zeros((144, 64), BF16)


def join_heads_body(*refs):
    pieces, joined, held, row = refs[:4], refs[4], refs[5], refs[6]
    blk = lax.axis_index("blk")
    for r in range(4):
        held[blk ^ r] = pieces[r][...]
    joined[96:160, :] = jnp.zeros((64, 1152), BF16)
    for s in range(4):
        joined[0:108, 288 * s : 288 * s + 288] = held[s, 0:108, 0:288]
        for q in range(3):
            at = 288 * q + 72 * s
            joined[112:160, at : at + 72] = held[s, 48 * q : 48 * q + 48, 288:360]
        row[:, 216 * s : 216 * s + 216] = held[s, 112:120, 0:216].astype(F32)
    for j in range(3):
        joined[112 + 16 * j : 120 + 16 * j, 864:1152] = row[:, 288 * j : 288 * j + 288].astype(BF16)


def join_updown_body(*refs):
    pieces, up, down, held = refs[:4], refs[4], refs[5], refs[6]
    blk = lax.axis_index("blk")
    for r in range(4):
        held[blk ^ r] = pieces[r][...]
    for s in range(4):
        up[:, 288 * s : 288 * s + 288] = held[s, :, 0:288]
        down[:, 288 * s : 288 * s + 288] = held[s, :, 288:576]


FIRST_PLACES = (
    (0, 0, 0, 160, 0),
    (-1, 1, 0, 160, 0),
    (1, 2, 0, 160, 0),
    (-2, 3, 0, 160, 0),
    (2, 4, 0, 160, 0),
    (-3, 5, 0, 160, 0),
    (3, 6, 0, 160, 0),
    (4, 7, 0, 80, 0),
    (4, 8, 0, 80, 80),
)
UP_PLACES = (
    (0, 0, 0, 144, 0),
    (-1, 2, 80, 144, 0),
    (1, 3, 80, 144, 0),
    (-2, 4, 0, 144, 0),
    (2, 5, 0, 144, 0),
    (-3, 6, 0, 144, 0),
    (3, 7, 0, 144, 0),
    (4, 8, 0, 80, 0),
    (4, 9, 0, 64, 80),
)
DOWN_PLACES = (
    (0, 1, 0, 144, 0),
    (-1, 4, 144, 144, 0),
    (1, 5, 144, 144, 0),
    (-2, 6, 144, 144, 0),
    (2, 7, 144, 144, 0),
    (-3, 8, 80, 144, 0),
    (3, 9, 64, 144, 0),
    (4, 10, 0, 80, 0),
    (4, 11, 0, 64, 80),
)


def load_chunks(arrays, places, full, first=0, count=144, pitch=None):
    pitch = pitch or count
    for offset, index, start, rows, row in places:
        low, high = max(first, row), min(first + count, row + rows)
        if low < high:
            at = pl.multiple_of(member_at(offset) * pitch + low - first, 16)
            full[pl.ds(at, high - low), :] = arrays[index][start + low - row : start + high - row, :]


def split_halves(total, keep, send):
    for f in range(2):
        keep[128 * f : 128 * f + 128, :] = total[256 * f : 256 * f + 128, :]
        send[128 * f : 128 * f + 128, :] = total[256 * f + 128 : 256 * f + 256, :].astype(BF16)


def join_halves(mine, theirs, full):
    for f in range(2):
        full[256 * f : 256 * f + 128, :] = mine[128 * f : 128 * f + 128, :]
        full[256 * f + 128 : 256 * f + 256, :] = theirs[128 * f : 128 * f + 128, :]


def attend_body(t0, t1, t2, t3, halves, *refs):
    chunks = refs[:9]
    hidden, parts, probs, attended, low, out, mod, keep, send = refs[9:18]
    full, slots, tail = refs[18:]
    load_chunks(chunks, FIRST_PLACES, tail, 112, 48)
    load_chunks(chunks, FIRST_PLACES, full, 0, 112, 160)
    clip = lax.axis_index("dp")
    own = lax.broadcasted_iota(jnp.int32, (8, 288), 0) == clip
    for m in range(24):
        d, j = divmod(m, 3)
        rows = tail[48 * d + 16 * j : 48 * d + 16 * j + 8, 864:1152].astype(F32)
        row = jnp.sum(jnp.where(own, rows, 0.0), axis=0, keepdims=True)
        mod[m // 4 : m // 4 + 1, 288 * (m % 4) : 288 * (m % 4) + 288] = row
        out[48 * m : 48 * m + 48, :] = tail[48 * d : 48 * d + 48, 288 * j : 288 * j + 288]
    for i, block in enumerate((t0, t1, t2, t3)):
        for f in range(2):
            normed, _ = norm_rows(block[f].astype(F32))
            at = 256 * f + 64 * i
            hidden[at : at + 64, :] = (normed * (1.0 + mod[1:2, :]) + mod[0:1, :]).astype(BF16)
    for k, offset in enumerate(NEAR_FIRST):
        at = pl.multiple_of(member_at(offset) * 160 + 112, 16)
        full[pl.ds(at, 48), :] = jnp.concatenate([halves[40 * k : 40 * k + 40, :], jnp.zeros((8, 1152), BF16)], axis=0)
    slots[...] = dot_nt(hidden[...], full[...]).astype(BF16)
    first = lax.axis_index("blk") % 2 == 0
    for e in range(4):
        at = 320 * e
        parts[3 * e] = slots[:, at : at + 72]
        parts[3 * e + 2] = slots[:, at + 160 : at + 232]
        near = jnp.where(first, slots[:, at + 72 : at + 108], slots[:, at + 272 : at + 308])
        far = jnp.where(first, slots[:, at + 112 : at + 148], slots[:, at + 232 : at + 268])
        parts[3 * e + 1, :, 0:36] = near
        parts[3 * e + 1, :, 36:72] = far
    scale = HEAD_DIM ** (-0.5)
    for f in range(2):
        rows = slice(256 * f, 256 * f + 256)
        for h in range(4):
            scores = dot_nt(parts[h, rows, :], parts[4 + h, rows, :]) * scale
            weights = jnp.exp(scores - jnp.max(scores, axis=-1, keepdims=True))
            prob = weights / jnp.sum(weights, axis=-1, keepdims=True)
            probs[4 * f + h] = prob
            mixed = dot_nn(prob.astype(BF16), parts[8 + h, rows, :])
            attended[h, rows, :] = mixed
            low[rows, 72 * h : 72 * h + 72] = mixed.astype(BF16)
    split_halves(dot_nt(low[...], out[...]), keep, send)


def middle_body(keep, near, far, t0, t1, mod, hidden, normed, root, branch, middle):
    for f in range(2):
        for i, block in enumerate((t0, t1)):
            rows = slice(128 * f + 64 * i, 128 * f + 64 * i + 64)
            cross = slice(128 * f + 64 * (1 - i), 128 * f + 64 * (1 - i) + 64)
            part = keep[rows, :] + near[rows, :].astype(F32) + far[cross, :].astype(F32)
            mid = block[f].astype(F32) + mod[2:3, :] * part
            norm, inv = norm_rows(mid)
            hidden[rows, :] = (norm * (1.0 + mod[4:5, :]) + mod[3:4, :]).astype(BF16)
            normed[rows, :] = norm
            root[rows, :] = jnp.broadcast_to(inv, (64, 128))
            if i == 0:
                branch[64 * f : 64 * f + 64, :] = part
                middle[64 * f : 64 * f + 64, :] = mid


def write_parts(total, outs):
    cut = outs[7].shape[0]
    for k in range(8):
        at = pl.multiple_of(member_at(NEAR_FIRST[k]) * 144, 144)
        if k < 7:
            outs[k][...] = total[pl.ds(at, 144), :]
        else:
            outs[7][...] = total[pl.ds(at, cut), :]
            outs[8][...] = total[pl.ds(at + cut, 144 - cut), :]


def up_body(mine, theirs, g0, g1, g2, g3, mod, *refs):
    chunks = refs[:10]
    hidden, act, slope, d_branch = refs[10:14]
    parts = refs[14:23]
    up, total = refs[23:]
    load_chunks(chunks, UP_PLACES, up)
    join_halves(mine, theirs, hidden)
    for f in range(2):
        for i, block in enumerate((g0, g1, g2, g3)):
            row = 256 * f + 64 * i
            d_branch[row : row + 64, :] = (mod[5:6, :] * block[f].astype(F32)).astype(BF16)
    for at in range(0, 512, 128):
        rows = slice(at, at + 128)
        pre = dot_nt(hidden[rows, :], up[...])
        square = pre * pre
        bend = jnp.tanh(GELU_IN * (pre + GELU_CUBE * (square * pre)))
        half = 0.5 * (1.0 + bend)
        act[rows, :] = (pre * half).astype(BF16)
        inner = GELU_IN * (1.0 + (3.0 * GELU_CUBE) * square)
        slope[rows, :] = half + (0.5 * pre) * ((1.0 - bend * bend) * inner)
    total[...] = dot_tn(d_branch[...], act[...]).astype(BF16)
    write_parts(total, parts)


def down_body(d_branch, slope, *refs):
    chunks = refs[:12]
    d_pre, keep, send, down, up = refs[12:]
    load_chunks(chunks, DOWN_PLACES, down)
    load_chunks(chunks, UP_PLACES, up)
    d_pre[...] = (dot_nn(d_branch[...], down[...]) * slope[...]).astype(BF16)
    split_halves(dot_nn(d_pre[...], up[...]), keep, send)


def grad_body(left, right, *refs):
    parts, total = refs[:9], refs[9]
    total[...] = dot_tn(left[...], right[...]).astype(BF16)
    write_parts(total, parts)


def branch_b_body(act, g0, g1, g2, g3, *refs):
    chunks = refs[:12]
    keep, send, d_gate, full, total = refs[12:]
    load_chunks(chunks, DOWN_PLACES, full)
    total[...] = dot_nt(act[...], full[...])
    split_halves(total, keep, send)
    gate = jnp.zeros((1, 1152), F32)
    for f in range(2):
        for i, block in enumerate((g0, g1, g2, g3)):
            row = 256 * f + 64 * i
            gate = gate + jnp.sum(block[f].astype(F32) * total[row : row + 64, :], axis=0, keepdims=True)
    d_gate[...] = gate


def d_middle_body(keep, near, far, normed, root, g0, g1, branch, mod, d_low, d_mid, sums):
    d_shift = jnp.zeros((1, 1152), F32)
    d_scale = jnp.zeros((1, 1152), F32)
    d_gate = jnp.zeros((1, 1152), F32)
    for f in range(2):
        for i, block in enumerate((g0, g1)):
            rows = slice(128 * f + 64 * i, 128 * f + 64 * i + 64)
            cross = slice(128 * f + 64 * (1 - i), 128 * f + 64 * (1 - i) + 64)
            d_hidden = keep[rows, :] + near[rows, :].astype(F32) + far[cross, :].astype(F32)
            norm = normed[rows, :]
            back = norm_back(d_hidden * (1.0 + mod[4:5, :]), norm, root[rows, 0:1])
            mid = block[f].astype(F32) + back
            d_low[rows, :] = (mod[2:3, :] * mid).astype(BF16)
            if i == 0:
                own = slice(64 * f, 64 * f + 64)
                d_mid[own, :] = mid
                d_shift = d_shift + jnp.sum(d_hidden, axis=0, keepdims=True)
                d_scale = d_scale + jnp.sum(d_hidden * norm, axis=0, keepdims=True)
                d_gate = d_gate + jnp.sum(mid * branch[own, :], axis=0, keepdims=True)
    sums[0:1, :] = d_gate
    sums[1:2, :] = d_shift
    sums[2:3, :] = d_scale


def d_attend_body(mine, theirs, parts, probs, attended, out, d_branch, d_slots, d_others, d_att):
    join_halves(mine, theirs, d_branch)
    d_att[...] = dot_nn(d_branch[...], out[...]).astype(BF16)
    scale = HEAD_DIM ** (-0.5)

    first = lax.axis_index("blk") % 2 == 0
    d_slots[...] = jnp.zeros_like(d_slots)

    def place(rows, m, value):
        e, k = divmod(m, 3)
        low = value.astype(BF16)
        at = 224 * e
        if k == 0:
            d_slots[rows, at : at + 72] = low
        elif k == 2:
            d_slots[rows, at + 112 : at + 184] = low
        else:
            near = jnp.where(first, low[:, 0:36], low[:, 36:72])
            d_slots[rows, at + 72 : at + 108] = near
            d_slots[rows, at + 184 : at + 220] = near
            other = jnp.where(first, low[:, 36:72], low[:, 0:36])
            start = rows.start
            d_others[start : start + 128, 36 * e : 36 * e + 36] = other[128:256]
            d_others[start + 128 : start + 256, 36 * e : 36 * e + 36] = other[0:128]

    for f in range(2):
        rows = slice(256 * f, 256 * f + 256)
        for h in range(4):
            d_out = d_att[rows, 72 * h : 72 * h + 72]
            delta = jnp.sum(d_out.astype(F32) * attended[h, rows, :], axis=-1, keepdims=True)
            prob = probs[4 * f + h]
            d_prob = dot_nt(d_out, parts[8 + h, rows, :])
            d_score = (prob * (d_prob - delta)).astype(BF16)
            place(rows, h, dot_nn(d_score, parts[4 + h, rows, :]) * scale)
            place(rows, 4 + h, dot_tn(d_score, parts[h, rows, :]) * scale)
            place(rows, 8 + h, dot_tn(prob.astype(BF16), d_out))


def grad_first_body(d_mine, d_others, hidden, d_branch, low, *refs):
    outs, d_slots, total, below = refs[:9], refs[9], refs[10], refs[11]
    first = lax.axis_index("blk") % 2 == 0
    d_slots[...] = d_mine[...]
    for e in range(4):
        other = d_others[:, 36 * e : 36 * e + 36]
        for odd in range(2):
            at = 224 * e + 112 * odd + 72
            mine = d_mine[:, at : at + 36]
            d_slots[:, at : at + 36] = jnp.where(first == (odd == 0), mine, other)
    total[...] = dot_tn(d_slots[...], hidden[...]).astype(BF16)
    below[...] = dot_tn(d_branch[...], low[...]).astype(BF16)
    for k in range(8):
        at = pl.multiple_of(member_at(NEAR_FIRST[k]) * 112, 112)
        if k < 7:
            outs[k][0:112, :] = total[pl.ds(at, 112), :]
            tail, row = outs[k], 112
        else:
            outs[7][...] = total[pl.ds(at, 80), :]
            outs[8][0:32, :] = total[pl.ds(at + 80, 32), :]
            tail, row = outs[8], 32
        at = pl.multiple_of(member_at(NEAR_FIRST[k]) * 144, 144)
        for q in range(3):
            tail[row : row + 48, 288 * q : 288 * q + 288] = below[pl.ds(at + 48 * q, 48), :]
        tail[row : row + 48, 864:1152] = jnp.zeros((48, 288), BF16)


def d_hidden_a_body(d_slots, t0, t1, t2, t3, sums_b, d_gate_b, *refs):
    chunks = refs[:9]
    keep, send = refs[9:11]
    shares = refs[11:15]
    full, total, flat, d_mod, held = refs[15:]
    load_chunks(chunks, FIRST_PLACES, full, 0, 112)
    total[...] = dot_nn(d_slots[...], full[...])
    split_halves(total, keep, send)
    d_shift = jnp.zeros((1, 1152), F32)
    d_scale = jnp.zeros((1, 1152), F32)
    for f in range(2):
        for i, block in enumerate((t0, t1, t2, t3)):
            row = 256 * f + 64 * i
            norm, _ = norm_rows(block[f].astype(F32))
            part = total[row : row + 64, :]
            d_shift = d_shift + jnp.sum(part, axis=0, keepdims=True)
            d_scale = d_scale + jnp.sum(part * norm, axis=0, keepdims=True)
    d_mod[0:1, :] = d_shift
    d_mod[1:2, :] = d_scale
    d_mod[2:5, :] = sums_b[0:3, :]
    d_mod[5:6, :] = d_gate_b[...]
    for m in range(24):
        d, j = divmod(m, 3)
        flat[d : d + 1, 288 * j : 288 * j + 288] = d_mod[m // 4 : m // 4 + 1, 288 * (m % 4) : 288 * (m % 4) + 288]
    blk = lax.axis_index("blk")
    for t in range(4):
        held[t] = flat[:, 216 * t : 216 * t + 216]
    for r in range(4):
        shares[r][...] = held[blk ^ r]


def mod_parts_body(s0, s1, s2, s3, *refs):
    outs, total = refs[:8], refs[8]
    total[...] = s0[...] + s1[...] + s2[...] + s3[...]
    mine = lax.broadcasted_iota(jnp.int32, (8, 216), 0) == lax.axis_index("dp")
    for k, out in enumerate(outs):
        row = total[pl.ds(member_at(NEAR_FIRST[k]), 1), :]
        out[...] = jnp.zeros((8, 1152), BF16)
        out[:, 0:216] = jnp.where(mine, row, 0.0).astype(BF16)


def own_half_body(keep, near, own, cross):
    for f in range(2):
        for i, block in enumerate((own, cross)):
            rows = slice(128 * f + 64 * i, 128 * f + 64 * i + 64)
            part = keep[rows, :] + near[rows, :].astype(F32)
            block[64 * f : 64 * f + 64, :] = part.astype(block.dtype)


def output_body(own, far, middle, mod, output):
    for f in range(2):
        rows = slice(64 * f, 64 * f + 64)
        output[f] = middle[rows, :] + mod[5:6, :] * (own[rows, :] + far[rows, :].astype(F32))


def grad_tokens_body(own, far, t0, d_mid, mod, grad):
    for f in range(2):
        rows = slice(64 * f, 64 * f + 64)
        norm, inv = norm_rows(t0[f].astype(F32))
        d_hidden = own[rows, :] + far[rows, :].astype(F32)
        grad[f] = d_mid[rows, :] + norm_back(d_hidden * (1.0 + mod[1:2, :]), norm, inv)


def cut_updown_body(u0, u1, u2, d0, d1, d2, *refs):
    pieces, held = refs[:4], refs[4]
    blk = lax.axis_index("blk")
    up = u0[...].astype(F32) + u1[0:144, :].astype(F32) + u2[0:144, :].astype(F32)
    down = d0[...].astype(F32) + d1[144:288, :].astype(F32) + d2[144:288, :].astype(F32)
    for t in range(4):
        held[t, :, 0:288] = up[:, 288 * t : 288 * t + 288].astype(BF16)
        held[t, :, 288:576] = down[:, 288 * t : 288 * t + 288].astype(BF16)
        held[t, :, 576:640] = jnp.zeros((144, 64), BF16)
    for r in range(4):
        pieces[r][...] = held[blk ^ r]


def final_updown_body(p0, p1, p2, p3, up, down, held):
    blk = lax.axis_index("blk")
    for r, piece in enumerate((p0, p1, p2, p3)):
        held[blk ^ r] = piece[...]
    for s in range(4):
        up[:, 144 * s : 144 * s + 144] = held[s, :, 0:288].astype(F32).T
        for part in range(2):
            at = 576 * part + 144 * s
            down[:, at : at + 144] = held[s, :, 288 + 144 * part : 432 + 144 * part].astype(F32)


def cut_heads_body(s0, s1, s2, *refs):
    pieces, held = refs[:4], refs[4]
    blk = lax.axis_index("blk")
    total = s0[...].astype(F32) + s1[0:160, :].astype(F32) + s2[0:160, :].astype(F32)
    for t in range(4):
        held[t, :, 0:288] = jnp.zeros((144, 288), BF16)
        held[t, 0:108, 0:288] = total[0:108, 288 * t : 288 * t + 288].astype(BF16)
        for q in range(3):
            at = 288 * q + 72 * t
            held[t, 48 * q : 48 * q + 48, 288:360] = total[112:160, at : at + 72].astype(BF16)
        held[t, :, 360:384] = jnp.zeros((144, 24), BF16)
    for r in range(4):
        pieces[r][...] = held[blk ^ r]


def final_heads_body(p0, p1, p2, p3, qkv, out, held, placed):
    blk = lax.axis_index("blk")
    for r, piece in enumerate((p0, p1, p2, p3)):
        sender = blk ^ r
        alone, shared = columns_of(sender)
        placed[0, alone] = piece[0:36, 0:288].astype(F32)
        placed[1, alone] = piece[36:72, 0:288].astype(F32)
        placed[sender & 1, shared] = piece[72:108, 0:288].astype(F32)
        held[kind_of(sender)] = piece[:, 288:360].astype(F32)
    for i in range(6):
        for half in range(2):
            at = 72 * i + 36 * half
            qkv[:, at : at + 36] = placed[half, i].T
    for s in range(4):
        out[:, 72 * s : 72 * s + 72] = held[s]


def vmem(shape, kind=BF16):
    return (shape, kind)


def local_kernels(tokens, timestep, mod_table, w_qkv, w_out, w_up, w_down, cotangent):
    nd, nb = 8, 4
    ring = Ring(nd, lax.axis_index("dp"))
    group = Group(nb, lax.axis_index("blk"))
    width = tokens.shape[3]
    own_tokens = tokens[0]
    own_cot = cotangent[0]
    full_low = ((512, 1152), BF16)
    chunk_low = ((144, 1152), BF16)
    part_low = [chunk_low] * 7 + [((80, 1152), BF16), ((64, 1152), BF16)]
    half_low = ((256, 1152), BF16)
    half_wide = ((256, 1152), F32)
    own_wide = ((128, 1152), F32)

    def send_out(pieces):
        return [pieces[0]] + [group.swap(pieces[r], r) for r in (1, 2, 3)]

    def add_low(keep, near):
        return (keep + near.astype(F32)).astype(BF16)

    def own_half(keep, near, name):
        return run_kernel(own_half_body, [own_wide, ((128, 1152), BF16)], keep, near, name=name)

    picker = (timestep[:, None] == jnp.arange(mod_table.shape[0], dtype=jnp.int32)[None, :]).astype(BF16)
    table_cols = dot_nn(picker, mod_table).astype(BF16)
    heads_cut = run_kernel(
        pack_heads_body,
        [((144, 384), BF16)] * 4,
        w_qkv, w_out.T, table_cols,
        scratch=[vmem((2, 6, 36, 288)), vmem((4, 144, 72))],
        name="pack_heads",
    )
    heads_got = send_out(heads_cut)
    (first_own,) = run_kernel(
        join_heads_body,
        [((160, 1152), BF16)],
        *heads_got,
        scratch=[vmem((4, 144, 384)), vmem((8, 864), F32)],
        name="join_heads",
    )
    updown_cut = run_kernel(
        pack_updown_body,
        [((144, 640), BF16)] * 4,
        *after((w_up, w_down.T), heads_got[1]),
        scratch=[vmem((4, 144, 288)), vmem((4, 144, 288))],
        name="pack_updown",
    )
    updown_got = send_out(updown_cut)
    fore1, rear1, _ = step(ring, first_own, first_own)
    fore2, rear2, held = step(ring, fore1, rear1, own_tokens, *updown_got)
    far_t = group.swap(held[0], 2)
    up_own, down_own = run_kernel(
        join_updown_body, [chunk_low] * 2, *held[1:], scratch=[vmem((4, 144, 640))], name="join_updown"
    )
    fore3, rear3, held = step(ring, fore2, rear2, up_own, down_own, far_t, own_tokens, own_cot)
    up_own, down_own, far_t, own_t, own_c = held
    token_blocks = [own_tokens, far_t, group.swap(own_t, 1), group.swap(far_t, 1)]
    far_c = group.swap(own_c, 2)
    fore4, rear4, held = step(
        ring, stack(fore3[:80], up_own), stack(rear3[80:], up_own), far_c, own_cot, *token_blocks
    )
    far_c, own_c, *token_blocks = held
    cot_blocks = [own_cot, far_c, group.swap(own_c, 1), group.swap(far_c, 1)]
    first_got = [first_own, fore1, rear1, fore2, rear2, fore3, rear3, fore4, rear4]
    fore5, rear5, held = step(
        ring, stack(fore4[80:], down_own), stack(rear4[80:], down_own), *cot_blocks, *token_blocks, *first_got
    )
    cot_blocks, token_blocks, first_got = held[:4], held[4:8], held[8:]
    other_halves = stack(*(chunk[72:112] for chunk in first_got[:7]), first_got[7][72:80], first_got[8][:32])
    hidden_a, parts, probs, attended, low, out_full, mod, keep_a, send_a = run_kernel(
        attend_body,
        [
            full_low,
            ((12, 512, 72), BF16),
            ((8, 256, 256), F32),
            ((4, 512, 72), F32),
            ((512, 288), BF16),
            ((1152, 288), BF16),
            ((8, 1152), F32),
            half_wide,
            half_low,
        ],
        *token_blocks, group.swap(other_halves, 1), *first_got,
        scratch=[vmem((1280, 1152)), vmem((512, 1280)), vmem((384, 1152))],
        flops=4 * 10**9,
        name="attend",
    )
    fore6, rear6, (keep_a, send_a) = step(ring, fore5, rear5, keep_a, send_a)
    near_a = group.swap(send_a, 1)
    far_a = group.swap(add_low(keep_a, near_a), 2)
    fore7, rear7, (keep_a, near_a, far_a) = step(
        ring, stack(fore6[:80], fore6[144:]), rear6[80:], keep_a, near_a, far_a
    )
    hidden_mine, normed_b, root_b, branch_a, middle = run_kernel(
        middle_body,
        [half_low, half_wide, ((256, 128), F32), own_wide, own_wide],
        keep_a, near_a, far_a, *token_blocks[:2], mod,
        name="middle",
    )
    hidden_theirs = group.swap(hidden_mine, 1)
    fore8, rear8, (hidden_mine, hidden_theirs) = step(ring, fore7[80:160], rear7[144:], hidden_mine, hidden_theirs)
    up_got = [up_own, down_own, fore4, rear4, fore5, rear5, fore6, rear6, fore7, rear7]
    down_got = [*up_got, fore8, rear8]
    hidden_b, act, slope, d_branch_b, *grad_down = run_kernel(
        up_body,
        [full_low, full_low, ((512, 1152), F32), full_low] + part_low,
        hidden_mine, hidden_theirs, *cot_blocks, mod, *up_got,
        scratch=[vmem((1152, 1152)), vmem((1152, 1152))],
        flops=4 * 10**9,
        name="up",
    )
    fore1, rear1, held = step(ring, *grad_down[7:], d_branch_b, slope, *down_got)
    d_branch_b, slope, down_got = held[0], held[1], held[2:]
    d_pre, keep_d, send_d = run_kernel(
        down_body,
        [full_low, half_wide, half_low],
        d_branch_b, slope, *down_got,
        scratch=[vmem((1152, 1152)), vmem((1152, 1152))],
        flops=4 * 10**9,
        name="down",
    )
    near_d = group.swap(send_d, 1)
    low_d = add_low(keep_d, near_d)
    grad_up = run_kernel(
        grad_body,
        part_low,
        d_pre, hidden_b,
        scratch=[vmem((1152, 1152))],
        flops=2 * 10**9,
        name="grad_up",
    )
    fore2, rear2, (keep_d, near_d, low_d, act) = step(
        ring,
        stack(grad_up[7], sum_low(grad_down[6][:80], fore1), grad_down[6][80:]),
        stack(grad_up[8], grad_down[5][:80], sum_low(grad_down[5][80:], rear1)),
        keep_d, near_d, low_d, act,
    )
    far_d = group.swap(low_d, 2)
    keep_b, send_b, d_gate_b = run_kernel(
        branch_b_body,
        [half_wide, half_low, ((1, 1152), F32)],
        act, *cot_blocks, *down_got,
        scratch=[vmem((1152, 1152)), vmem((512, 1152), F32)],
        flops=2 * 10**9,
        name="branch_b",
    )
    near_b = group.swap(send_b, 1)
    fore3, rear3, (keep_d, near_d, far_d, keep_b, near_b) = step(
        ring,
        stack(sum_low(grad_up[6][:80], fore2[:80]), grad_up[6][80:], sum_low(grad_down[4], fore2[80:])),
        stack(grad_up[5][:80], sum_low(grad_up[5][80:], rear2[:64]), sum_low(grad_down[3], rear2[64:])),
        keep_d, near_d, far_d, keep_b, near_b,
    )
    d_low, d_mid, sums_b = run_kernel(
        d_middle_body,
        [half_low, own_wide, ((3, 1152), F32)],
        keep_d, near_d, far_d, normed_b, root_b, *cot_blocks[:2], branch_a, mod,
        name="d_middle",
    )
    d_branch_a, d_mine, d_others = run_kernel(
        d_attend_body,
        [full_low, ((512, 896), BF16), ((512, 144), BF16)],
        d_low, group.swap(d_low, 1), parts, probs, attended, out_full,
        scratch=[vmem((512, 288))],
        flops=3 * 10**9,
        name="d_attend",
    )
    d_others = group.swap(d_others, 1)
    fore4, rear4, held = step(
        ring,
        stack(sum_low(grad_up[4], fore3[:144]), sum_low(grad_down[2], fore3[144:])),
        stack(sum_low(grad_up[3], rear3[:144]), sum_low(grad_down[1], rear3[144:])),
        keep_b, near_b, d_mine, d_others, d_branch_a,
    )
    keep_b, near_b, d_mine, d_others, d_branch_a = held
    own_b, cross_b = own_half(keep_b, near_b, "own_b")
    far_b = group.swap(cross_b, 2)
    *grad_first, d_slots = run_kernel(
        grad_first_body,
        [((160, 1152), BF16)] * 7 + [((80, 1152), BF16)] * 2 + [((512, 896), BF16)],
        d_mine, d_others, hidden_a, d_branch_a, low,
        scratch=[vmem((896, 1152)), vmem((1152, 288))],
        flops=2 * 10**9,
        name="grad_first",
    )
    fore5, rear5, (d_slots, own_b, far_b) = step(
        ring,
        stack(sum_low(grad_up[2], fore4[:144]), grad_first[7]),
        stack(sum_low(grad_up[1], rear4[:144]), grad_first[8]),
        d_slots, own_b, far_b,
    )
    keep_h, send_h, *d_mod = run_kernel(
        d_hidden_a_body,
        [half_wide, half_low] + [((8, 216), F32)] * 4,
        d_slots, *token_blocks, sums_b, d_gate_b, *first_got,
        scratch=[
            vmem((896, 1152)),
            vmem((512, 1152), F32),
            vmem((8, 864), F32),
            vmem((6, 1152), F32),
            vmem((4, 8, 216), F32),
        ],
        flops=2 * 10**9,
        name="d_hidden_a",
    )
    mods = run_kernel(
        mod_parts_body,
        [((8, 1152), BF16)] * 8,
        *send_out(d_mod),
        scratch=[vmem((8, 216), F32)],
        spare=1,
        name="mod_parts",
    )
    near_h = group.swap(send_h, 1)
    fore6, rear6, held = step(
        ring,
        stack(sum_low(grad_first[6][:80], fore5[144:]), grad_first[6][80:], mods[7]),
        stack(grad_first[5][:80], sum_low(grad_first[5][80:], rear5[144:])),
        keep_h, near_h, fore4, rear4, fore5, rear5,
    )
    keep_h, near_h, *up_down = held
    own_h, cross_h = own_half(keep_h, near_h, "own_h")
    far_h = group.swap(cross_h, 2)
    updown_cut = run_kernel(
        cut_updown_body,
        [((144, 640), BF16)] * 4,
        grad_up[0], *up_down[2:], grad_down[0], *up_down[:2],
        scratch=[vmem((4, 144, 640))],
        name="cut_updown",
    )
    fore7, rear7, held = step(
        ring,
        stack(sum_low(grad_first[4], fore6[:160]), sum_low(mods[6], fore6[160:])),
        stack(sum_low(grad_first[3], rear6), mods[5]),
        own_h, far_h, own_b, far_b, *updown_cut,
    )
    own_h, far_h, own_b, far_b, *updown_cut = held
    updown_back = send_out(updown_cut)
    (output,) = run_kernel(
        output_body, [((2, 64, 1152), F32)], own_b, far_b, middle, mod, name="output"
    )
    (grad_tokens,) = run_kernel(
        grad_tokens_body, [((2, 64, 1152), F32)], own_h, far_h, own_tokens, d_mid, mod, name="grad_tokens"
    )
    fore8, rear8, (output, grad_tokens, *updown_back) = step(
        ring,
        stack(sum_low(grad_first[2], fore7[:160]), sum_low(mods[4], fore7[160:])),
        stack(sum_low(grad_first[1], rear7[:160]), sum_low(mods[3], rear7[160:])),
        output, grad_tokens, *updown_back,
    )
    final_up, final_down = run_kernel(
        final_updown_body,
        [((288, 576), F32), ((144, 1152), F32)],
        *updown_back,
        scratch=[vmem((4, 144, 640))],
        name="final_updown",
    )
    fore9, rear9, (final_up, final_down) = step(
        ring, sum_low(mods[2], fore8[160:]), sum_low(mods[1], rear8[160:]), final_up, final_down
    )
    mod_sums = (mods[0].astype(F32) + fore9.astype(F32) + rear9.astype(F32))[:, :216]
    grad_table = lax.dot_general(
        picker.astype(F32),
        mod_sums,
        (((0,), (0,)), ((), ())),
        precision=HIGHEST,
        preferred_element_type=F32,
    )
    heads_cut = run_kernel(
        cut_heads_body, [((144, 384), BF16)] * 4, grad_first[0], fore8, rear8, scratch=[vmem((4, 144, 384))], name="cut_heads"
    )
    final_qkv, final_out = run_kernel(
        final_heads_body,
        [((288, 432), F32), ((144, 288), F32)],
        *send_out(heads_cut),
        scratch=[vmem((4, 144, 72), F32), vmem((2, 6, 36, 288), F32)],
        name="final_heads",
    )
    return (output[None], grad_tokens[None], grad_table, final_qkv, final_out.T, final_up, final_down.T)


def local(tokens, timestep, mod_table, w_qkv, w_out, w_up, w_down, cotangent):
    sizes = (lax.axis_size("dp"), lax.axis_size("blk"), tokens.shape, w_qkv.shape, w_up.shape, w_down.shape)
    known = (8, 4, (1, 2, 64, 1152), (288, 432), (288, 576), (1152, 144))
    chosen = local_kernels if sizes == known else local_plain
    return chosen(tokens, timestep, mod_table, w_qkv, w_out, w_up, w_down, cotangent)


def solution(mesh):
    in_specs = (
        P("dp", None, "blk", None),
        P(),
        P(None, ("dp", "blk")),
        P("blk", "dp"),
        P("blk", "dp"),
        P("blk", "dp"),
        P("blk", "dp"),
        P("dp", None, "blk", None),
    )
    out_specs = (
        P("dp", None, "blk", None),
        P("dp", None, "blk", None),
        P(None, ("dp", "blk")),
        P("blk", "dp"),
        P("blk", "dp"),
        P("blk", "dp"),
        P("blk", "dp"),
    )
    return jax.shard_map(local, mesh=mesh, in_specs=in_specs, out_specs=out_specs, check_vma=False)
```

```python
import math
from functools import partial

import jax
import jax.numpy as jnp
from jax import lax
from jax.experimental import pallas as pl
from jax.experimental.pallas import tpu as pltpu
from jax.sharding import PartitionSpec as P

HEADS = 16
HEAD_DIM = 72
EPS = 1e-06
HIGHEST = lax.Precision.HIGHEST
BF16 = jnp.bfloat16
F32 = jnp.float32


def norm_rows(values):
    center = values - jnp.mean(values, axis=-1, keepdims=True)
    spread = jnp.mean(center * center, axis=-1, keepdims=True)
    root_inv = lax.rsqrt(spread + EPS)
    return (center * root_inv, root_inv)


def norm_back(d_normed, normed, root_inv):
    mean_one = jnp.mean(d_normed, axis=-1, keepdims=True)
    mean_two = jnp.mean(d_normed * normed, axis=-1, keepdims=True)
    return root_inv * (d_normed - mean_one - normed * mean_two)


def dot_nn(left, right):
    return jnp.dot(left, right, preferred_element_type=F32)


def dot_tn(left, right):
    return lax.dot_general(left, right, (((0,), (0,)), ((), ())), preferred_element_type=F32)


def dot_nt(left, right):
    return lax.dot_general(left, right, (((1,), (1,)), ((), ())), preferred_element_type=F32)


class Ring:
    def __init__(self, size, index):
        self.size = size
        self.order = list(range(0, size, 2)) + list(range(size - 1, 0, -2))
        place = [0] * size
        for spot, member in enumerate(self.order):
            place[member] = spot
        self.spot = jnp.array(place, jnp.int32)[index]
        self.table = jnp.array(self.order, jnp.int32)
        self.ahead = [(self.order[i], self.order[(i + 1) % size]) for i in range(size)]
        self.back = [(right, left) for left, right in self.ahead]

    def member(self, offset):
        return self.table[(self.spot + offset) % self.size]

    def gather(self, chunk):
        half = self.size // 2
        cut = chunk.shape[0] // 2
        out = jnp.zeros((self.size,) + chunk.shape, chunk.dtype)

        def put(out, piece, offset, row=0):
            return lax.dynamic_update_slice(out, piece[None], (self.member(offset), row, 0))

        out = put(out, chunk, 0)
        fore = rear = chunk
        for step in range(1, half):
            fore = lax.ppermute(fore, "dp", self.ahead)
            rear = lax.ppermute(rear, "dp", self.back)
            out = put(put(out, fore, -step), rear, step)
        fore = lax.ppermute(fore[:cut], "dp", self.ahead)
        rear = lax.ppermute(rear[cut:], "dp", self.back)
        return put(put(out, fore, half), rear, half, cut)

    def scatter(self, parts):
        half = self.size // 2
        cut = parts.shape[1] // 2

        def own(offset):
            return lax.dynamic_index_in_dim(parts, self.member(offset), 0, keepdims=False)

        far = own(half)
        fore = lax.ppermute(far[:cut], "dp", self.ahead)
        rear = lax.ppermute(far[cut:], "dp", self.back)
        for step in range(half - 1, 0, -1):
            mine_fore = own(step).astype(F32)
            mine_rear = own(-step).astype(F32)
            if step == half - 1:
                fore = jnp.concatenate([mine_fore[:cut] + fore.astype(F32), mine_fore[cut:]], axis=0)
                rear = jnp.concatenate([mine_rear[:cut], mine_rear[cut:] + rear.astype(F32)], axis=0)
            else:
                fore = mine_fore + fore.astype(F32)
                rear = mine_rear + rear.astype(F32)
            fore = lax.ppermute(fore.astype(BF16), "dp", self.ahead)
            rear = lax.ppermute(rear.astype(BF16), "dp", self.back)
        return own(0).astype(F32) + fore.astype(F32) + rear.astype(F32)


class Group:
    def __init__(self, size, index):
        self.size = size
        self.index = index
        self.bits = []
        bit = size // 2
        while bit:
            self.bits.append(bit)
            bit //= 2

    def swap(self, values, bit):
        return lax.ppermute(values, "blk", [(i, i ^ bit) for i in range(self.size)])

    def exchange(self, pieces):
        if self.size > 4:
            return lax.all_to_all(pieces, "blk", 0, 0, tiled=True)
        got = []
        for r in range(self.size):
            piece = lax.dynamic_index_in_dim(pieces, self.index ^ r, 0, keepdims=False)
            got.append(self.swap(piece, r) if r else piece)
        bit = 1
        while bit < self.size:
            odd = (self.index & bit) != 0
            got = [jnp.where(odd, got[r ^ bit], got[r]) for r in range(self.size)]
            bit *= 2
        return jnp.stack(got)

    def gather(self, block, bits=None):
        for bit in self.bits if bits is None else bits:
            block = jnp.concatenate([block, self.swap(block, bit)], axis=0)
        return block

    def scatter(self, parts, share):
        for bit in reversed(self.bits[1:]):
            half = parts.shape[0] // 2
            parts = parts[:half] + self.swap(parts[half:].astype(BF16), bit).astype(F32)
        top = self.bits[0]
        if share:
            return parts + self.swap(parts.astype(BF16), top)[::-1].astype(F32)
        return parts[:1] + self.swap(parts[1:].astype(BF16), top).astype(F32)


def local_plain(tokens, timestep, mod_table, w_qkv, w_out, w_up, w_down, cotangent):
    frames, patches, width = tokens.shape[1:]
    nd = lax.axis_size("dp")
    nb = lax.axis_size("blk")
    dp = lax.axis_index("dp")
    blk = lax.axis_index("blk")
    ring = Ring(nd, dp)
    group = Group(nb, blk)
    rows = nb * frames * patches
    scale = HEAD_DIM ** (-0.5)
    heads = HEADS // nb
    deep = width // nb
    ff = w_down.shape[0]
    hidden = w_up.shape[1]
    out_cols = w_out.shape[1]

    columns = w_qkv.shape[1] // HEAD_DIM
    slots = -(-columns // nb)
    offset = (columns * dp) % nb
    qkv_t = w_qkv.T.reshape(columns, HEAD_DIM, deep)
    qkv_pos = jnp.zeros((2 * slots * nb, HEAD_DIM, deep), BF16)
    qkv_pos = lax.dynamic_update_slice(qkv_pos, qkv_t, (offset, 0, 0))
    qkv_pos = qkv_pos[: slots * nb] + qkv_pos[slots * nb :]
    qkv_send = qkv_pos.reshape(slots, nb, HEAD_DIM, deep).transpose(1, 0, 2, 3)
    qkv_send = qkv_send.reshape(nb, slots * HEAD_DIM, deep)
    spread = heads // nb
    if spread:
        out_send = w_out.T.reshape(out_cols, spread, nb, HEAD_DIM).transpose(2, 0, 1, 3)
        out_send = out_send.reshape(nb, out_cols, spread * HEAD_DIM)
    up_send = w_up.T.reshape(nb, hidden // nb, deep)
    many = ff // hidden
    down_send = w_down.T.reshape(out_cols, many, nb, hidden // nb).transpose(2, 0, 1, 3)
    down_send = down_send.reshape(nb, out_cols, many * hidden // nb)
    first = group.exchange(jnp.concatenate([qkv_send, out_send], axis=2) if spread else qkv_send)
    up_got = group.exchange(up_send)
    down_got = group.exchange(down_send)
    qkv_own = first[:, :, :deep].transpose(1, 0, 2).reshape(slots * HEAD_DIM, width)
    out_own = first[:, :, deep:].transpose(1, 0, 2).reshape(out_cols, heads * HEAD_DIM) if spread else w_out.T
    up_own = up_got.transpose(1, 0, 2).reshape(hidden // nb, width)
    down_own = down_got.transpose(1, 0, 2).reshape(out_cols, nd * hidden // nb)

    token_all = group.gather(tokens)
    cot_all = group.gather(cotangent)

    picker = (timestep[:, None] == jnp.arange(mod_table.shape[0], dtype=jnp.int32)[None, :]).astype(BF16)
    table_cols = dot_nn(picker, mod_table).astype(BF16)
    piece = table_cols.shape[1]
    mods_send = jnp.broadcast_to(table_cols[:, None, :], (nd, nb, piece)).reshape(nd * nb, piece)
    mod_row = lax.all_to_all(mods_send, ("dp", "blk"), 0, 0, tiled=True).reshape(6, width).astype(F32)
    shift_a, scale_a, gate_a, shift_b, scale_b, gate_b = (mod_row[i] for i in range(6))

    first_all = ring.gather(jnp.concatenate([qkv_own, out_own], axis=1))
    up_full = ring.gather(up_own).reshape(ff, width)
    down_full = ring.gather(down_own).reshape(width, ff)
    out_full = first_all[:, :, width:].reshape(width, heads * HEAD_DIM)
    wanted = blk + nb * jnp.arange(3 * heads, dtype=jnp.int32)
    holder = wanted // columns
    place = ((wanted - columns * holder + (columns * holder) % nb) % (slots * nb)) // nb
    slot_of = holder * slots + place
    qkv_slots = first_all[:, :, :width].reshape(nd * slots, HEAD_DIM, width)
    qkv_full = jnp.take(qkv_slots, slot_of, axis=0).reshape(3 * heads * HEAD_DIM, width)

    inputs = token_all.reshape(rows, width).astype(F32)
    normed_a, root_a = norm_rows(inputs)
    hidden_a = (normed_a * (1.0 + scale_a) + shift_a).astype(BF16)
    projected = dot_nt(hidden_a, qkv_full).astype(BF16)

    def by_head(values, parts):
        split = values.reshape(nb, frames, patches, parts, heads, HEAD_DIM)
        split = split.transpose(3, 1, 4, 0, 2, 5)
        return split.reshape(parts, frames, heads, nb * patches, HEAD_DIM)

    def by_row(values):
        split = values.reshape(-1, frames, heads, nb, patches, HEAD_DIM)
        return split.transpose(3, 1, 4, 0, 2, 5).reshape(rows, -1)

    query, keys, values = by_head(projected, 3)
    scores = jnp.einsum("fhqe,fhke->fhqk", query, keys, preferred_element_type=F32) * scale
    top = jnp.max(scores, axis=-1, keepdims=True)
    weights = jnp.exp(scores - top)
    probs = weights / jnp.sum(weights, axis=-1, keepdims=True)
    probs_low = probs.astype(BF16)
    attended = jnp.einsum("fhqk,fhke->fhqe", probs_low, values, preferred_element_type=F32)
    attn_low = by_row(attended).astype(BF16)
    share = 2 * frames * patches
    own = frames * patches

    def blocks(partial_sum):
        return partial_sum.reshape(nb, own, width)

    branch_a = group.scatter(blocks(dot_nt(attn_low, out_full)), True).reshape(share, width)
    middle = inputs[:share] + gate_a * branch_a
    normed_b, root_b = norm_rows(middle)
    hidden_low = (normed_b * (1.0 + scale_b) + shift_b).astype(BF16)
    hidden_b = group.gather(hidden_low.reshape(2, own, width), group.bits[1:]).reshape(rows, width)
    pre_act = dot_nt(hidden_b, up_full)
    activated, gelu_back = jax.vjp(partial(jax.nn.gelu, approximate=True), pre_act)
    act_low = activated.astype(BF16)
    grad_in = cot_all.reshape(rows, width).astype(F32)
    d_branch_b = (gate_b * grad_in).astype(BF16)
    grad_down = dot_tn(d_branch_b, act_low).astype(BF16)
    down_sum = ring.scatter(grad_down.reshape(nd, out_cols, ff))
    d_act = dot_nn(d_branch_b, down_full)
    d_pre = gelu_back(d_act)[0].astype(BF16)
    grad_up = dot_tn(d_pre, hidden_b).astype(BF16)
    up_sum = ring.scatter(grad_up.reshape(nd, hidden // nb, width))
    d_hidden_b = group.scatter(blocks(dot_nn(d_pre, up_full)), True).reshape(share, width)
    branch_b = group.scatter(blocks(dot_nt(act_low, down_full)), False).reshape(own, width)
    output = (middle[:own] + gate_b * branch_b).reshape(tokens.shape)
    d_gate_b = jnp.sum(grad_in[:own] * branch_b, axis=0)
    d_shift_b = jnp.sum(d_hidden_b[:own], axis=0)
    d_scale_b = jnp.sum(d_hidden_b[:own] * normed_b[:own], axis=0)
    d_middle = grad_in[:share] + norm_back(d_hidden_b * (1.0 + scale_b), normed_b, root_b)
    d_gate_a = jnp.sum(d_middle[:own] * branch_a[:own], axis=0)
    d_branch_a = (gate_a * d_middle).astype(BF16).reshape(2, own, width)
    d_branch_a = group.gather(d_branch_a, group.bits[1:]).reshape(rows, width)
    grad_out = dot_tn(d_branch_a, attn_low).astype(BF16)
    d_attended = dot_nn(d_branch_a, out_full).astype(BF16)
    d_att = by_head(d_attended, 1)[0]
    delta = jnp.sum(d_att.astype(F32) * attended, axis=-1, keepdims=True)
    d_probs = jnp.einsum("fhqe,fhke->fhqk", d_att, values, preferred_element_type=F32)
    d_scores = (probs * (d_probs - delta)).astype(BF16)
    d_query = jnp.einsum("fhqk,fhke->fhqe", d_scores, keys, preferred_element_type=F32) * scale
    d_key = jnp.einsum("fhqk,fhqe->fhke", d_scores, query, preferred_element_type=F32) * scale
    d_value = jnp.einsum("fhqk,fhqe->fhke", probs_low, d_att, preferred_element_type=F32)
    d_projected = by_row(jnp.stack([d_query, d_key, d_value]).astype(BF16))
    grad_qkv = dot_tn(d_projected, hidden_a).astype(BF16).reshape(3 * heads, HEAD_DIM, width)
    grad_slots = jnp.zeros((nd * slots, HEAD_DIM, width), BF16).at[slot_of].set(grad_qkv)
    grad_first = jnp.concatenate(
        [
            grad_slots.reshape(nd, slots * HEAD_DIM, width),
            grad_out.reshape(nd, out_cols, heads * HEAD_DIM),
        ],
        axis=2,
    )
    first_sum = ring.scatter(grad_first)
    d_hidden_a = group.scatter(blocks(dot_nn(d_projected, qkv_full)), False).reshape(own, width)
    d_shift_a = jnp.sum(d_hidden_a, axis=0)
    d_scale_a = jnp.sum(d_hidden_a * normed_a[:own], axis=0)
    d_normed = norm_back(d_hidden_a * (1.0 + scale_a), normed_a[:own], root_a[:own])
    grad_tokens = (d_middle[:own] + d_normed).reshape(tokens.shape)

    d_mod = jnp.concatenate([d_shift_a, d_scale_a, d_gate_a, d_shift_b, d_scale_b, d_gate_b])
    mod_got = lax.all_to_all(d_mod.reshape(nd * nb, piece), ("dp", "blk"), 0, 0, tiled=True)
    mod_sums = jnp.sum(mod_got.reshape(nd, nb, piece), axis=1)
    grad_table = lax.dot_general(
        picker.astype(F32),
        mod_sums,
        (((0,), (0,)), ((), ())),
        precision=HIGHEST,
        preferred_element_type=F32,
    )

    up_back = group.exchange(up_sum.astype(BF16).reshape(hidden // nb, nb, deep).transpose(1, 0, 2))
    final_up = up_back.reshape(hidden, deep).T.astype(F32)
    down_back = down_sum.astype(BF16).reshape(out_cols, nb, many, hidden // nb).transpose(1, 0, 2, 3)
    down_back = group.exchange(down_back.reshape(nb, out_cols, many * hidden // nb))
    down_back = down_back.reshape(nb, out_cols, many, hidden // nb).transpose(2, 0, 3, 1)
    final_down = down_back.reshape(ff, out_cols).astype(F32)
    first_low = first_sum.astype(BF16)
    qkv_back = first_low[:, :width].reshape(slots * HEAD_DIM, nb, deep).transpose(1, 0, 2)
    out_back = first_low[:, width:]
    if spread:
        out_back = out_back.reshape(out_cols, nb, spread * HEAD_DIM).transpose(1, 0, 2)
        back = group.exchange(jnp.concatenate([qkv_back, out_back], axis=2))
        out_back = back[:, :, deep:].reshape(nb, out_cols, spread, HEAD_DIM).transpose(2, 0, 3, 1)
        final_out = out_back.reshape(deep, out_cols).astype(F32)
    else:
        back = group.exchange(qkv_back)
        final_out = out_back.T.astype(F32)
    qkv_back = back[:, :, :deep].reshape(nb, slots, HEAD_DIM, deep).transpose(1, 0, 2, 3)
    qkv_back = qkv_back.reshape(slots * nb, HEAD_DIM, deep)
    qkv_back = lax.dynamic_slice(
        jnp.concatenate([qkv_back, qkv_back], axis=0), (offset, 0, 0), (columns, HEAD_DIM, deep)
    )
    final_qkv = qkv_back.reshape(columns * HEAD_DIM, deep).T.astype(F32)
    return (output, grad_tokens, grad_table, final_qkv, final_out, final_up, final_down)


GELU_IN = 0.7978845608028654
GELU_CUBE = 0.044715


def padded_bytes(shape, kind):
    *lead, rows, lanes = shape
    return math.prod(lead) * -(-rows // 16) * 16 * -(-lanes // 128) * 128 * jnp.dtype(kind).itemsize


def run_kernel(body, outs, *args, scalars=0, scratch=(), spare=8, flops=0, name=None):
    held = list(outs) + list(scratch) + [(a.shape, a.dtype) for a in args[scalars:]]
    limit = sum(padded_bytes(*h) for h in held) + (spare << 20)
    moved = sum(padded_bytes(*o) for o in outs) + sum(padded_bytes(a.shape, a.dtype) for a in args[scalars:])
    return pl.pallas_call(
        body,
        out_shape=[jax.ShapeDtypeStruct(shape, t) for shape, t in outs],
        in_specs=[pl.BlockSpec(memory_space=pltpu.SMEM if i < scalars else pltpu.VMEM) for i in range(len(args))],
        out_specs=[pl.BlockSpec(memory_space=pltpu.VMEM) for _ in outs],
        scratch_shapes=[pltpu.VMEM(*h) for h in scratch],
        compiler_params=pltpu.CompilerParams(vmem_limit_bytes=limit),
        cost_estimate=pl.CostEstimate(flops=flops, bytes_accessed=moved, transcendentals=0),
        name=name,
    )(*args)


def after(value, *others):
    return lax.optimization_barrier((value, *others))[0]


def step(ring, fore, rear, *carry):
    (fore, rear), carry = lax.optimization_barrier(((fore, rear), carry))
    return lax.ppermute(fore, "dp", ring.ahead), lax.ppermute(rear, "dp", ring.back), carry


def sum_low(mine, got):
    return (mine.astype(F32) + got.astype(F32)).astype(BF16)


def stack(*blocks):
    return jnp.concatenate(blocks, axis=0)


NEAR_FIRST = (0, -1, 1, -2, 2, -3, 3, 4)


def member_at(offset):
    dp = lax.axis_index("dp")
    spot = jnp.where(dp % 2 == 0, dp // 2, 7 - dp // 2)
    at = (spot + offset + 8) % 8
    return jnp.where(at < 4, 2 * at, 15 - 2 * at)


def kind_of(device):
    return (device >> 1) | ((device & 1) << 1)


def columns_of(device):
    odd = lax.axis_index("dp") & 1
    return kind_of(device) + 2 * odd, (device >> 1) + 4 - 4 * odd


def turn(values):
    return values.astype(F32).T.astype(BF16)


def pack_heads_body(qkv, out, mods, *refs):
    heads, held_q, held_o = refs[:4], refs[4], refs[5]
    blk = lax.axis_index("blk")
    for i in range(6):
        for half in range(2):
            at = 72 * i + 36 * half
            held_q[half, i] = turn(qkv[:, at : at + 36])
    for t in range(4):
        held_o[t] = out[:, 72 * kind_of(t) : 72 * kind_of(t) + 72]
    for r in range(4):
        t = blk ^ r
        alone, shared = columns_of(t)
        heads[r][...] = jnp.zeros((144, 384), BF16)
        heads[r][0:36, 0:288] = held_q[0, alone]
        heads[r][36:72, 0:288] = held_q[1, alone]
        heads[r][72:108, 0:288] = held_q[t & 1, shared]
        heads[r][112:120, 0:216] = mods[...]
        heads[r][:, 288:360] = held_o[t]


def pack_updown_body(up, down, *refs):
    updown, held_u, held_d = refs[:4], refs[4], refs[5]
    blk = lax.axis_index("blk")
    for t in range(4):
        held_u[t] = turn(up[:, 144 * t : 144 * t + 144])
        for part in range(2):
            at = 576 * part + 144 * t
            held_d[t, :, 144 * part : 144 * part + 144] = down[:, at : at + 144]
    for r in range(4):
        t = blk ^ r
        updown[r][:, 0:288] = held_u[t]
        updown[r][:, 288:576] = held_d[t]
        updown[r][:, 576:640] = jnp.zeros((144, 64), BF16)


def join_heads_body(*refs):
    pieces, joined, held, row = refs[:4], refs[4], refs[5], refs[6]
    blk = lax.axis_index("blk")
    for r in range(4):
        held[blk ^ r] = pieces[r][...]
    joined[96:160, :] = jnp.zeros((64, 1152), BF16)
    for s in range(4):
        joined[0:108, 288 * s : 288 * s + 288] = held[s, 0:108, 0:288]
        for q in range(3):
            at = 288 * q + 72 * s
            joined[112:160, at : at + 72] = held[s, 48 * q : 48 * q + 48, 288:360]
        row[:, 216 * s : 216 * s + 216] = held[s, 112:120, 0:216].astype(F32)
    for j in range(3):
        joined[112 + 16 * j : 120 + 16 * j, 864:1152] = row[:, 288 * j : 288 * j + 288].astype(BF16)


def join_updown_body(*refs):
    pieces, up, down, held = refs[:4], refs[4], refs[5], refs[6]
    blk = lax.axis_index("blk")
    for r in range(4):
        held[blk ^ r] = pieces[r][...]
    for s in range(4):
        up[:, 288 * s : 288 * s + 288] = held[s, :, 0:288]
        down[:, 288 * s : 288 * s + 288] = held[s, :, 288:576]


FIRST_PLACES = (
    (0, 0, 0, 160, 0),
    (-1, 1, 0, 160, 0),
    (1, 2, 0, 160, 0),
    (-2, 3, 0, 160, 0),
    (2, 4, 0, 160, 0),
    (-3, 5, 0, 160, 0),
    (3, 6, 0, 160, 0),
    (4, 7, 0, 80, 0),
    (4, 8, 0, 80, 80),
)
UP_PLACES = (
    (0, 0, 0, 144, 0),
    (-1, 2, 80, 144, 0),
    (1, 3, 80, 144, 0),
    (-2, 4, 0, 144, 0),
    (2, 5, 0, 144, 0),
    (-3, 6, 0, 144, 0),
    (3, 7, 0, 144, 0),
    (4, 8, 0, 80, 0),
    (4, 9, 0, 64, 80),
)
DOWN_PLACES = (
    (0, 1, 0, 144, 0),
    (-1, 4, 144, 144, 0),
    (1, 5, 144, 144, 0),
    (-2, 6, 144, 144, 0),
    (2, 7, 144, 144, 0),
    (-3, 8, 80, 144, 0),
    (3, 9, 64, 144, 0),
    (4, 10, 0, 80, 0),
    (4, 11, 0, 64, 80),
)


def load_chunks(arrays, places, full, first=0, count=144, pitch=None):
    pitch = pitch or count
    for offset, index, start, rows, row in places:
        low, high = max(first, row), min(first + count, row + rows)
        if low < high:
            at = pl.multiple_of(member_at(offset) * pitch + low - first, 16)
            full[pl.ds(at, high - low), :] = arrays[index][start + low - row : start + high - row, :]


def split_halves(total, keep, send):
    for f in range(2):
        keep[128 * f : 128 * f + 128, :] = total[256 * f : 256 * f + 128, :]
        send[128 * f : 128 * f + 128, :] = total[256 * f + 128 : 256 * f + 256, :].astype(BF16)


def join_halves(mine, theirs, full):
    for f in range(2):
        full[256 * f : 256 * f + 128, :] = mine[128 * f : 128 * f + 128, :]
        full[256 * f + 128 : 256 * f + 256, :] = theirs[128 * f : 128 * f + 128, :]


def attend_body(t0, t1, t2, t3, halves, *refs):
    chunks = refs[:9]
    hidden, parts, probs, attended, low, out, mod, keep, send = refs[9:18]
    full, slots, tail = refs[18:]
    load_chunks(chunks, FIRST_PLACES, tail, 112, 48)
    load_chunks(chunks, FIRST_PLACES, full, 0, 112, 160)
    clip = lax.axis_index("dp")
    own = lax.broadcasted_iota(jnp.int32, (8, 288), 0) == clip
    for m in range(24):
        d, j = divmod(m, 3)
        rows = tail[48 * d + 16 * j : 48 * d + 16 * j + 8, 864:1152].astype(F32)
        row = jnp.sum(jnp.where(own, rows, 0.0), axis=0, keepdims=True)
        mod[m // 4 : m // 4 + 1, 288 * (m % 4) : 288 * (m % 4) + 288] = row
        out[48 * m : 48 * m + 48, :] = tail[48 * d : 48 * d + 48, 288 * j : 288 * j + 288]
    for i, block in enumerate((t0, t1, t2, t3)):
        for f in range(2):
            normed, _ = norm_rows(block[f].astype(F32))
            at = 256 * f + 64 * i
            hidden[at : at + 64, :] = (normed * (1.0 + mod[1:2, :]) + mod[0:1, :]).astype(BF16)
    for k, offset in enumerate(NEAR_FIRST):
        at = pl.multiple_of(member_at(offset) * 160 + 112, 16)
        full[pl.ds(at, 48), :] = jnp.concatenate([halves[40 * k : 40 * k + 40, :], jnp.zeros((8, 1152), BF16)], axis=0)
    slots[...] = dot_nt(hidden[...], full[...]).astype(BF16)
    first = lax.axis_index("blk") % 2 == 0
    for e in range(4):
        at = 320 * e
        parts[3 * e] = slots[:, at : at + 72]
        parts[3 * e + 2] = slots[:, at + 160 : at + 232]
        near = jnp.where(first, slots[:, at + 72 : at + 108], slots[:, at + 272 : at + 308])
        far = jnp.where(first, slots[:, at + 112 : at + 148], slots[:, at + 232 : at + 268])
        parts[3 * e + 1, :, 0:36] = near
        parts[3 * e + 1, :, 36:72] = far
    scale = HEAD_DIM ** (-0.5)
    for f in range(2):
        rows = slice(256 * f, 256 * f + 256)
        for h in range(4):
            scores = dot_nt(parts[h, rows, :], parts[4 + h, rows, :]) * scale
            weights = jnp.exp(scores - jnp.max(scores, axis=-1, keepdims=True))
            prob = weights / jnp.sum(weights, axis=-1, keepdims=True)
            probs[4 * f + h] = prob
            mixed = dot_nn(prob.astype(BF16), parts[8 + h, rows, :])
            attended[h, rows, :] = mixed
            low[rows, 72 * h : 72 * h + 72] = mixed.astype(BF16)
    split_halves(dot_nt(low[...], out[...]), keep, send)


def middle_body(keep, near, far, t0, t1, mod, hidden, normed, root, branch, middle):
    for f in range(2):
        for i, block in enumerate((t0, t1)):
            rows = slice(128 * f + 64 * i, 128 * f + 64 * i + 64)
            cross = slice(128 * f + 64 * (1 - i), 128 * f + 64 * (1 - i) + 64)
            part = keep[rows, :] + near[rows, :].astype(F32) + far[cross, :].astype(F32)
            mid = block[f].astype(F32) + mod[2:3, :] * part
            norm, inv = norm_rows(mid)
            hidden[rows, :] = (norm * (1.0 + mod[4:5, :]) + mod[3:4, :]).astype(BF16)
            normed[rows, :] = norm
            root[rows, :] = jnp.broadcast_to(inv, (64, 128))
            if i == 0:
                branch[64 * f : 64 * f + 64, :] = part
                middle[64 * f : 64 * f + 64, :] = mid


def write_parts(total, outs):
    cut = outs[7].shape[0]
    for k in range(8):
        at = pl.multiple_of(member_at(NEAR_FIRST[k]) * 144, 144)
        if k < 7:
            outs[k][...] = total[pl.ds(at, 144), :]
        else:
            outs[7][...] = total[pl.ds(at, cut), :]
            outs[8][...] = total[pl.ds(at + cut, 144 - cut), :]


def up_body(mine, theirs, g0, g1, g2, g3, mod, *refs):
    chunks = refs[:10]
    hidden, act, slope, d_branch = refs[10:14]
    parts = refs[14:23]
    up, total = refs[23:]
    load_chunks(chunks, UP_PLACES, up)
    join_halves(mine, theirs, hidden)
    for f in range(2):
        for i, block in enumerate((g0, g1, g2, g3)):
            row = 256 * f + 64 * i
            d_branch[row : row + 64, :] = (mod[5:6, :] * block[f].astype(F32)).astype(BF16)
    for at in range(0, 512, 256):
        rows = slice(at, at + 256)
        pre = dot_nt(hidden[rows, :], up[...])
        square = pre * pre
        bend = jnp.tanh(GELU_IN * (pre + GELU_CUBE * (square * pre)))
        half = 0.5 * (1.0 + bend)
        act[rows, :] = (pre * half).astype(BF16)
        inner = GELU_IN * (1.0 + (3.0 * GELU_CUBE) * square)
        slope[rows, :] = half + (0.5 * pre) * ((1.0 - bend * bend) * inner)
    total[...] = dot_tn(d_branch[...], act[...]).astype(BF16)
    write_parts(total, parts)


def down_body(d_branch, slope, *refs):
    chunks = refs[:12]
    d_pre, keep, send, down, up = refs[12:]
    load_chunks(chunks, DOWN_PLACES, down)
    load_chunks(chunks, UP_PLACES, up)
    d_pre[...] = (dot_nn(d_branch[...], down[...]) * slope[...]).astype(BF16)
    split_halves(dot_nn(d_pre[...], up[...]), keep, send)


def grad_body(left, right, *refs):
    parts, total = refs[:9], refs[9]
    total[...] = dot_tn(left[...], right[...]).astype(BF16)
    write_parts(total, parts)


def branch_b_body(act, g0, g1, g2, g3, *refs):
    chunks = refs[:12]
    keep, send, d_gate, full, total = refs[12:]
    load_chunks(chunks, DOWN_PLACES, full)
    total[...] = dot_nt(act[...], full[...])
    split_halves(total, keep, send)
    gate = jnp.zeros((1, 1152), F32)
    for f in range(2):
        for i, block in enumerate((g0, g1, g2, g3)):
            row = 256 * f + 64 * i
            gate = gate + jnp.sum(block[f].astype(F32) * total[row : row + 64, :], axis=0, keepdims=True)
    d_gate[...] = gate


def d_middle_body(keep, near, far, normed, root, g0, g1, branch, mod, d_low, d_mid, sums):
    d_shift = jnp.zeros((1, 1152), F32)
    d_scale = jnp.zeros((1, 1152), F32)
    d_gate = jnp.zeros((1, 1152), F32)
    for f in range(2):
        for i, block in enumerate((g0, g1)):
            rows = slice(128 * f + 64 * i, 128 * f + 64 * i + 64)
            cross = slice(128 * f + 64 * (1 - i), 128 * f + 64 * (1 - i) + 64)
            d_hidden = keep[rows, :] + near[rows, :].astype(F32) + far[cross, :].astype(F32)
            norm = normed[rows, :]
            back = norm_back(d_hidden * (1.0 + mod[4:5, :]), norm, root[rows, 0:1])
            mid = block[f].astype(F32) + back
            d_low[rows, :] = (mod[2:3, :] * mid).astype(BF16)
            if i == 0:
                own = slice(64 * f, 64 * f + 64)
                d_mid[own, :] = mid
                d_shift = d_shift + jnp.sum(d_hidden, axis=0, keepdims=True)
                d_scale = d_scale + jnp.sum(d_hidden * norm, axis=0, keepdims=True)
                d_gate = d_gate + jnp.sum(mid * branch[own, :], axis=0, keepdims=True)
    sums[0:1, :] = d_gate
    sums[1:2, :] = d_shift
    sums[2:3, :] = d_scale


def d_attend_body(mine, theirs, parts, probs, attended, out, d_branch, d_slots, d_others, d_att):
    join_halves(mine, theirs, d_branch)
    d_att[...] = dot_nn(d_branch[...], out[...]).astype(BF16)
    scale = HEAD_DIM ** (-0.5)

    first = lax.axis_index("blk") % 2 == 0
    d_slots[...] = jnp.zeros_like(d_slots)

    def place(rows, m, value):
        e, k = divmod(m, 3)
        low = value.astype(BF16)
        at = 224 * e
        if k == 0:
            d_slots[rows, at : at + 72] = low
        elif k == 2:
            d_slots[rows, at + 112 : at + 184] = low
        else:
            near = jnp.where(first, low[:, 0:36], low[:, 36:72])
            d_slots[rows, at + 72 : at + 108] = near
            d_slots[rows, at + 184 : at + 220] = near
            other = jnp.where(first, low[:, 36:72], low[:, 0:36])
            start = rows.start
            d_others[start : start + 128, 36 * e : 36 * e + 36] = other[128:256]
            d_others[start + 128 : start + 256, 36 * e : 36 * e + 36] = other[0:128]

    for f in range(2):
        rows = slice(256 * f, 256 * f + 256)
        for h in range(4):
            d_out = d_att[rows, 72 * h : 72 * h + 72]
            delta = jnp.sum(d_out.astype(F32) * attended[h, rows, :], axis=-1, keepdims=True)
            prob = probs[4 * f + h]
            d_prob = dot_nt(d_out, parts[8 + h, rows, :])
            d_score = (prob * (d_prob - delta)).astype(BF16)
            place(rows, h, dot_nn(d_score, parts[4 + h, rows, :]) * scale)
            place(rows, 4 + h, dot_tn(d_score, parts[h, rows, :]) * scale)
            place(rows, 8 + h, dot_tn(prob.astype(BF16), d_out))


def grad_first_body(d_mine, d_others, hidden, d_branch, low, *refs):
    outs, d_slots, total, below = refs[:9], refs[9], refs[10], refs[11]
    first = lax.axis_index("blk") % 2 == 0
    d_slots[...] = d_mine[...]
    for e in range(4):
        other = d_others[:, 36 * e : 36 * e + 36]
        for odd in range(2):
            at = 224 * e + 112 * odd + 72
            mine = d_mine[:, at : at + 36]
            d_slots[:, at : at + 36] = jnp.where(first == (odd == 0), mine, other)
    total[...] = dot_tn(d_slots[...], hidden[...]).astype(BF16)
    below[...] = dot_tn(d_branch[...], low[...]).astype(BF16)
    for k in range(8):
        at = pl.multiple_of(member_at(NEAR_FIRST[k]) * 112, 112)
        if k < 7:
            outs[k][0:112, :] = total[pl.ds(at, 112), :]
            tail, row = outs[k], 112
        else:
            outs[7][...] = total[pl.ds(at, 80), :]
            outs[8][0:32, :] = total[pl.ds(at + 80, 32), :]
            tail, row = outs[8], 32
        at = pl.multiple_of(member_at(NEAR_FIRST[k]) * 144, 144)
        for q in range(3):
            tail[row : row + 48, 288 * q : 288 * q + 288] = below[pl.ds(at + 48 * q, 48), :]
        tail[row : row + 48, 864:1152] = jnp.zeros((48, 288), BF16)


def d_hidden_a_body(d_slots, t0, t1, t2, t3, sums_b, d_gate_b, *refs):
    chunks = refs[:9]
    keep, send = refs[9:11]
    mods = refs[11:19]
    full, total, flat, d_mod = refs[19:]
    load_chunks(chunks, FIRST_PLACES, full, 0, 112)
    total[...] = dot_nn(d_slots[...], full[...])
    split_halves(total, keep, send)
    d_shift = jnp.zeros((1, 1152), F32)
    d_scale = jnp.zeros((1, 1152), F32)
    for f in range(2):
        for i, block in enumerate((t0, t1, t2, t3)):
            row = 256 * f + 64 * i
            norm, _ = norm_rows(block[f].astype(F32))
            part = total[row : row + 64, :]
            d_shift = d_shift + jnp.sum(part, axis=0, keepdims=True)
            d_scale = d_scale + jnp.sum(part * norm, axis=0, keepdims=True)
    d_mod[0:1, :] = d_shift
    d_mod[1:2, :] = d_scale
    d_mod[2:5, :] = sums_b[0:3, :]
    d_mod[5:6, :] = d_gate_b[...]
    for m in range(24):
        d, j = divmod(m, 3)
        flat[d : d + 1, 288 * j : 288 * j + 288] = d_mod[m // 4 : m // 4 + 1, 288 * (m % 4) : 288 * (m % 4) + 288]
    mine = lax.broadcasted_iota(jnp.int32, (8, 864), 0) == lax.axis_index("dp")
    for k, out in enumerate(mods):
        row = flat[pl.ds(member_at(NEAR_FIRST[k]), 1), :]
        out[...] = jnp.zeros((8, 1152), BF16)
        out[:, 0:864] = jnp.where(mine, row, 0.0).astype(BF16)


def own_half_body(keep, near, own, cross):
    for f in range(2):
        for i, block in enumerate((own, cross)):
            rows = slice(128 * f + 64 * i, 128 * f + 64 * i + 64)
            part = keep[rows, :] + near[rows, :].astype(F32)
            block[64 * f : 64 * f + 64, :] = part.astype(block.dtype)


def output_body(own, far, middle, mod, output):
    for f in range(2):
        rows = slice(64 * f, 64 * f + 64)
        output[f] = middle[rows, :] + mod[5:6, :] * (own[rows, :] + far[rows, :].astype(F32))


def grad_tokens_body(own, far, t0, d_mid, mod, grad):
    for f in range(2):
        rows = slice(64 * f, 64 * f + 64)
        norm, inv = norm_rows(t0[f].astype(F32))
        d_hidden = own[rows, :] + far[rows, :].astype(F32)
        grad[f] = d_mid[rows, :] + norm_back(d_hidden * (1.0 + mod[1:2, :]), norm, inv)


def cut_updown_body(u0, u1, u2, d0, d1, d2, here, near, cross, held):
    blk = lax.axis_index("blk")
    up = u0[...].astype(F32) + u1[0:144, :].astype(F32) + u2[0:144, :].astype(F32)
    down = d0[...].astype(F32) + d1[144:288, :].astype(F32) + d2[144:288, :].astype(F32)
    for t in range(4):
        held[t, :, 0:288] = up[:, 288 * t : 288 * t + 288].astype(BF16)
        held[t, :, 288:576] = down[:, 288 * t : 288 * t + 288].astype(BF16)
        held[t, :, 576:640] = jnp.zeros((144, 64), BF16)
    here[...] = held[blk]
    near[...] = held[blk ^ 1]
    cross[0:144, :] = held[blk ^ 2]
    cross[144:288, :] = held[blk ^ 3]


def final_updown_body(here, far, near, up, down, held):
    blk = lax.axis_index("blk")
    held[blk] = here[...]
    held[blk ^ 1] = near[0:144, :]
    held[blk ^ 2] = far[0:144, :]
    held[blk ^ 3] = near[144:288, :]
    for s in range(4):
        up[:, 144 * s : 144 * s + 144] = held[s, :, 0:288].astype(F32).T
        for part in range(2):
            at = 576 * part + 144 * s
            down[:, at : at + 144] = held[s, :, 288 + 144 * part : 432 + 144 * part].astype(F32)


def cut_heads_body(s0, s1, s2, m0, *refs):
    pieces, held = refs[:4], refs[4]
    blk = lax.axis_index("blk")
    total = s0[...].astype(F32) + s1[0:160, :].astype(F32) + s2[0:160, :].astype(F32)
    mods = m0[...].astype(F32) + s1[160:168, :].astype(F32) + s2[160:168, :].astype(F32)
    for t in range(4):
        held[t, :, 0:288] = jnp.zeros((144, 288), BF16)
        held[t, 0:108, 0:288] = total[0:108, 288 * t : 288 * t + 288].astype(BF16)
        held[t, 112:120, 0:216] = mods[:, 216 * t : 216 * t + 216].astype(BF16)
        for q in range(3):
            at = 288 * q + 72 * t
            held[t, 48 * q : 48 * q + 48, 288:360] = total[112:160, at : at + 72].astype(BF16)
        held[t, :, 360:384] = jnp.zeros((144, 24), BF16)
    for r in range(4):
        pieces[r][...] = held[blk ^ r]


def final_heads_body(timestep, p0, p1, p2, p3, qkv, out, table, held, placed, pieces, wide):
    blk = lax.axis_index("blk")
    mods = p0[112:120, 0:216].astype(F32) + p1[112:120, 0:216].astype(F32)
    mods = (mods + p2[112:120, 0:216].astype(F32) + p3[112:120, 0:216].astype(F32)).T
    wide[...] = jnp.zeros_like(wide)
    lane = lax.broadcasted_iota(jnp.int32, (216, 128), 1)
    for c in range(8):
        step = timestep[c]
        lanes = pl.ds(pl.multiple_of((step // 128) * 128, 128), 128)
        wide[:, lanes] = wide[:, lanes] + jnp.where(lane == step % 128, mods[:, c : c + 1], 0.0)
    table[...] = wide[:, 0 : table.shape[1]]
    for r, piece in enumerate((p0, p1, p2, p3)):
        pieces[blk ^ r] = piece[...]
    for sender in range(4):
        alone, shared = columns_of(sender)
        half = 36 * (sender & 1)
        placed[alone] = pieces[sender, 0:72, 0:288].astype(F32)
        placed[shared, half : half + 36, :] = pieces[sender, 72:108, 0:288].astype(F32)
        held[kind_of(sender)] = pieces[sender, :, 288:360].astype(F32)
    for i in range(6):
        qkv[:, 72 * i : 72 * i + 72] = placed[i].T
    for s in range(4):
        out[:, 72 * s : 72 * s + 72] = held[s]


def vmem(shape, kind=BF16):
    return (shape, kind)


def local_kernels(tokens, timestep, mod_table, w_qkv, w_out, w_up, w_down, cotangent):
    nd, nb = 8, 4
    ring = Ring(nd, lax.axis_index("dp"))
    group = Group(nb, lax.axis_index("blk"))
    width = tokens.shape[3]
    own_tokens = tokens[0]
    own_cot = cotangent[0]
    full_low = ((512, 1152), BF16)
    chunk_low = ((144, 1152), BF16)
    part_low = [chunk_low] * 7 + [((80, 1152), BF16), ((64, 1152), BF16)]
    half_low = ((256, 1152), BF16)
    half_wide = ((256, 1152), F32)
    own_wide = ((128, 1152), F32)

    def send_out(pieces):
        return [pieces[0]] + [group.swap(pieces[r], r) for r in (1, 2, 3)]

    def add_low(keep, near):
        return (keep + near.astype(F32)).astype(BF16)

    def own_half(keep, near, name):
        return run_kernel(own_half_body, [own_wide, ((128, 1152), BF16)], keep, near, name=name)

    picker = (timestep[:, None] == jnp.arange(mod_table.shape[0], dtype=jnp.int32)[None, :]).astype(BF16)
    table_cols = dot_nn(picker, mod_table).astype(BF16)
    heads_cut = run_kernel(
        pack_heads_body,
        [((144, 384), BF16)] * 4,
        w_qkv, w_out.T, table_cols,
        scratch=[vmem((2, 6, 36, 288)), vmem((4, 144, 72))],
        name="pack_heads",
    )
    heads_got = send_out(heads_cut)
    (first_own,) = run_kernel(
        join_heads_body,
        [((160, 1152), BF16)],
        *heads_got,
        scratch=[vmem((4, 144, 384)), vmem((8, 864), F32)],
        name="join_heads",
    )
    updown_cut = run_kernel(
        pack_updown_body,
        [((144, 640), BF16)] * 4,
        *after((w_up, w_down.T), heads_got[1]),
        scratch=[vmem((4, 144, 288)), vmem((4, 144, 288))],
        name="pack_updown",
    )
    updown_got = send_out(updown_cut)
    fore1, rear1, _ = step(ring, first_own, first_own)
    fore2, rear2, held = step(ring, fore1, rear1, own_tokens, *updown_got)
    far_t = group.swap(held[0], 2)
    up_own, down_own = run_kernel(
        join_updown_body, [chunk_low] * 2, *held[1:], scratch=[vmem((4, 144, 640))], name="join_updown"
    )
    fore3, rear3, held = step(ring, fore2, rear2, up_own, down_own, far_t, own_tokens, own_cot)
    up_own, down_own, far_t, own_t, own_c = held
    token_blocks = [own_tokens, far_t, group.swap(own_t, 1), group.swap(far_t, 1)]
    far_c = group.swap(own_c, 2)
    fore4, rear4, held = step(
        ring, stack(fore3[:80], up_own), stack(rear3[80:], up_own), far_c, own_cot, *token_blocks
    )
    far_c, own_c, *token_blocks = held
    cot_blocks = [own_cot, far_c, group.swap(own_c, 1), group.swap(far_c, 1)]
    first_got = [first_own, fore1, rear1, fore2, rear2, fore3, rear3, fore4, rear4]
    fore5, rear5, held = step(
        ring, stack(fore4[80:], down_own), stack(rear4[80:], down_own), *cot_blocks, *token_blocks, *first_got
    )
    cot_blocks, token_blocks, first_got = held[:4], held[4:8], held[8:]
    other_halves = stack(*(chunk[72:112] for chunk in first_got[:7]), first_got[7][72:80], first_got[8][:32])
    hidden_a, parts, probs, attended, low, out_full, mod, keep_a, send_a = run_kernel(
        attend_body,
        [
            full_low,
            ((12, 512, 72), BF16),
            ((8, 256, 256), F32),
            ((4, 512, 72), F32),
            ((512, 288), BF16),
            ((1152, 288), BF16),
            ((8, 1152), F32),
            half_wide,
            half_low,
        ],
        *token_blocks, group.swap(other_halves, 1), *first_got,
        scratch=[vmem((1280, 1152)), vmem((512, 1280)), vmem((384, 1152))],
        flops=4 * 10**9,
        name="attend",
    )
    fore6, rear6, (keep_a, send_a) = step(ring, fore5, rear5, keep_a, send_a)
    near_a = group.swap(send_a, 1)
    far_a = group.swap(add_low(keep_a, near_a), 2)
    fore7, rear7, (keep_a, near_a, far_a) = step(
        ring, stack(fore6[:80], fore6[144:]), rear6[80:], keep_a, near_a, far_a
    )
    hidden_mine, normed_b, root_b, branch_a, middle = run_kernel(
        middle_body,
        [half_low, half_wide, ((256, 128), F32), own_wide, own_wide],
        keep_a, near_a, far_a, *token_blocks[:2], mod,
        name="middle",
    )
    hidden_theirs = group.swap(hidden_mine, 1)
    fore8, rear8, (hidden_mine, hidden_theirs) = step(ring, fore7[80:160], rear7[144:], hidden_mine, hidden_theirs)
    up_got = [up_own, down_own, fore4, rear4, fore5, rear5, fore6, rear6, fore7, rear7]
    down_got = [*up_got, fore8, rear8]
    hidden_b, act, slope, d_branch_b, *grad_down = run_kernel(
        up_body,
        [full_low, full_low, ((512, 1152), F32), full_low] + part_low,
        hidden_mine, hidden_theirs, *cot_blocks, mod, *up_got,
        scratch=[vmem((1152, 1152)), vmem((1152, 1152))],
        flops=4 * 10**9,
        name="up",
    )
    fore1, rear1, held = step(ring, *grad_down[7:], d_branch_b, slope, *down_got)
    d_branch_b, slope, down_got = held[0], held[1], held[2:]
    d_pre, keep_d, send_d = run_kernel(
        down_body,
        [full_low, half_wide, half_low],
        d_branch_b, slope, *down_got,
        scratch=[vmem((1152, 1152)), vmem((1152, 1152))],
        flops=4 * 10**9,
        name="down",
    )
    near_d = group.swap(send_d, 1)
    low_d = add_low(keep_d, near_d)
    grad_up = run_kernel(
        grad_body,
        part_low,
        d_pre, hidden_b,
        scratch=[vmem((1152, 1152))],
        flops=2 * 10**9,
        name="grad_up",
    )
    fore2, rear2, (keep_d, near_d, low_d, act) = step(
        ring,
        stack(grad_up[7], sum_low(grad_down[6][:80], fore1), grad_down[6][80:]),
        stack(grad_up[8], grad_down[5][:80], sum_low(grad_down[5][80:], rear1)),
        keep_d, near_d, low_d, act,
    )
    far_d = group.swap(low_d, 2)
    keep_b, send_b, d_gate_b = run_kernel(
        branch_b_body,
        [half_wide, half_low, ((1, 1152), F32)],
        act, *cot_blocks, *down_got,
        scratch=[vmem((1152, 1152)), vmem((512, 1152), F32)],
        flops=2 * 10**9,
        name="branch_b",
    )
    near_b = group.swap(send_b, 1)
    fore3, rear3, (keep_d, near_d, far_d, keep_b, near_b) = step(
        ring,
        stack(sum_low(grad_up[6][:80], fore2[:80]), grad_up[6][80:], sum_low(grad_down[4], fore2[80:])),
        stack(grad_up[5][:80], sum_low(grad_up[5][80:], rear2[:64]), sum_low(grad_down[3], rear2[64:])),
        keep_d, near_d, far_d, keep_b, near_b,
    )
    d_low, d_mid, sums_b = run_kernel(
        d_middle_body,
        [half_low, own_wide, ((3, 1152), F32)],
        keep_d, near_d, far_d, normed_b, root_b, *cot_blocks[:2], branch_a, mod,
        name="d_middle",
    )
    d_branch_a, d_mine, d_others = run_kernel(
        d_attend_body,
        [full_low, ((512, 896), BF16), ((512, 144), BF16)],
        d_low, group.swap(d_low, 1), parts, probs, attended, out_full,
        scratch=[vmem((512, 288))],
        flops=3 * 10**9,
        name="d_attend",
    )
    d_others = group.swap(d_others, 1)
    fore4, rear4, held = step(
        ring,
        stack(sum_low(grad_up[4], fore3[:144]), sum_low(grad_down[2], fore3[144:])),
        stack(sum_low(grad_up[3], rear3[:144]), sum_low(grad_down[1], rear3[144:])),
        keep_b, near_b, d_mine, d_others, d_branch_a,
    )
    keep_b, near_b, d_mine, d_others, d_branch_a = held
    own_b, cross_b = own_half(keep_b, near_b, "own_b")
    far_b = group.swap(cross_b, 2)
    *grad_first, d_slots = run_kernel(
        grad_first_body,
        [((160, 1152), BF16)] * 7 + [((80, 1152), BF16)] * 2 + [((512, 896), BF16)],
        d_mine, d_others, hidden_a, d_branch_a, low,
        scratch=[vmem((896, 1152)), vmem((1152, 288))],
        flops=2 * 10**9,
        name="grad_first",
    )
    keep_h, send_h, *mods = run_kernel(
        d_hidden_a_body,
        [half_wide, half_low] + [((8, 1152), BF16)] * 8,
        d_slots, *token_blocks, sums_b, d_gate_b, *first_got,
        scratch=[
            vmem((896, 1152)),
            vmem((512, 1152), F32),
            vmem((8, 864), F32),
            vmem((6, 1152), F32),
        ],
        flops=2 * 10**9,
        name="d_hidden_a",
    )
    fore5, rear5, (keep_h, send_h, own_b, far_b) = step(
        ring,
        stack(sum_low(grad_up[2], fore4[:144]), grad_first[7], mods[7]),
        stack(sum_low(grad_up[1], rear4[:144]), grad_first[8]),
        keep_h, send_h, own_b, far_b,
    )
    near_h = group.swap(send_h, 1)
    fore6, rear6, held = step(
        ring,
        stack(sum_low(grad_first[6][:80], fore5[144:224]), grad_first[6][80:], sum_low(mods[6], fore5[224:])),
        stack(grad_first[5][:80], sum_low(grad_first[5][80:], rear5[144:]), mods[5]),
        keep_h, near_h, fore4, rear4, fore5, rear5,
    )
    keep_h, near_h, *up_down = held
    own_h, cross_h = own_half(keep_h, near_h, "own_h")
    far_h = group.swap(cross_h, 2)
    here, near_u, cross_u = run_kernel(
        cut_updown_body,
        [((144, 640), BF16)] * 2 + [((288, 640), BF16)],
        grad_up[0], *up_down[2:], grad_down[0], *up_down[:2],
        scratch=[vmem((4, 144, 640))],
        name="cut_updown",
    )
    fore7, rear7, held = step(
        ring,
        stack(sum_low(grad_first[4], fore6[:160]), sum_low(mods[4], fore6[160:])),
        stack(sum_low(grad_first[3], rear6[:160]), sum_low(mods[3], rear6[160:])),
        here, near_u, cross_u,
    )
    here, near_u, cross_u = held
    far_u = group.swap(cross_u, 2)
    fore8, rear8, held = step(
        ring,
        stack(sum_low(grad_first[2], fore7[:160]), sum_low(mods[2], fore7[160:])),
        stack(sum_low(grad_first[1], rear7[:160]), sum_low(mods[1], rear7[160:])),
        own_h, far_h, own_b, far_b, here, near_u, far_u,
    )
    own_h, far_h, own_b, far_b, here, near_u, far_u = held
    (output,) = run_kernel(
        output_body, [((2, 64, 1152), F32)], own_b, far_b, middle, mod, name="output"
    )
    (grad_tokens,) = run_kernel(
        grad_tokens_body, [((2, 64, 1152), F32)], own_h, far_h, own_tokens, d_mid, mod, name="grad_tokens"
    )
    final_up, final_down = run_kernel(
        final_updown_body,
        [((288, 576), F32), ((144, 1152), F32)],
        here, far_u, group.swap(stack(near_u, far_u[144:]), 1),
        scratch=[vmem((4, 144, 640))],
        name="final_updown",
    )
    heads_cut = run_kernel(
        cut_heads_body, [((144, 384), BF16)] * 4, grad_first[0], fore8, rear8, mods[0], scratch=[vmem((4, 144, 384))], name="cut_heads"
    )
    final_qkv, final_out, grad_table = run_kernel(
        final_heads_body,
        [((288, 432), F32), ((144, 288), F32), ((216, mod_table.shape[0]), F32)],
        timestep, *send_out(heads_cut),
        scalars=1,
        scratch=[
            vmem((4, 144, 72), F32),
            vmem((6, 72, 288), F32),
            vmem((4, 144, 384)),
            vmem((216, -(-mod_table.shape[0] // 128) * 128), F32),
        ],
        name="final_heads",
    )
    return (output[None], grad_tokens[None], grad_table.T, final_qkv, final_out.T, final_up, final_down.T)


def local(tokens, timestep, mod_table, w_qkv, w_out, w_up, w_down, cotangent):
    sizes = (lax.axis_size("dp"), lax.axis_size("blk"), tokens.shape, w_qkv.shape, w_up.shape, w_down.shape)
    known = (8, 4, (1, 2, 64, 1152), (288, 432), (288, 576), (1152, 144))
    chosen = local_kernels if sizes == known else local_plain
    return chosen(tokens, timestep, mod_table, w_qkv, w_out, w_up, w_down, cotangent)


def solution(mesh):
    in_specs = (
        P("dp", None, "blk", None),
        P(),
        P(None, ("dp", "blk")),
        P("blk", "dp"),
        P("blk", "dp"),
        P("blk", "dp"),
        P("blk", "dp"),
        P("dp", None, "blk", None),
    )
    out_specs = (
        P("dp", None, "blk", None),
        P("dp", None, "blk", None),
        P(None, ("dp", "blk")),
        P("blk", "dp"),
        P("blk", "dp"),
        P("blk", "dp"),
        P("blk", "dp"),
    )
    return jax.shard_map(local, mesh=mesh, in_specs=in_specs, out_specs=out_specs, check_vma=False)
```

```python
import math
from functools import partial

import jax
import jax.numpy as jnp
from jax import lax
from jax.experimental import pallas as pl
from jax.experimental.pallas import tpu as pltpu
from jax.sharding import PartitionSpec as P

HEADS = 16
HEAD_DIM = 72
EPS = 1e-06
HIGHEST = lax.Precision.HIGHEST
BF16 = jnp.bfloat16
F32 = jnp.float32


def norm_rows(values):
    center = values - jnp.mean(values, axis=-1, keepdims=True)
    spread = jnp.mean(center * center, axis=-1, keepdims=True)
    root_inv = lax.rsqrt(spread + EPS)
    return (center * root_inv, root_inv)


def norm_back(d_normed, normed, root_inv):
    mean_one = jnp.mean(d_normed, axis=-1, keepdims=True)
    mean_two = jnp.mean(d_normed * normed, axis=-1, keepdims=True)
    return root_inv * (d_normed - mean_one - normed * mean_two)


def dot_nn(left, right):
    return jnp.dot(left, right, preferred_element_type=F32)


def dot_tn(left, right):
    return lax.dot_general(left, right, (((0,), (0,)), ((), ())), preferred_element_type=F32)


def dot_nt(left, right):
    return lax.dot_general(left, right, (((1,), (1,)), ((), ())), preferred_element_type=F32)


class Ring:
    def __init__(self, size, index):
        self.size = size
        self.order = list(range(0, size, 2)) + list(range(size - 1, 0, -2))
        place = [0] * size
        for spot, member in enumerate(self.order):
            place[member] = spot
        self.spot = jnp.array(place, jnp.int32)[index]
        self.table = jnp.array(self.order, jnp.int32)
        self.ahead = [(self.order[i], self.order[(i + 1) % size]) for i in range(size)]
        self.back = [(right, left) for left, right in self.ahead]

    def member(self, offset):
        return self.table[(self.spot + offset) % self.size]

    def gather(self, chunk):
        half = self.size // 2
        cut = chunk.shape[0] // 2
        out = jnp.zeros((self.size,) + chunk.shape, chunk.dtype)

        def put(out, piece, offset, row=0):
            return lax.dynamic_update_slice(out, piece[None], (self.member(offset), row, 0))

        out = put(out, chunk, 0)
        fore = rear = chunk
        for step in range(1, half):
            fore = lax.ppermute(fore, "dp", self.ahead)
            rear = lax.ppermute(rear, "dp", self.back)
            out = put(put(out, fore, -step), rear, step)
        fore = lax.ppermute(fore[:cut], "dp", self.ahead)
        rear = lax.ppermute(rear[cut:], "dp", self.back)
        return put(put(out, fore, half), rear, half, cut)

    def scatter(self, parts):
        half = self.size // 2
        cut = parts.shape[1] // 2

        def own(offset):
            return lax.dynamic_index_in_dim(parts, self.member(offset), 0, keepdims=False)

        far = own(half)
        fore = lax.ppermute(far[:cut], "dp", self.ahead)
        rear = lax.ppermute(far[cut:], "dp", self.back)
        for step in range(half - 1, 0, -1):
            mine_fore = own(step).astype(F32)
            mine_rear = own(-step).astype(F32)
            if step == half - 1:
                fore = jnp.concatenate([mine_fore[:cut] + fore.astype(F32), mine_fore[cut:]], axis=0)
                rear = jnp.concatenate([mine_rear[:cut], mine_rear[cut:] + rear.astype(F32)], axis=0)
            else:
                fore = mine_fore + fore.astype(F32)
                rear = mine_rear + rear.astype(F32)
            fore = lax.ppermute(fore.astype(BF16), "dp", self.ahead)
            rear = lax.ppermute(rear.astype(BF16), "dp", self.back)
        return own(0).astype(F32) + fore.astype(F32) + rear.astype(F32)


class Group:
    def __init__(self, size, index):
        self.size = size
        self.index = index
        self.bits = []
        bit = size // 2
        while bit:
            self.bits.append(bit)
            bit //= 2

    def swap(self, values, bit):
        return lax.ppermute(values, "blk", [(i, i ^ bit) for i in range(self.size)])

    def exchange(self, pieces):
        if self.size > 4:
            return lax.all_to_all(pieces, "blk", 0, 0, tiled=True)
        got = []
        for r in range(self.size):
            piece = lax.dynamic_index_in_dim(pieces, self.index ^ r, 0, keepdims=False)
            got.append(self.swap(piece, r) if r else piece)
        bit = 1
        while bit < self.size:
            odd = (self.index & bit) != 0
            got = [jnp.where(odd, got[r ^ bit], got[r]) for r in range(self.size)]
            bit *= 2
        return jnp.stack(got)

    def gather(self, block, bits=None):
        for bit in self.bits if bits is None else bits:
            block = jnp.concatenate([block, self.swap(block, bit)], axis=0)
        return block

    def scatter(self, parts, share):
        for bit in reversed(self.bits[1:]):
            half = parts.shape[0] // 2
            parts = parts[:half] + self.swap(parts[half:].astype(BF16), bit).astype(F32)
        top = self.bits[0]
        if share:
            return parts + self.swap(parts.astype(BF16), top)[::-1].astype(F32)
        return parts[:1] + self.swap(parts[1:].astype(BF16), top).astype(F32)


def local_plain(tokens, timestep, mod_table, w_qkv, w_out, w_up, w_down, cotangent):
    frames, patches, width = tokens.shape[1:]
    nd = lax.axis_size("dp")
    nb = lax.axis_size("blk")
    dp = lax.axis_index("dp")
    blk = lax.axis_index("blk")
    ring = Ring(nd, dp)
    group = Group(nb, blk)
    rows = nb * frames * patches
    scale = HEAD_DIM ** (-0.5)
    heads = HEADS // nb
    deep = width // nb
    ff = w_down.shape[0]
    hidden = w_up.shape[1]
    out_cols = w_out.shape[1]

    columns = w_qkv.shape[1] // HEAD_DIM
    slots = -(-columns // nb)
    offset = (columns * dp) % nb
    qkv_t = w_qkv.T.reshape(columns, HEAD_DIM, deep)
    qkv_pos = jnp.zeros((2 * slots * nb, HEAD_DIM, deep), BF16)
    qkv_pos = lax.dynamic_update_slice(qkv_pos, qkv_t, (offset, 0, 0))
    qkv_pos = qkv_pos[: slots * nb] + qkv_pos[slots * nb :]
    qkv_send = qkv_pos.reshape(slots, nb, HEAD_DIM, deep).transpose(1, 0, 2, 3)
    qkv_send = qkv_send.reshape(nb, slots * HEAD_DIM, deep)
    spread = heads // nb
    if spread:
        out_send = w_out.T.reshape(out_cols, spread, nb, HEAD_DIM).transpose(2, 0, 1, 3)
        out_send = out_send.reshape(nb, out_cols, spread * HEAD_DIM)
    up_send = w_up.T.reshape(nb, hidden // nb, deep)
    many = ff // hidden
    down_send = w_down.T.reshape(out_cols, many, nb, hidden // nb).transpose(2, 0, 1, 3)
    down_send = down_send.reshape(nb, out_cols, many * hidden // nb)
    first = group.exchange(jnp.concatenate([qkv_send, out_send], axis=2) if spread else qkv_send)
    up_got = group.exchange(up_send)
    down_got = group.exchange(down_send)
    qkv_own = first[:, :, :deep].transpose(1, 0, 2).reshape(slots * HEAD_DIM, width)
    out_own = first[:, :, deep:].transpose(1, 0, 2).reshape(out_cols, heads * HEAD_DIM) if spread else w_out.T
    up_own = up_got.transpose(1, 0, 2).reshape(hidden // nb, width)
    down_own = down_got.transpose(1, 0, 2).reshape(out_cols, nd * hidden // nb)

    token_all = group.gather(tokens)
    cot_all = group.gather(cotangent)

    picker = (timestep[:, None] == jnp.arange(mod_table.shape[0], dtype=jnp.int32)[None, :]).astype(BF16)
    table_cols = dot_nn(picker, mod_table).astype(BF16)
    piece = table_cols.shape[1]
    mods_send = jnp.broadcast_to(table_cols[:, None, :], (nd, nb, piece)).reshape(nd * nb, piece)
    mod_row = lax.all_to_all(mods_send, ("dp", "blk"), 0, 0, tiled=True).reshape(6, width).astype(F32)
    shift_a, scale_a, gate_a, shift_b, scale_b, gate_b = (mod_row[i] for i in range(6))

    first_all = ring.gather(jnp.concatenate([qkv_own, out_own], axis=1))
    up_full = ring.gather(up_own).reshape(ff, width)
    down_full = ring.gather(down_own).reshape(width, ff)
    out_full = first_all[:, :, width:].reshape(width, heads * HEAD_DIM)
    wanted = blk + nb * jnp.arange(3 * heads, dtype=jnp.int32)
    holder = wanted // columns
    place = ((wanted - columns * holder + (columns * holder) % nb) % (slots * nb)) // nb
    slot_of = holder * slots + place
    qkv_slots = first_all[:, :, :width].reshape(nd * slots, HEAD_DIM, width)
    qkv_full = jnp.take(qkv_slots, slot_of, axis=0).reshape(3 * heads * HEAD_DIM, width)

    inputs = token_all.reshape(rows, width).astype(F32)
    normed_a, root_a = norm_rows(inputs)
    hidden_a = (normed_a * (1.0 + scale_a) + shift_a).astype(BF16)
    projected = dot_nt(hidden_a, qkv_full).astype(BF16)

    def by_head(values, parts):
        split = values.reshape(nb, frames, patches, parts, heads, HEAD_DIM)
        split = split.transpose(3, 1, 4, 0, 2, 5)
        return split.reshape(parts, frames, heads, nb * patches, HEAD_DIM)

    def by_row(values):
        split = values.reshape(-1, frames, heads, nb, patches, HEAD_DIM)
        return split.transpose(3, 1, 4, 0, 2, 5).reshape(rows, -1)

    query, keys, values = by_head(projected, 3)
    scores = jnp.einsum("fhqe,fhke->fhqk", query, keys, preferred_element_type=F32) * scale
    top = jnp.max(scores, axis=-1, keepdims=True)
    weights = jnp.exp(scores - top)
    probs = weights / jnp.sum(weights, axis=-1, keepdims=True)
    probs_low = probs.astype(BF16)
    attended = jnp.einsum("fhqk,fhke->fhqe", probs_low, values, preferred_element_type=F32)
    attn_low = by_row(attended).astype(BF16)
    share = 2 * frames * patches
    own = frames * patches

    def blocks(partial_sum):
        return partial_sum.reshape(nb, own, width)

    branch_a = group.scatter(blocks(dot_nt(attn_low, out_full)), True).reshape(share, width)
    middle = inputs[:share] + gate_a * branch_a
    normed_b, root_b = norm_rows(middle)
    hidden_low = (normed_b * (1.0 + scale_b) + shift_b).astype(BF16)
    hidden_b = group.gather(hidden_low.reshape(2, own, width), group.bits[1:]).reshape(rows, width)
    pre_act = dot_nt(hidden_b, up_full)
    activated, gelu_back = jax.vjp(partial(jax.nn.gelu, approximate=True), pre_act)
    act_low = activated.astype(BF16)
    grad_in = cot_all.reshape(rows, width).astype(F32)
    d_branch_b = (gate_b * grad_in).astype(BF16)
    grad_down = dot_tn(d_branch_b, act_low).astype(BF16)
    down_sum = ring.scatter(grad_down.reshape(nd, out_cols, ff))
    d_act = dot_nn(d_branch_b, down_full)
    d_pre = gelu_back(d_act)[0].astype(BF16)
    grad_up = dot_tn(d_pre, hidden_b).astype(BF16)
    up_sum = ring.scatter(grad_up.reshape(nd, hidden // nb, width))
    d_hidden_b = group.scatter(blocks(dot_nn(d_pre, up_full)), True).reshape(share, width)
    branch_b = group.scatter(blocks(dot_nt(act_low, down_full)), False).reshape(own, width)
    output = (middle[:own] + gate_b * branch_b).reshape(tokens.shape)
    d_gate_b = jnp.sum(grad_in[:own] * branch_b, axis=0)
    d_shift_b = jnp.sum(d_hidden_b[:own], axis=0)
    d_scale_b = jnp.sum(d_hidden_b[:own] * normed_b[:own], axis=0)
    d_middle = grad_in[:share] + norm_back(d_hidden_b * (1.0 + scale_b), normed_b, root_b)
    d_gate_a = jnp.sum(d_middle[:own] * branch_a[:own], axis=0)
    d_branch_a = (gate_a * d_middle).astype(BF16).reshape(2, own, width)
    d_branch_a = group.gather(d_branch_a, group.bits[1:]).reshape(rows, width)
    grad_out = dot_tn(d_branch_a, attn_low).astype(BF16)
    d_attended = dot_nn(d_branch_a, out_full).astype(BF16)
    d_att = by_head(d_attended, 1)[0]
    delta = jnp.sum(d_att.astype(F32) * attended, axis=-1, keepdims=True)
    d_probs = jnp.einsum("fhqe,fhke->fhqk", d_att, values, preferred_element_type=F32)
    d_scores = (probs * (d_probs - delta)).astype(BF16)
    d_query = jnp.einsum("fhqk,fhke->fhqe", d_scores, keys, preferred_element_type=F32) * scale
    d_key = jnp.einsum("fhqk,fhqe->fhke", d_scores, query, preferred_element_type=F32) * scale
    d_value = jnp.einsum("fhqk,fhqe->fhke", probs_low, d_att, preferred_element_type=F32)
    d_projected = by_row(jnp.stack([d_query, d_key, d_value]).astype(BF16))
    grad_qkv = dot_tn(d_projected, hidden_a).astype(BF16).reshape(3 * heads, HEAD_DIM, width)
    grad_slots = jnp.zeros((nd * slots, HEAD_DIM, width), BF16).at[slot_of].set(grad_qkv)
    grad_first = jnp.concatenate(
        [
            grad_slots.reshape(nd, slots * HEAD_DIM, width),
            grad_out.reshape(nd, out_cols, heads * HEAD_DIM),
        ],
        axis=2,
    )
    first_sum = ring.scatter(grad_first)
    d_hidden_a = group.scatter(blocks(dot_nn(d_projected, qkv_full)), False).reshape(own, width)
    d_shift_a = jnp.sum(d_hidden_a, axis=0)
    d_scale_a = jnp.sum(d_hidden_a * normed_a[:own], axis=0)
    d_normed = norm_back(d_hidden_a * (1.0 + scale_a), normed_a[:own], root_a[:own])
    grad_tokens = (d_middle[:own] + d_normed).reshape(tokens.shape)

    d_mod = jnp.concatenate([d_shift_a, d_scale_a, d_gate_a, d_shift_b, d_scale_b, d_gate_b])
    mod_got = lax.all_to_all(d_mod.reshape(nd * nb, piece), ("dp", "blk"), 0, 0, tiled=True)
    mod_sums = jnp.sum(mod_got.reshape(nd, nb, piece), axis=1)
    grad_table = lax.dot_general(
        picker.astype(F32),
        mod_sums,
        (((0,), (0,)), ((), ())),
        precision=HIGHEST,
        preferred_element_type=F32,
    )

    up_back = group.exchange(up_sum.astype(BF16).reshape(hidden // nb, nb, deep).transpose(1, 0, 2))
    final_up = up_back.reshape(hidden, deep).T.astype(F32)
    down_back = down_sum.astype(BF16).reshape(out_cols, nb, many, hidden // nb).transpose(1, 0, 2, 3)
    down_back = group.exchange(down_back.reshape(nb, out_cols, many * hidden // nb))
    down_back = down_back.reshape(nb, out_cols, many, hidden // nb).transpose(2, 0, 3, 1)
    final_down = down_back.reshape(ff, out_cols).astype(F32)
    first_low = first_sum.astype(BF16)
    qkv_back = first_low[:, :width].reshape(slots * HEAD_DIM, nb, deep).transpose(1, 0, 2)
    out_back = first_low[:, width:]
    if spread:
        out_back = out_back.reshape(out_cols, nb, spread * HEAD_DIM).transpose(1, 0, 2)
        back = group.exchange(jnp.concatenate([qkv_back, out_back], axis=2))
        out_back = back[:, :, deep:].reshape(nb, out_cols, spread, HEAD_DIM).transpose(2, 0, 3, 1)
        final_out = out_back.reshape(deep, out_cols).astype(F32)
    else:
        back = group.exchange(qkv_back)
        final_out = out_back.T.astype(F32)
    qkv_back = back[:, :, :deep].reshape(nb, slots, HEAD_DIM, deep).transpose(1, 0, 2, 3)
    qkv_back = qkv_back.reshape(slots * nb, HEAD_DIM, deep)
    qkv_back = lax.dynamic_slice(
        jnp.concatenate([qkv_back, qkv_back], axis=0), (offset, 0, 0), (columns, HEAD_DIM, deep)
    )
    final_qkv = qkv_back.reshape(columns * HEAD_DIM, deep).T.astype(F32)
    return (output, grad_tokens, grad_table, final_qkv, final_out, final_up, final_down)


GELU_IN = 0.7978845608028654
GELU_CUBE = 0.044715


def padded_bytes(shape, kind):
    *lead, rows, lanes = shape
    return math.prod(lead) * -(-rows // 16) * 16 * -(-lanes // 128) * 128 * jnp.dtype(kind).itemsize


def run_kernel(body, outs, *args, scalars=0, scratch=(), spare=8, flops=0, name=None):
    held = list(outs) + list(scratch) + [(a.shape, a.dtype) for a in args[scalars:]]
    limit = sum(padded_bytes(*h) for h in held) + (spare << 20)
    moved = sum(padded_bytes(*o) for o in outs) + sum(padded_bytes(a.shape, a.dtype) for a in args[scalars:])
    return pl.pallas_call(
        body,
        out_shape=[jax.ShapeDtypeStruct(shape, t) for shape, t in outs],
        in_specs=[pl.BlockSpec(memory_space=pltpu.SMEM if i < scalars else pltpu.VMEM) for i in range(len(args))],
        out_specs=[pl.BlockSpec(memory_space=pltpu.VMEM) for _ in outs],
        scratch_shapes=[pltpu.VMEM(*h) for h in scratch],
        compiler_params=pltpu.CompilerParams(vmem_limit_bytes=limit),
        cost_estimate=pl.CostEstimate(flops=flops, bytes_accessed=moved, transcendentals=0),
        name=name,
    )(*args)


def after(value, *others):
    return lax.optimization_barrier((value, *others))[0]


def step(ring, fore, rear, *carry):
    (fore, rear), carry = lax.optimization_barrier(((fore, rear), carry))
    return lax.ppermute(fore, "dp", ring.ahead), lax.ppermute(rear, "dp", ring.back), carry


def sum_low(mine, got):
    return (mine.astype(F32) + got.astype(F32)).astype(BF16)


def stack(*blocks):
    return jnp.concatenate(blocks, axis=0)


NEAR_FIRST = (0, -1, 1, -2, 2, -3, 3, 4)


def member_at(offset):
    dp = lax.axis_index("dp")
    spot = jnp.where(dp % 2 == 0, dp // 2, 7 - dp // 2)
    at = (spot + offset + 8) % 8
    return jnp.where(at < 4, 2 * at, 15 - 2 * at)


def kind_of(device):
    return (device >> 1) | ((device & 1) << 1)


def columns_of(device):
    odd = lax.axis_index("dp") & 1
    return kind_of(device) + 2 * odd, (device >> 1) + 4 - 4 * odd


def turn(values):
    return values.astype(F32).T.astype(BF16)


def pack_heads_body(qkv, out, mods, *refs):
    heads, held_q, held_o = refs[:4], refs[4], refs[5]
    blk = lax.axis_index("blk")
    for i in range(6):
        for half in range(2):
            at = 72 * i + 36 * half
            held_q[half, i] = turn(qkv[:, at : at + 36])
    for t in range(4):
        held_o[t] = out[:, 72 * kind_of(t) : 72 * kind_of(t) + 72]
    for r in range(4):
        t = blk ^ r
        alone, shared = columns_of(t)
        heads[r][...] = jnp.zeros((144, 384), BF16)
        heads[r][0:36, 0:288] = held_q[0, alone]
        heads[r][36:72, 0:288] = held_q[1, alone]
        heads[r][72:108, 0:288] = held_q[t & 1, shared]
        heads[r][112:120, 0:216] = mods[...]
        heads[r][:, 288:360] = held_o[t]


def pack_updown_body(up, down, *refs):
    updown, held_u, held_d = refs[:4], refs[4], refs[5]
    blk = lax.axis_index("blk")
    for t in range(4):
        held_u[t] = turn(up[:, 144 * t : 144 * t + 144])
        for part in range(2):
            at = 576 * part + 144 * t
            held_d[t, :, 144 * part : 144 * part + 144] = down[:, at : at + 144]
    for r in range(4):
        t = blk ^ r
        updown[r][:, 0:288] = held_u[t]
        updown[r][:, 288:576] = held_d[t]
        updown[r][:, 576:640] = jnp.zeros((144, 64), BF16)


def join_heads_body(*refs):
    pieces, joined, held, row = refs[:4], refs[4], refs[5], refs[6]
    blk = lax.axis_index("blk")
    for r in range(4):
        held[blk ^ r] = pieces[r][...]
    joined[96:160, :] = jnp.zeros((64, 1152), BF16)
    for s in range(4):
        joined[0:108, 288 * s : 288 * s + 288] = held[s, 0:108, 0:288]
        for q in range(3):
            at = 288 * q + 72 * s
            joined[112:160, at : at + 72] = held[s, 48 * q : 48 * q + 48, 288:360]
        row[:, 216 * s : 216 * s + 216] = held[s, 112:120, 0:216].astype(F32)
    for j in range(3):
        joined[112 + 16 * j : 120 + 16 * j, 864:1152] = row[:, 288 * j : 288 * j + 288].astype(BF16)


def join_updown_body(*refs):
    pieces, up, down, held = refs[:4], refs[4], refs[5], refs[6]
    blk = lax.axis_index("blk")
    for r in range(4):
        held[blk ^ r] = pieces[r][...]
    for s in range(4):
        up[:, 288 * s : 288 * s + 288] = held[s, :, 0:288]
        down[:, 288 * s : 288 * s + 288] = held[s, :, 288:576]


FIRST_PLACES = (
    (0, 0, 0, 160, 0),
    (-1, 1, 0, 160, 0),
    (1, 2, 0, 160, 0),
    (-2, 3, 0, 160, 0),
    (2, 4, 0, 160, 0),
    (-3, 5, 0, 160, 0),
    (3, 6, 0, 160, 0),
    (4, 7, 0, 80, 0),
    (4, 8, 0, 80, 80),
)
UP_PLACES = (
    (0, 0, 0, 144, 0),
    (-1, 2, 80, 144, 0),
    (1, 3, 80, 144, 0),
    (-2, 4, 0, 144, 0),
    (2, 5, 0, 144, 0),
    (-3, 6, 0, 144, 0),
    (3, 7, 0, 144, 0),
    (4, 8, 0, 80, 0),
    (4, 9, 0, 64, 80),
)
DOWN_PLACES = (
    (0, 1, 0, 144, 0),
    (-1, 4, 144, 144, 0),
    (1, 5, 144, 144, 0),
    (-2, 6, 144, 144, 0),
    (2, 7, 144, 144, 0),
    (-3, 8, 80, 144, 0),
    (3, 9, 64, 144, 0),
    (4, 10, 0, 80, 0),
    (4, 11, 0, 64, 80),
)


def load_chunks(arrays, places, full, first=0, count=144, pitch=None):
    pitch = pitch or count
    for offset, index, start, rows, row in places:
        low, high = max(first, row), min(first + count, row + rows)
        if low < high:
            at = pl.multiple_of(member_at(offset) * pitch + low - first, 16)
            full[pl.ds(at, high - low), :] = arrays[index][start + low - row : start + high - row, :]


def split_halves(total, keep, send):
    for f in range(2):
        keep[128 * f : 128 * f + 128, :] = total[256 * f : 256 * f + 128, :]
        send[128 * f : 128 * f + 128, :] = total[256 * f + 128 : 256 * f + 256, :].astype(BF16)


def join_halves(mine, theirs, full):
    for f in range(2):
        full[256 * f : 256 * f + 128, :] = mine[128 * f : 128 * f + 128, :]
        full[256 * f + 128 : 256 * f + 256, :] = theirs[128 * f : 128 * f + 128, :]


def attend_body(t0, t1, t2, t3, halves, g0, g1, g2, g3, *refs):
    chunks = refs[:9]
    hidden, parts, probs, attended, low, out, mod, keep, send, d_branch = refs[9:19]
    full, slots, tail = refs[19:]
    load_chunks(chunks, FIRST_PLACES, tail, 112, 48)
    load_chunks(chunks, FIRST_PLACES, full, 0, 112, 160)
    clip = lax.axis_index("dp")
    own = lax.broadcasted_iota(jnp.int32, (8, 288), 0) == clip
    for m in range(24):
        d, j = divmod(m, 3)
        rows = tail[48 * d + 16 * j : 48 * d + 16 * j + 8, 864:1152].astype(F32)
        row = jnp.sum(jnp.where(own, rows, 0.0), axis=0, keepdims=True)
        mod[m // 4 : m // 4 + 1, 288 * (m % 4) : 288 * (m % 4) + 288] = row
        out[48 * m : 48 * m + 48, :] = tail[48 * d : 48 * d + 48, 288 * j : 288 * j + 288]
    for i, block in enumerate((t0, t1, t2, t3)):
        for f in range(2):
            normed, _ = norm_rows(block[f].astype(F32))
            at = 256 * f + 64 * i
            hidden[at : at + 64, :] = (normed * (1.0 + mod[1:2, :]) + mod[0:1, :]).astype(BF16)
    for i, block in enumerate((g0, g1, g2, g3)):
        for f in range(2):
            at = 256 * f + 64 * i
            d_branch[at : at + 64, :] = (mod[5:6, :] * block[f].astype(F32)).astype(BF16)
    for k, offset in enumerate(NEAR_FIRST):
        at = pl.multiple_of(member_at(offset) * 160 + 112, 16)
        full[pl.ds(at, 48), :] = jnp.concatenate([halves[40 * k : 40 * k + 40, :], jnp.zeros((8, 1152), BF16)], axis=0)
    slots[...] = dot_nt(hidden[...], full[...]).astype(BF16)
    first = lax.axis_index("blk") % 2 == 0
    for e in range(4):
        at = 320 * e
        parts[3 * e] = slots[:, at : at + 72]
        parts[3 * e + 2] = slots[:, at + 160 : at + 232]
        near = jnp.where(first, slots[:, at + 72 : at + 108], slots[:, at + 272 : at + 308])
        far = jnp.where(first, slots[:, at + 112 : at + 148], slots[:, at + 232 : at + 268])
        parts[3 * e + 1, :, 0:36] = near
        parts[3 * e + 1, :, 36:72] = far
    scale = HEAD_DIM ** (-0.5)
    for f in range(2):
        rows = slice(256 * f, 256 * f + 256)
        for h in range(4):
            scores = dot_nt(parts[h, rows, :], parts[4 + h, rows, :]) * scale
            weights = jnp.exp(scores - jnp.max(scores, axis=-1, keepdims=True))
            prob = weights / jnp.sum(weights, axis=-1, keepdims=True)
            probs[4 * f + h] = prob
            mixed = dot_nn(prob.astype(BF16), parts[8 + h, rows, :])
            attended[h, rows, :] = mixed
            low[rows, 72 * h : 72 * h + 72] = mixed.astype(BF16)
    split_halves(dot_nt(low[...], out[...]), keep, send)


def middle_body(keep, near, far, t0, t1, mod, hidden, normed, root, branch, middle):
    for f in range(2):
        for i, block in enumerate((t0, t1)):
            rows = slice(128 * f + 64 * i, 128 * f + 64 * i + 64)
            cross = slice(128 * f + 64 * (1 - i), 128 * f + 64 * (1 - i) + 64)
            part = keep[rows, :] + near[rows, :].astype(F32) + far[cross, :].astype(F32)
            mid = block[f].astype(F32) + mod[2:3, :] * part
            norm, inv = norm_rows(mid)
            hidden[rows, :] = (norm * (1.0 + mod[4:5, :]) + mod[3:4, :]).astype(BF16)
            normed[rows, :] = norm
            root[rows, :] = jnp.broadcast_to(inv, (64, 128))
            if i == 0:
                branch[64 * f : 64 * f + 64, :] = part
                middle[64 * f : 64 * f + 64, :] = mid


def write_parts(total, outs):
    cut = outs[7].shape[0]
    for k in range(8):
        at = pl.multiple_of(member_at(NEAR_FIRST[k]) * 144, 144)
        if k < 7:
            outs[k][...] = total[pl.ds(at, 144), :]
        else:
            outs[7][...] = total[pl.ds(at, cut), :]
            outs[8][...] = total[pl.ds(at + cut, 144 - cut), :]


def up_body(mine, theirs, d_branch, *refs):
    chunks = refs[:10]
    hidden, act, slope = refs[10:13]
    parts = refs[13:22]
    up, total = refs[22:]
    load_chunks(chunks, UP_PLACES, up)
    join_halves(mine, theirs, hidden)
    for at in range(0, 512, 256):
        rows = slice(at, at + 256)
        pre = dot_nt(hidden[rows, :], up[...])
        square = pre * pre
        bend = jnp.tanh(GELU_IN * (pre + GELU_CUBE * (square * pre)))
        half = 0.5 * (1.0 + bend)
        act[rows, :] = (pre * half).astype(BF16)
        inner = GELU_IN * (1.0 + (3.0 * GELU_CUBE) * square)
        slope[rows, :] = half + (0.5 * pre) * ((1.0 - bend * bend) * inner)
    total[...] = dot_tn(d_branch[...], act[...]).astype(BF16)
    write_parts(total, parts)


def down_body(d_branch, slope, *refs):
    chunks = refs[:12]
    d_pre, keep, send, down, up = refs[12:]
    load_chunks(chunks, DOWN_PLACES, down)
    load_chunks(chunks, UP_PLACES, up)
    d_pre[...] = (dot_nn(d_branch[...], down[...]) * slope[...]).astype(BF16)
    split_halves(dot_nn(d_pre[...], up[...]), keep, send)


def grad_body(left, right, *refs):
    parts, total = refs[:9], refs[9]
    total[...] = dot_tn(left[...], right[...]).astype(BF16)
    write_parts(total, parts)


def branch_b_body(act, g0, g1, g2, g3, *refs):
    chunks = refs[:12]
    keep, send, d_gate, full, total = refs[12:]
    load_chunks(chunks, DOWN_PLACES, full)
    total[...] = dot_nt(act[...], full[...])
    split_halves(total, keep, send)
    gate = jnp.zeros((1, 1152), F32)
    for f in range(2):
        for i, block in enumerate((g0, g1, g2, g3)):
            row = 256 * f + 64 * i
            gate = gate + jnp.sum(block[f].astype(F32) * total[row : row + 64, :], axis=0, keepdims=True)
    d_gate[...] = gate


def d_middle_body(keep, near, far, normed, root, g0, g1, branch, mod, d_low, d_mid, sums):
    d_shift = jnp.zeros((1, 1152), F32)
    d_scale = jnp.zeros((1, 1152), F32)
    d_gate = jnp.zeros((1, 1152), F32)
    for f in range(2):
        for i, block in enumerate((g0, g1)):
            rows = slice(128 * f + 64 * i, 128 * f + 64 * i + 64)
            cross = slice(128 * f + 64 * (1 - i), 128 * f + 64 * (1 - i) + 64)
            d_hidden = keep[rows, :] + near[rows, :].astype(F32) + far[cross, :].astype(F32)
            norm = normed[rows, :]
            back = norm_back(d_hidden * (1.0 + mod[4:5, :]), norm, root[rows, 0:1])
            mid = block[f].astype(F32) + back
            d_low[rows, :] = (mod[2:3, :] * mid).astype(BF16)
            if i == 0:
                own = slice(64 * f, 64 * f + 64)
                d_mid[own, :] = mid
                d_shift = d_shift + jnp.sum(d_hidden, axis=0, keepdims=True)
                d_scale = d_scale + jnp.sum(d_hidden * norm, axis=0, keepdims=True)
                d_gate = d_gate + jnp.sum(mid * branch[own, :], axis=0, keepdims=True)
    sums[0:1, :] = d_gate
    sums[1:2, :] = d_shift
    sums[2:3, :] = d_scale


def d_attend_body(mine, theirs, parts, probs, attended, out, d_branch, d_slots, d_others, d_att):
    join_halves(mine, theirs, d_branch)
    d_att[...] = dot_nn(d_branch[...], out[...]).astype(BF16)
    scale = HEAD_DIM ** (-0.5)

    first = lax.axis_index("blk") % 2 == 0
    d_slots[...] = jnp.zeros_like(d_slots)

    def place(rows, m, value):
        e, k = divmod(m, 3)
        low = value.astype(BF16)
        at = 224 * e
        if k == 0:
            d_slots[rows, at : at + 72] = low
        elif k == 2:
            d_slots[rows, at + 112 : at + 184] = low
        else:
            near = jnp.where(first, low[:, 0:36], low[:, 36:72])
            d_slots[rows, at + 72 : at + 108] = near
            d_slots[rows, at + 184 : at + 220] = near
            other = jnp.where(first, low[:, 36:72], low[:, 0:36])
            start = rows.start
            d_others[start : start + 128, 36 * e : 36 * e + 36] = other[128:256]
            d_others[start + 128 : start + 256, 36 * e : 36 * e + 36] = other[0:128]

    for f in range(2):
        rows = slice(256 * f, 256 * f + 256)
        for h in range(4):
            d_out = d_att[rows, 72 * h : 72 * h + 72]
            delta = jnp.sum(d_out.astype(F32) * attended[h, rows, :], axis=-1, keepdims=True)
            prob = probs[4 * f + h]
            d_prob = dot_nt(d_out, parts[8 + h, rows, :])
            d_score = (prob * (d_prob - delta)).astype(BF16)
            place(rows, h, dot_nn(d_score, parts[4 + h, rows, :]) * scale)
            place(rows, 4 + h, dot_tn(d_score, parts[h, rows, :]) * scale)
            place(rows, 8 + h, dot_tn(prob.astype(BF16), d_out))


def grad_first_body(d_mine, d_others, hidden, d_branch, low, *refs):
    outs, d_slots, total, below = refs[:9], refs[9], refs[10], refs[11]
    first = lax.axis_index("blk") % 2 == 0
    d_slots[...] = d_mine[...]
    for e in range(4):
        other = d_others[:, 36 * e : 36 * e + 36]
        for odd in range(2):
            at = 224 * e + 112 * odd + 72
            mine = d_mine[:, at : at + 36]
            d_slots[:, at : at + 36] = jnp.where(first == (odd == 0), mine, other)
    total[...] = dot_tn(d_slots[...], hidden[...]).astype(BF16)
    below[...] = dot_tn(d_branch[...], low[...]).astype(BF16)
    for k in range(8):
        at = pl.multiple_of(member_at(NEAR_FIRST[k]) * 112, 112)
        if k < 7:
            outs[k][0:112, :] = total[pl.ds(at, 112), :]
            tail, row = outs[k], 112
        else:
            outs[7][...] = total[pl.ds(at, 80), :]
            outs[8][0:32, :] = total[pl.ds(at + 80, 32), :]
            tail, row = outs[8], 32
        at = pl.multiple_of(member_at(NEAR_FIRST[k]) * 144, 144)
        for q in range(3):
            tail[row : row + 48, 288 * q : 288 * q + 288] = below[pl.ds(at + 48 * q, 48), :]
        tail[row : row + 48, 864:1152] = jnp.zeros((48, 288), BF16)


def d_hidden_a_body(d_slots, t0, t1, t2, t3, sums_b, d_gate_b, *refs):
    chunks = refs[:9]
    keep, send = refs[9:11]
    mods = refs[11:19]
    full, total, flat, d_mod = refs[19:]
    load_chunks(chunks, FIRST_PLACES, full, 0, 112)
    total[...] = dot_nn(d_slots[...], full[...])
    split_halves(total, keep, send)
    d_shift = jnp.zeros((1, 1152), F32)
    d_scale = jnp.zeros((1, 1152), F32)
    for f in range(2):
        for i, block in enumerate((t0, t1, t2, t3)):
            row = 256 * f + 64 * i
            norm, _ = norm_rows(block[f].astype(F32))
            part = total[row : row + 64, :]
            d_shift = d_shift + jnp.sum(part, axis=0, keepdims=True)
            d_scale = d_scale + jnp.sum(part * norm, axis=0, keepdims=True)
    d_mod[0:1, :] = d_shift
    d_mod[1:2, :] = d_scale
    d_mod[2:5, :] = sums_b[0:3, :]
    d_mod[5:6, :] = d_gate_b[...]
    for m in range(24):
        d, j = divmod(m, 3)
        flat[d : d + 1, 288 * j : 288 * j + 288] = d_mod[m // 4 : m // 4 + 1, 288 * (m % 4) : 288 * (m % 4) + 288]
    mine = lax.broadcasted_iota(jnp.int32, (8, 864), 0) == lax.axis_index("dp")
    for k, out in enumerate(mods):
        row = flat[pl.ds(member_at(NEAR_FIRST[k]), 1), :]
        out[...] = jnp.zeros((8, 1152), BF16)
        out[:, 0:864] = jnp.where(mine, row, 0.0).astype(BF16)


def own_half_body(keep, near, own, cross):
    for f in range(2):
        for i, block in enumerate((own, cross)):
            rows = slice(128 * f + 64 * i, 128 * f + 64 * i + 64)
            part = keep[rows, :] + near[rows, :].astype(F32)
            block[64 * f : 64 * f + 64, :] = part.astype(block.dtype)


def output_body(own, far, middle, mod, output):
    for f in range(2):
        rows = slice(64 * f, 64 * f + 64)
        output[f] = middle[rows, :] + mod[5:6, :] * (own[rows, :] + far[rows, :].astype(F32))


def grad_tokens_body(own, far, t0, d_mid, mod, grad):
    for f in range(2):
        rows = slice(64 * f, 64 * f + 64)
        norm, inv = norm_rows(t0[f].astype(F32))
        d_hidden = own[rows, :] + far[rows, :].astype(F32)
        grad[f] = d_mid[rows, :] + norm_back(d_hidden * (1.0 + mod[1:2, :]), norm, inv)


def cut_updown_body(u0, u1, u2, d0, d1, d2, here, near, cross, held):
    blk = lax.axis_index("blk")
    up = u0[...].astype(F32) + u1[0:144, :].astype(F32) + u2[0:144, :].astype(F32)
    down = d0[...].astype(F32) + d1[144:288, :].astype(F32) + d2[144:288, :].astype(F32)
    for t in range(4):
        held[t, :, 0:288] = up[:, 288 * t : 288 * t + 288].astype(BF16)
        held[t, :, 288:576] = down[:, 288 * t : 288 * t + 288].astype(BF16)
        held[t, :, 576:640] = jnp.zeros((144, 64), BF16)
    here[...] = held[blk]
    near[...] = held[blk ^ 1]
    cross[0:144, :] = held[blk ^ 2]
    cross[144:288, :] = held[blk ^ 3]


def final_updown_body(here, far, near, up, down, held):
    blk = lax.axis_index("blk")
    held[blk] = here[...]
    held[blk ^ 1] = near[0:144, :]
    held[blk ^ 2] = far[0:144, :]
    held[blk ^ 3] = near[144:288, :]
    for s in range(4):
        up[:, 144 * s : 144 * s + 144] = held[s, :, 0:288].astype(F32).T
        for part in range(2):
            at = 576 * part + 144 * s
            down[:, at : at + 144] = held[s, :, 288 + 144 * part : 432 + 144 * part].astype(F32)


def cut_heads_body(s0, s1, s2, m0, *refs):
    pieces, held = refs[:4], refs[4]
    blk = lax.axis_index("blk")
    total = s0[...].astype(F32) + s1[0:160, :].astype(F32) + s2[0:160, :].astype(F32)
    mods = m0[...].astype(F32) + s1[160:168, :].astype(F32) + s2[160:168, :].astype(F32)
    for t in range(4):
        held[t, :, 0:288] = jnp.zeros((144, 288), BF16)
        held[t, 0:108, 0:288] = total[0:108, 288 * t : 288 * t + 288].astype(BF16)
        held[t, 112:120, 0:216] = mods[:, 216 * t : 216 * t + 216].astype(BF16)
        for q in range(3):
            at = 288 * q + 72 * t
            held[t, 48 * q : 48 * q + 48, 288:360] = total[112:160, at : at + 72].astype(BF16)
        held[t, :, 360:384] = jnp.zeros((144, 24), BF16)
    for r in range(4):
        pieces[r][...] = held[blk ^ r]


def final_heads_body(timestep, p0, p1, p2, p3, qkv, out, table, held, placed, pieces, wide):
    blk = lax.axis_index("blk")
    mods = p0[112:120, 0:216].astype(F32) + p1[112:120, 0:216].astype(F32)
    mods = (mods + p2[112:120, 0:216].astype(F32) + p3[112:120, 0:216].astype(F32)).T
    wide[...] = jnp.zeros_like(wide)
    lane = lax.broadcasted_iota(jnp.int32, (216, 128), 1)
    for c in range(8):
        step = timestep[c]
        lanes = pl.ds(pl.multiple_of((step // 128) * 128, 128), 128)
        wide[:, lanes] = wide[:, lanes] + jnp.where(lane == step % 128, mods[:, c : c + 1], 0.0)
    table[...] = wide[:, 0 : table.shape[1]]
    for r, piece in enumerate((p0, p1, p2, p3)):
        pieces[blk ^ r] = piece[...]
    for sender in range(4):
        alone, shared = columns_of(sender)
        half = 36 * (sender & 1)
        placed[alone] = pieces[sender, 0:72, 0:288].astype(F32)
        placed[shared, half : half + 36, :] = pieces[sender, 72:108, 0:288].astype(F32)
        held[kind_of(sender)] = pieces[sender, :, 288:360].astype(F32)
    for i in range(6):
        qkv[:, 72 * i : 72 * i + 72] = placed[i].T
    for s in range(4):
        out[:, 72 * s : 72 * s + 72] = held[s]


def vmem(shape, kind=BF16):
    return (shape, kind)


def local_kernels(tokens, timestep, mod_table, w_qkv, w_out, w_up, w_down, cotangent):
    nd, nb = 8, 4
    ring = Ring(nd, lax.axis_index("dp"))
    group = Group(nb, lax.axis_index("blk"))
    width = tokens.shape[3]
    own_tokens = tokens[0]
    own_cot = cotangent[0]
    full_low = ((512, 1152), BF16)
    chunk_low = ((144, 1152), BF16)
    part_low = [chunk_low] * 7 + [((80, 1152), BF16), ((64, 1152), BF16)]
    half_low = ((256, 1152), BF16)
    half_wide = ((256, 1152), F32)
    own_wide = ((128, 1152), F32)

    def send_out(pieces):
        return [pieces[0]] + [group.swap(pieces[r], r) for r in (1, 2, 3)]

    def add_low(keep, near):
        return (keep + near.astype(F32)).astype(BF16)

    def own_half(keep, near, name):
        return run_kernel(own_half_body, [own_wide, ((128, 1152), BF16)], keep, near, name=name)

    picker = (timestep[:, None] == jnp.arange(mod_table.shape[0], dtype=jnp.int32)[None, :]).astype(BF16)
    table_cols = dot_nn(picker, mod_table).astype(BF16)
    heads_cut = run_kernel(
        pack_heads_body,
        [((144, 384), BF16)] * 4,
        w_qkv, w_out.T, table_cols,
        scratch=[vmem((2, 6, 36, 288)), vmem((4, 144, 72))],
        name="pack_heads",
    )
    heads_got = send_out(heads_cut)
    (first_own,) = run_kernel(
        join_heads_body,
        [((160, 1152), BF16)],
        *heads_got,
        scratch=[vmem((4, 144, 384)), vmem((8, 864), F32)],
        name="join_heads",
    )
    updown_cut = run_kernel(
        pack_updown_body,
        [((144, 640), BF16)] * 4,
        *after((w_up, w_down.T), heads_got[2]),
        scratch=[vmem((4, 144, 288)), vmem((4, 144, 288))],
        name="pack_updown",
    )
    updown_got = send_out(updown_cut)
    fore1, rear1, _ = step(ring, first_own, first_own)
    fore2, rear2, held = step(ring, fore1, rear1, own_tokens, *updown_got)
    far_t = group.swap(held[0], 2)
    up_own, down_own = run_kernel(
        join_updown_body, [chunk_low] * 2, *held[1:], scratch=[vmem((4, 144, 640))], name="join_updown"
    )
    fore3, rear3, held = step(ring, fore2, rear2, up_own, down_own, far_t, own_tokens, own_cot)
    up_own, down_own, far_t, own_t, own_c = held
    token_blocks = [own_tokens, far_t, group.swap(own_t, 1), group.swap(far_t, 1)]
    far_c = group.swap(own_c, 2)
    fore4, rear4, held = step(
        ring, stack(fore3[:80], up_own), stack(rear3[80:], up_own), far_c, own_cot, *token_blocks
    )
    far_c, own_c, *token_blocks = held
    cot_blocks = [own_cot, far_c, group.swap(own_c, 1), group.swap(far_c, 1)]
    first_got = [first_own, fore1, rear1, fore2, rear2, fore3, rear3, fore4, rear4]
    fore5, rear5, held = step(
        ring, stack(fore4[80:], down_own), stack(rear4[80:], down_own), *cot_blocks, *token_blocks, *first_got
    )
    cot_blocks, token_blocks, first_got = held[:4], held[4:8], held[8:]
    other_halves = stack(*(chunk[72:112] for chunk in first_got[:7]), first_got[7][72:80], first_got[8][:32])
    hidden_a, parts, probs, attended, low, out_full, mod, keep_a, send_a, d_branch_b = run_kernel(
        attend_body,
        [
            full_low,
            ((12, 512, 72), BF16),
            ((8, 256, 256), F32),
            ((4, 512, 72), F32),
            ((512, 288), BF16),
            ((1152, 288), BF16),
            ((8, 1152), F32),
            half_wide,
            half_low,
            full_low,
        ],
        *token_blocks, group.swap(other_halves, 1), *cot_blocks, *first_got,
        scratch=[vmem((1280, 1152)), vmem((512, 1280)), vmem((384, 1152))],
        flops=4 * 10**9,
        name="attend",
    )
    fore6, rear6, (keep_a, send_a) = step(ring, fore5, rear5, keep_a, send_a)
    near_a = group.swap(send_a, 1)
    far_a = group.swap(add_low(keep_a, near_a), 2)
    fore7, rear7, (keep_a, near_a, far_a) = step(
        ring, stack(fore6[:80], fore6[144:]), rear6[80:], keep_a, near_a, far_a
    )
    hidden_mine, normed_b, root_b, branch_a, middle = run_kernel(
        middle_body,
        [half_low, half_wide, ((256, 128), F32), own_wide, own_wide],
        keep_a, near_a, far_a, *token_blocks[:2], mod,
        name="middle",
    )
    hidden_theirs = group.swap(hidden_mine, 1)
    fore8, rear8, (hidden_mine, hidden_theirs) = step(ring, fore7[80:160], rear7[144:], hidden_mine, hidden_theirs)
    up_got = [up_own, down_own, fore4, rear4, fore5, rear5, fore6, rear6, fore7, rear7]
    down_got = [*up_got, fore8, rear8]
    hidden_b, act, slope, *grad_down = run_kernel(
        up_body,
        [full_low, full_low, ((512, 1152), F32)] + part_low,
        hidden_mine, hidden_theirs, d_branch_b, *up_got,
        scratch=[vmem((1152, 1152)), vmem((1152, 1152))],
        flops=4 * 10**9,
        name="up",
    )
    fore1, rear1, held = step(ring, *grad_down[7:], d_branch_b, slope, *down_got)
    d_branch_b, slope, down_got = held[0], held[1], held[2:]
    d_pre, keep_d, send_d = run_kernel(
        down_body,
        [full_low, half_wide, half_low],
        d_branch_b, slope, *down_got,
        scratch=[vmem((1152, 1152)), vmem((1152, 1152))],
        flops=4 * 10**9,
        name="down",
    )
    near_d = group.swap(send_d, 1)
    low_d = add_low(keep_d, near_d)
    grad_up = run_kernel(
        grad_body,
        part_low,
        d_pre, hidden_b,
        scratch=[vmem((1152, 1152))],
        flops=2 * 10**9,
        name="grad_up",
    )
    fore2, rear2, (keep_d, near_d, low_d, act) = step(
        ring,
        stack(grad_up[7], sum_low(grad_down[6][:80], fore1), grad_down[6][80:]),
        stack(grad_up[8], grad_down[5][:80], sum_low(grad_down[5][80:], rear1)),
        keep_d, near_d, low_d, act,
    )
    far_d = group.swap(low_d, 2)
    keep_b, send_b, d_gate_b = run_kernel(
        branch_b_body,
        [half_wide, half_low, ((1, 1152), F32)],
        act, *cot_blocks, *down_got,
        scratch=[vmem((1152, 1152)), vmem((512, 1152), F32)],
        flops=2 * 10**9,
        name="branch_b",
    )
    near_b = group.swap(send_b, 1)
    fore3, rear3, (keep_d, near_d, far_d, keep_b, near_b) = step(
        ring,
        stack(sum_low(grad_up[6][:80], fore2[:80]), grad_up[6][80:], sum_low(grad_down[4], fore2[80:])),
        stack(grad_up[5][:80], sum_low(grad_up[5][80:], rear2[:64]), sum_low(grad_down[3], rear2[64:])),
        keep_d, near_d, far_d, keep_b, near_b,
    )
    d_low, d_mid, sums_b = run_kernel(
        d_middle_body,
        [half_low, own_wide, ((3, 1152), F32)],
        keep_d, near_d, far_d, normed_b, root_b, *cot_blocks[:2], branch_a, mod,
        name="d_middle",
    )
    d_branch_a, d_mine, d_others = run_kernel(
        d_attend_body,
        [full_low, ((512, 896), BF16), ((512, 144), BF16)],
        d_low, group.swap(d_low, 1), parts, probs, attended, out_full,
        scratch=[vmem((512, 288))],
        flops=3 * 10**9,
        name="d_attend",
    )
    d_others = group.swap(d_others, 1)
    fore4, rear4, held = step(
        ring,
        stack(sum_low(grad_up[4], fore3[:144]), sum_low(grad_down[2], fore3[144:])),
        stack(sum_low(grad_up[3], rear3[:144]), sum_low(grad_down[1], rear3[144:])),
        keep_b, near_b, d_mine, d_others, d_branch_a,
    )
    keep_b, near_b, d_mine, d_others, d_branch_a = held
    own_b, cross_b = own_half(keep_b, near_b, "own_b")
    far_b = group.swap(cross_b, 2)
    *grad_first, d_slots = run_kernel(
        grad_first_body,
        [((160, 1152), BF16)] * 7 + [((80, 1152), BF16)] * 2 + [((512, 896), BF16)],
        d_mine, d_others, hidden_a, d_branch_a, low,
        scratch=[vmem((896, 1152)), vmem((1152, 288))],
        flops=2 * 10**9,
        name="grad_first",
    )
    keep_h, send_h, *mods = run_kernel(
        d_hidden_a_body,
        [half_wide, half_low] + [((8, 1152), BF16)] * 8,
        d_slots, *token_blocks, sums_b, d_gate_b, *first_got,
        scratch=[
            vmem((896, 1152)),
            vmem((512, 1152), F32),
            vmem((8, 864), F32),
            vmem((6, 1152), F32),
        ],
        flops=2 * 10**9,
        name="d_hidden_a",
    )
    fore5, rear5, (keep_h, send_h, own_b, far_b) = step(
        ring,
        stack(sum_low(grad_up[2], fore4[:144]), grad_first[7], mods[7]),
        stack(sum_low(grad_up[1], rear4[:144]), grad_first[8]),
        keep_h, send_h, own_b, far_b,
    )
    near_h = group.swap(send_h, 1)
    fore6, rear6, held = step(
        ring,
        stack(sum_low(grad_first[6][:80], fore5[144:224]), grad_first[6][80:], sum_low(mods[6], fore5[224:])),
        stack(grad_first[5][:80], sum_low(grad_first[5][80:], rear5[144:]), mods[5]),
        keep_h, near_h, fore4, rear4, fore5, rear5,
    )
    keep_h, near_h, *up_down = held
    own_h, cross_h = own_half(keep_h, near_h, "own_h")
    far_h = group.swap(cross_h, 2)
    here, near_u, cross_u = run_kernel(
        cut_updown_body,
        [((144, 640), BF16)] * 2 + [((288, 640), BF16)],
        grad_up[0], *up_down[2:], grad_down[0], *up_down[:2],
        scratch=[vmem((4, 144, 640))],
        name="cut_updown",
    )
    fore7, rear7, held = step(
        ring,
        stack(sum_low(grad_first[4], fore6[:160]), sum_low(mods[4], fore6[160:])),
        stack(sum_low(grad_first[3], rear6[:160]), sum_low(mods[3], rear6[160:])),
        here, near_u, cross_u,
    )
    here, near_u, cross_u = held
    far_u = group.swap(cross_u, 2)
    fore8, rear8, held = step(
        ring,
        stack(sum_low(grad_first[2], fore7[:160]), sum_low(mods[2], fore7[160:])),
        stack(sum_low(grad_first[1], rear7[:160]), sum_low(mods[1], rear7[160:])),
        own_h, far_h, own_b, far_b, here, near_u, far_u,
    )
    own_h, far_h, own_b, far_b, here, near_u, far_u = held
    (output,) = run_kernel(
        output_body, [((2, 64, 1152), F32)], own_b, far_b, middle, mod, name="output"
    )
    (grad_tokens,) = run_kernel(
        grad_tokens_body, [((2, 64, 1152), F32)], own_h, far_h, own_tokens, d_mid, mod, name="grad_tokens"
    )
    final_up, final_down = run_kernel(
        final_updown_body,
        [((288, 576), F32), ((144, 1152), F32)],
        here, far_u, group.swap(stack(near_u, far_u[144:]), 1),
        scratch=[vmem((4, 144, 640))],
        name="final_updown",
    )
    heads_cut = run_kernel(
        cut_heads_body, [((144, 384), BF16)] * 4, grad_first[0], fore8, rear8, mods[0], scratch=[vmem((4, 144, 384))], name="cut_heads"
    )
    final_qkv, final_out, grad_table = run_kernel(
        final_heads_body,
        [((288, 432), F32), ((144, 288), F32), ((216, mod_table.shape[0]), F32)],
        timestep, *send_out(heads_cut),
        scalars=1,
        scratch=[
            vmem((4, 144, 72), F32),
            vmem((6, 72, 288), F32),
            vmem((4, 144, 384)),
            vmem((216, -(-mod_table.shape[0] // 128) * 128), F32),
        ],
        name="final_heads",
    )
    return (output[None], grad_tokens[None], grad_table.T, final_qkv, final_out.T, final_up, final_down.T)


def local(tokens, timestep, mod_table, w_qkv, w_out, w_up, w_down, cotangent):
    sizes = (lax.axis_size("dp"), lax.axis_size("blk"), tokens.shape, w_qkv.shape, w_up.shape, w_down.shape)
    known = (8, 4, (1, 2, 64, 1152), (288, 432), (288, 576), (1152, 144))
    chosen = local_kernels if sizes == known else local_plain
    return chosen(tokens, timestep, mod_table, w_qkv, w_out, w_up, w_down, cotangent)


def solution(mesh):
    in_specs = (
        P("dp", None, "blk", None),
        P(),
        P(None, ("dp", "blk")),
        P("blk", "dp"),
        P("blk", "dp"),
        P("blk", "dp"),
        P("blk", "dp"),
        P("dp", None, "blk", None),
    )
    out_specs = (
        P("dp", None, "blk", None),
        P("dp", None, "blk", None),
        P(None, ("dp", "blk")),
        P("blk", "dp"),
        P("blk", "dp"),
        P("blk", "dp"),
        P("blk", "dp"),
    )
    return jax.shard_map(local, mesh=mesh, in_specs=in_specs, out_specs=out_specs, check_vma=False)
```

```python
import math
from functools import partial

import jax
import jax.numpy as jnp
from jax import lax
from jax.experimental import pallas as pl
from jax.experimental.pallas import tpu as pltpu
from jax.sharding import PartitionSpec as P

HEADS = 16
HEAD_DIM = 72
EPS = 1e-06
HIGHEST = lax.Precision.HIGHEST
BF16 = jnp.bfloat16
F32 = jnp.float32


def norm_rows(values):
    center = values - jnp.mean(values, axis=-1, keepdims=True)
    spread = jnp.mean(center * center, axis=-1, keepdims=True)
    root_inv = lax.rsqrt(spread + EPS)
    return (center * root_inv, root_inv)


def norm_back(d_normed, normed, root_inv):
    mean_one = jnp.mean(d_normed, axis=-1, keepdims=True)
    mean_two = jnp.mean(d_normed * normed, axis=-1, keepdims=True)
    return root_inv * (d_normed - mean_one - normed * mean_two)


def dot_nn(left, right):
    return jnp.dot(left, right, preferred_element_type=F32)


def dot_tn(left, right):
    return lax.dot_general(left, right, (((0,), (0,)), ((), ())), preferred_element_type=F32)


def dot_nt(left, right):
    return lax.dot_general(left, right, (((1,), (1,)), ((), ())), preferred_element_type=F32)


class Ring:
    def __init__(self, size, index):
        self.size = size
        self.order = list(range(0, size, 2)) + list(range(size - 1, 0, -2))
        place = [0] * size
        for spot, member in enumerate(self.order):
            place[member] = spot
        self.spot = jnp.array(place, jnp.int32)[index]
        self.table = jnp.array(self.order, jnp.int32)
        self.ahead = [(self.order[i], self.order[(i + 1) % size]) for i in range(size)]
        self.back = [(right, left) for left, right in self.ahead]

    def member(self, offset):
        return self.table[(self.spot + offset) % self.size]

    def gather(self, chunk):
        half = self.size // 2
        cut = chunk.shape[0] // 2
        out = jnp.zeros((self.size,) + chunk.shape, chunk.dtype)

        def put(out, piece, offset, row=0):
            return lax.dynamic_update_slice(out, piece[None], (self.member(offset), row, 0))

        out = put(out, chunk, 0)
        fore = rear = chunk
        for step in range(1, half):
            fore = lax.ppermute(fore, "dp", self.ahead)
            rear = lax.ppermute(rear, "dp", self.back)
            out = put(put(out, fore, -step), rear, step)
        fore = lax.ppermute(fore[:cut], "dp", self.ahead)
        rear = lax.ppermute(rear[cut:], "dp", self.back)
        return put(put(out, fore, half), rear, half, cut)

    def scatter(self, parts):
        half = self.size // 2
        cut = parts.shape[1] // 2

        def own(offset):
            return lax.dynamic_index_in_dim(parts, self.member(offset), 0, keepdims=False)

        far = own(half)
        fore = lax.ppermute(far[:cut], "dp", self.ahead)
        rear = lax.ppermute(far[cut:], "dp", self.back)
        for step in range(half - 1, 0, -1):
            mine_fore = own(step).astype(F32)
            mine_rear = own(-step).astype(F32)
            if step == half - 1:
                fore = jnp.concatenate([mine_fore[:cut] + fore.astype(F32), mine_fore[cut:]], axis=0)
                rear = jnp.concatenate([mine_rear[:cut], mine_rear[cut:] + rear.astype(F32)], axis=0)
            else:
                fore = mine_fore + fore.astype(F32)
                rear = mine_rear + rear.astype(F32)
            fore = lax.ppermute(fore.astype(BF16), "dp", self.ahead)
            rear = lax.ppermute(rear.astype(BF16), "dp", self.back)
        return own(0).astype(F32) + fore.astype(F32) + rear.astype(F32)


class Group:
    def __init__(self, size, index):
        self.size = size
        self.index = index
        self.bits = []
        bit = size // 2
        while bit:
            self.bits.append(bit)
            bit //= 2

    def swap(self, values, bit):
        return lax.ppermute(values, "blk", [(i, i ^ bit) for i in range(self.size)])

    def exchange(self, pieces):
        if self.size > 4:
            return lax.all_to_all(pieces, "blk", 0, 0, tiled=True)
        got = []
        for r in range(self.size):
            piece = lax.dynamic_index_in_dim(pieces, self.index ^ r, 0, keepdims=False)
            got.append(self.swap(piece, r) if r else piece)
        bit = 1
        while bit < self.size:
            odd = (self.index & bit) != 0
            got = [jnp.where(odd, got[r ^ bit], got[r]) for r in range(self.size)]
            bit *= 2
        return jnp.stack(got)

    def gather(self, block, bits=None):
        for bit in self.bits if bits is None else bits:
            block = jnp.concatenate([block, self.swap(block, bit)], axis=0)
        return block

    def scatter(self, parts, share):
        for bit in reversed(self.bits[1:]):
            half = parts.shape[0] // 2
            parts = parts[:half] + self.swap(parts[half:].astype(BF16), bit).astype(F32)
        top = self.bits[0]
        if share:
            return parts + self.swap(parts.astype(BF16), top)[::-1].astype(F32)
        return parts[:1] + self.swap(parts[1:].astype(BF16), top).astype(F32)


def local_plain(tokens, timestep, mod_table, w_qkv, w_out, w_up, w_down, cotangent):
    frames, patches, width = tokens.shape[1:]
    nd = lax.axis_size("dp")
    nb = lax.axis_size("blk")
    dp = lax.axis_index("dp")
    blk = lax.axis_index("blk")
    ring = Ring(nd, dp)
    group = Group(nb, blk)
    rows = nb * frames * patches
    scale = HEAD_DIM ** (-0.5)
    heads = HEADS // nb
    deep = width // nb
    ff = w_down.shape[0]
    hidden = w_up.shape[1]
    out_cols = w_out.shape[1]

    columns = w_qkv.shape[1] // HEAD_DIM
    slots = -(-columns // nb)
    offset = (columns * dp) % nb
    qkv_t = w_qkv.T.reshape(columns, HEAD_DIM, deep)
    qkv_pos = jnp.zeros((2 * slots * nb, HEAD_DIM, deep), BF16)
    qkv_pos = lax.dynamic_update_slice(qkv_pos, qkv_t, (offset, 0, 0))
    qkv_pos = qkv_pos[: slots * nb] + qkv_pos[slots * nb :]
    qkv_send = qkv_pos.reshape(slots, nb, HEAD_DIM, deep).transpose(1, 0, 2, 3)
    qkv_send = qkv_send.reshape(nb, slots * HEAD_DIM, deep)
    spread = heads // nb
    if spread:
        out_send = w_out.T.reshape(out_cols, spread, nb, HEAD_DIM).transpose(2, 0, 1, 3)
        out_send = out_send.reshape(nb, out_cols, spread * HEAD_DIM)
    up_send = w_up.T.reshape(nb, hidden // nb, deep)
    many = ff // hidden
    down_send = w_down.T.reshape(out_cols, many, nb, hidden // nb).transpose(2, 0, 1, 3)
    down_send = down_send.reshape(nb, out_cols, many * hidden // nb)
    first = group.exchange(jnp.concatenate([qkv_send, out_send], axis=2) if spread else qkv_send)
    up_got = group.exchange(up_send)
    down_got = group.exchange(down_send)
    qkv_own = first[:, :, :deep].transpose(1, 0, 2).reshape(slots * HEAD_DIM, width)
    out_own = first[:, :, deep:].transpose(1, 0, 2).reshape(out_cols, heads * HEAD_DIM) if spread else w_out.T
    up_own = up_got.transpose(1, 0, 2).reshape(hidden // nb, width)
    down_own = down_got.transpose(1, 0, 2).reshape(out_cols, nd * hidden // nb)

    token_all = group.gather(tokens)
    cot_all = group.gather(cotangent)

    picker = (timestep[:, None] == jnp.arange(mod_table.shape[0], dtype=jnp.int32)[None, :]).astype(BF16)
    table_cols = dot_nn(picker, mod_table).astype(BF16)
    piece = table_cols.shape[1]
    mods_send = jnp.broadcast_to(table_cols[:, None, :], (nd, nb, piece)).reshape(nd * nb, piece)
    mod_row = lax.all_to_all(mods_send, ("dp", "blk"), 0, 0, tiled=True).reshape(6, width).astype(F32)
    shift_a, scale_a, gate_a, shift_b, scale_b, gate_b = (mod_row[i] for i in range(6))

    first_all = ring.gather(jnp.concatenate([qkv_own, out_own], axis=1))
    up_full = ring.gather(up_own).reshape(ff, width)
    down_full = ring.gather(down_own).reshape(width, ff)
    out_full = first_all[:, :, width:].reshape(width, heads * HEAD_DIM)
    wanted = blk + nb * jnp.arange(3 * heads, dtype=jnp.int32)
    holder = wanted // columns
    place = ((wanted - columns * holder + (columns * holder) % nb) % (slots * nb)) // nb
    slot_of = holder * slots + place
    qkv_slots = first_all[:, :, :width].reshape(nd * slots, HEAD_DIM, width)
    qkv_full = jnp.take(qkv_slots, slot_of, axis=0).reshape(3 * heads * HEAD_DIM, width)

    inputs = token_all.reshape(rows, width).astype(F32)
    normed_a, root_a = norm_rows(inputs)
    hidden_a = (normed_a * (1.0 + scale_a) + shift_a).astype(BF16)
    projected = dot_nt(hidden_a, qkv_full).astype(BF16)

    def by_head(values, parts):
        split = values.reshape(nb, frames, patches, parts, heads, HEAD_DIM)
        split = split.transpose(3, 1, 4, 0, 2, 5)
        return split.reshape(parts, frames, heads, nb * patches, HEAD_DIM)

    def by_row(values):
        split = values.reshape(-1, frames, heads, nb, patches, HEAD_DIM)
        return split.transpose(3, 1, 4, 0, 2, 5).reshape(rows, -1)

    query, keys, values = by_head(projected, 3)
    scores = jnp.einsum("fhqe,fhke->fhqk", query, keys, preferred_element_type=F32) * scale
    top = jnp.max(scores, axis=-1, keepdims=True)
    weights = jnp.exp(scores - top)
    probs = weights / jnp.sum(weights, axis=-1, keepdims=True)
    probs_low = probs.astype(BF16)
    attended = jnp.einsum("fhqk,fhke->fhqe", probs_low, values, preferred_element_type=F32)
    attn_low = by_row(attended).astype(BF16)
    share = 2 * frames * patches
    own = frames * patches

    def blocks(partial_sum):
        return partial_sum.reshape(nb, own, width)

    branch_a = group.scatter(blocks(dot_nt(attn_low, out_full)), True).reshape(share, width)
    middle = inputs[:share] + gate_a * branch_a
    normed_b, root_b = norm_rows(middle)
    hidden_low = (normed_b * (1.0 + scale_b) + shift_b).astype(BF16)
    hidden_b = group.gather(hidden_low.reshape(2, own, width), group.bits[1:]).reshape(rows, width)
    pre_act = dot_nt(hidden_b, up_full)
    activated, gelu_back = jax.vjp(partial(jax.nn.gelu, approximate=True), pre_act)
    act_low = activated.astype(BF16)
    grad_in = cot_all.reshape(rows, width).astype(F32)
    d_branch_b = (gate_b * grad_in).astype(BF16)
    grad_down = dot_tn(d_branch_b, act_low).astype(BF16)
    down_sum = ring.scatter(grad_down.reshape(nd, out_cols, ff))
    d_act = dot_nn(d_branch_b, down_full)
    d_pre = gelu_back(d_act)[0].astype(BF16)
    grad_up = dot_tn(d_pre, hidden_b).astype(BF16)
    up_sum = ring.scatter(grad_up.reshape(nd, hidden // nb, width))
    d_hidden_b = group.scatter(blocks(dot_nn(d_pre, up_full)), True).reshape(share, width)
    branch_b = group.scatter(blocks(dot_nt(act_low, down_full)), False).reshape(own, width)
    output = (middle[:own] + gate_b * branch_b).reshape(tokens.shape)
    d_gate_b = jnp.sum(grad_in[:own] * branch_b, axis=0)
    d_shift_b = jnp.sum(d_hidden_b[:own], axis=0)
    d_scale_b = jnp.sum(d_hidden_b[:own] * normed_b[:own], axis=0)
    d_middle = grad_in[:share] + norm_back(d_hidden_b * (1.0 + scale_b), normed_b, root_b)
    d_gate_a = jnp.sum(d_middle[:own] * branch_a[:own], axis=0)
    d_branch_a = (gate_a * d_middle).astype(BF16).reshape(2, own, width)
    d_branch_a = group.gather(d_branch_a, group.bits[1:]).reshape(rows, width)
    grad_out = dot_tn(d_branch_a, attn_low).astype(BF16)
    d_attended = dot_nn(d_branch_a, out_full).astype(BF16)
    d_att = by_head(d_attended, 1)[0]
    delta = jnp.sum(d_att.astype(F32) * attended, axis=-1, keepdims=True)
    d_probs = jnp.einsum("fhqe,fhke->fhqk", d_att, values, preferred_element_type=F32)
    d_scores = (probs * (d_probs - delta)).astype(BF16)
    d_query = jnp.einsum("fhqk,fhke->fhqe", d_scores, keys, preferred_element_type=F32) * scale
    d_key = jnp.einsum("fhqk,fhqe->fhke", d_scores, query, preferred_element_type=F32) * scale
    d_value = jnp.einsum("fhqk,fhqe->fhke", probs_low, d_att, preferred_element_type=F32)
    d_projected = by_row(jnp.stack([d_query, d_key, d_value]).astype(BF16))
    grad_qkv = dot_tn(d_projected, hidden_a).astype(BF16).reshape(3 * heads, HEAD_DIM, width)
    grad_slots = jnp.zeros((nd * slots, HEAD_DIM, width), BF16).at[slot_of].set(grad_qkv)
    grad_first = jnp.concatenate(
        [
            grad_slots.reshape(nd, slots * HEAD_DIM, width),
            grad_out.reshape(nd, out_cols, heads * HEAD_DIM),
        ],
        axis=2,
    )
    first_sum = ring.scatter(grad_first)
    d_hidden_a = group.scatter(blocks(dot_nn(d_projected, qkv_full)), False).reshape(own, width)
    d_shift_a = jnp.sum(d_hidden_a, axis=0)
    d_scale_a = jnp.sum(d_hidden_a * normed_a[:own], axis=0)
    d_normed = norm_back(d_hidden_a * (1.0 + scale_a), normed_a[:own], root_a[:own])
    grad_tokens = (d_middle[:own] + d_normed).reshape(tokens.shape)

    d_mod = jnp.concatenate([d_shift_a, d_scale_a, d_gate_a, d_shift_b, d_scale_b, d_gate_b])
    mod_got = lax.all_to_all(d_mod.reshape(nd * nb, piece), ("dp", "blk"), 0, 0, tiled=True)
    mod_sums = jnp.sum(mod_got.reshape(nd, nb, piece), axis=1)
    grad_table = lax.dot_general(
        picker.astype(F32),
        mod_sums,
        (((0,), (0,)), ((), ())),
        precision=HIGHEST,
        preferred_element_type=F32,
    )

    up_back = group.exchange(up_sum.astype(BF16).reshape(hidden // nb, nb, deep).transpose(1, 0, 2))
    final_up = up_back.reshape(hidden, deep).T.astype(F32)
    down_back = down_sum.astype(BF16).reshape(out_cols, nb, many, hidden // nb).transpose(1, 0, 2, 3)
    down_back = group.exchange(down_back.reshape(nb, out_cols, many * hidden // nb))
    down_back = down_back.reshape(nb, out_cols, many, hidden // nb).transpose(2, 0, 3, 1)
    final_down = down_back.reshape(ff, out_cols).astype(F32)
    first_low = first_sum.astype(BF16)
    qkv_back = first_low[:, :width].reshape(slots * HEAD_DIM, nb, deep).transpose(1, 0, 2)
    out_back = first_low[:, width:]
    if spread:
        out_back = out_back.reshape(out_cols, nb, spread * HEAD_DIM).transpose(1, 0, 2)
        back = group.exchange(jnp.concatenate([qkv_back, out_back], axis=2))
        out_back = back[:, :, deep:].reshape(nb, out_cols, spread, HEAD_DIM).transpose(2, 0, 3, 1)
        final_out = out_back.reshape(deep, out_cols).astype(F32)
    else:
        back = group.exchange(qkv_back)
        final_out = out_back.T.astype(F32)
    qkv_back = back[:, :, :deep].reshape(nb, slots, HEAD_DIM, deep).transpose(1, 0, 2, 3)
    qkv_back = qkv_back.reshape(slots * nb, HEAD_DIM, deep)
    qkv_back = lax.dynamic_slice(
        jnp.concatenate([qkv_back, qkv_back], axis=0), (offset, 0, 0), (columns, HEAD_DIM, deep)
    )
    final_qkv = qkv_back.reshape(columns * HEAD_DIM, deep).T.astype(F32)
    return (output, grad_tokens, grad_table, final_qkv, final_out, final_up, final_down)


GELU_IN = 0.7978845608028654
GELU_CUBE = 0.044715


def padded_bytes(shape, kind):
    *lead, rows, lanes = shape
    return math.prod(lead) * -(-rows // 16) * 16 * -(-lanes // 128) * 128 * jnp.dtype(kind).itemsize


def run_kernel(body, outs, *args, scalars=0, scratch=(), spare=8, flops=0, name=None):
    held = list(outs) + list(scratch) + [(a.shape, a.dtype) for a in args[scalars:]]
    limit = sum(padded_bytes(*h) for h in held) + (spare << 20)
    moved = sum(padded_bytes(*o) for o in outs) + sum(padded_bytes(a.shape, a.dtype) for a in args[scalars:])
    return pl.pallas_call(
        body,
        out_shape=[jax.ShapeDtypeStruct(shape, t) for shape, t in outs],
        in_specs=[pl.BlockSpec(memory_space=pltpu.SMEM if i < scalars else pltpu.VMEM) for i in range(len(args))],
        out_specs=[pl.BlockSpec(memory_space=pltpu.VMEM) for _ in outs],
        scratch_shapes=[pltpu.VMEM(*h) for h in scratch],
        compiler_params=pltpu.CompilerParams(vmem_limit_bytes=limit),
        cost_estimate=pl.CostEstimate(flops=flops, bytes_accessed=moved, transcendentals=0),
        name=name,
    )(*args)


def after(value, *others):
    return lax.optimization_barrier((value, *others))[0]


def step(ring, fore, rear, *carry):
    (fore, rear), carry = lax.optimization_barrier(((fore, rear), carry))
    return lax.ppermute(fore, "dp", ring.ahead), lax.ppermute(rear, "dp", ring.back), carry


def sum_low(mine, got):
    return (mine.astype(F32) + got.astype(F32)).astype(BF16)


def stack(*blocks):
    return jnp.concatenate(blocks, axis=0)


NEAR_FIRST = (0, -1, 1, -2, 2, -3, 3, 4)


def member_at(offset):
    dp = lax.axis_index("dp")
    spot = jnp.where(dp % 2 == 0, dp // 2, 7 - dp // 2)
    at = (spot + offset + 8) % 8
    return jnp.where(at < 4, 2 * at, 15 - 2 * at)


def kind_of(device):
    return (device >> 1) | ((device & 1) << 1)


def columns_of(device):
    odd = lax.axis_index("dp") & 1
    return kind_of(device) + 2 * odd, (device >> 1) + 4 - 4 * odd


def turn(values):
    return values.astype(F32).T.astype(BF16)


def pack_heads_body(qkv, out, mods, *refs):
    heads, held_q, held_o = refs[:4], refs[4], refs[5]
    blk = lax.axis_index("blk")
    for i in range(6):
        for half in range(2):
            at = 72 * i + 36 * half
            held_q[half, i] = turn(qkv[:, at : at + 36])
    for t in range(4):
        held_o[t] = out[:, 72 * kind_of(t) : 72 * kind_of(t) + 72]
    for r in range(4):
        t = blk ^ r
        alone, shared = columns_of(t)
        heads[r][...] = jnp.zeros((144, 384), BF16)
        heads[r][0:36, 0:288] = held_q[0, alone]
        heads[r][36:72, 0:288] = held_q[1, alone]
        heads[r][72:108, 0:288] = held_q[t & 1, shared]
        heads[r][112:120, 0:216] = mods[...]
        heads[r][:, 288:360] = held_o[t]


def pack_updown_body(up, down, *refs):
    updown, held_u, held_d = refs[:4], refs[4], refs[5]
    blk = lax.axis_index("blk")
    for t in range(4):
        held_u[t] = turn(up[:, 144 * t : 144 * t + 144])
        for part in range(2):
            at = 576 * part + 144 * t
            held_d[t, :, 144 * part : 144 * part + 144] = down[:, at : at + 144]
    for r in range(4):
        t = blk ^ r
        updown[r][:, 0:288] = held_u[t]
        updown[r][:, 288:576] = held_d[t]
        updown[r][:, 576:640] = jnp.zeros((144, 64), BF16)


def join_heads_body(*refs):
    pieces, joined, held, row = refs[:4], refs[4], refs[5], refs[6]
    blk = lax.axis_index("blk")
    for r in range(4):
        held[blk ^ r] = pieces[r][...]
    joined[96:160, :] = jnp.zeros((64, 1152), BF16)
    for s in range(4):
        joined[0:108, 288 * s : 288 * s + 288] = held[s, 0:108, 0:288]
        for q in range(3):
            at = 288 * q + 72 * s
            joined[112:160, at : at + 72] = held[s, 48 * q : 48 * q + 48, 288:360]
        row[:, 216 * s : 216 * s + 216] = held[s, 112:120, 0:216].astype(F32)
    for j in range(3):
        joined[112 + 16 * j : 120 + 16 * j, 864:1152] = row[:, 288 * j : 288 * j + 288].astype(BF16)


def join_updown_body(*refs):
    pieces, up, down, held = refs[:4], refs[4], refs[5], refs[6]
    blk = lax.axis_index("blk")
    for r in range(4):
        held[blk ^ r] = pieces[r][...]
    for s in range(4):
        up[:, 288 * s : 288 * s + 288] = held[s, :, 0:288]
        down[:, 288 * s : 288 * s + 288] = held[s, :, 288:576]


FIRST_PLACES = (
    (0, 0, 0, 160, 0),
    (-1, 1, 0, 160, 0),
    (1, 2, 0, 160, 0),
    (-2, 3, 0, 160, 0),
    (2, 4, 0, 160, 0),
    (-3, 5, 0, 160, 0),
    (3, 6, 0, 160, 0),
    (4, 7, 0, 80, 0),
    (4, 8, 0, 80, 80),
)
UP_PLACES = (
    (0, 0, 0, 144, 0),
    (-1, 2, 80, 144, 0),
    (1, 3, 80, 144, 0),
    (-2, 4, 0, 144, 0),
    (2, 5, 0, 144, 0),
    (-3, 6, 0, 144, 0),
    (3, 7, 0, 144, 0),
    (4, 8, 0, 80, 0),
    (4, 9, 0, 64, 80),
)
DOWN_PLACES = (
    (0, 1, 0, 144, 0),
    (-1, 4, 144, 144, 0),
    (1, 5, 144, 144, 0),
    (-2, 6, 144, 144, 0),
    (2, 7, 144, 144, 0),
    (-3, 8, 80, 144, 0),
    (3, 9, 64, 144, 0),
    (4, 10, 0, 80, 0),
    (4, 11, 0, 64, 80),
)


def load_chunks(arrays, places, full, first=0, count=144, pitch=None):
    pitch = pitch or count
    for offset, index, start, rows, row in places:
        low, high = max(first, row), min(first + count, row + rows)
        if low < high:
            at = pl.multiple_of(member_at(offset) * pitch + low - first, 16)
            full[pl.ds(at, high - low), :] = arrays[index][start + low - row : start + high - row, :]


def split_halves(total, keep, send):
    for f in range(2):
        keep[128 * f : 128 * f + 128, :] = total[256 * f : 256 * f + 128, :]
        send[128 * f : 128 * f + 128, :] = total[256 * f + 128 : 256 * f + 256, :].astype(BF16)


def join_halves(mine, theirs, full):
    for f in range(2):
        full[256 * f : 256 * f + 128, :] = mine[128 * f : 128 * f + 128, :]
        full[256 * f + 128 : 256 * f + 256, :] = theirs[128 * f : 128 * f + 128, :]


def attend_body(t0, t1, t2, t3, halves, *refs):
    chunks = refs[:9]
    hidden, parts, probs, attended, low, out, mod, keep, send = refs[9:18]
    full, slots, tail = refs[18:]
    load_chunks(chunks, FIRST_PLACES, tail, 112, 48)
    load_chunks(chunks, FIRST_PLACES, full, 0, 112, 160)
    clip = lax.axis_index("dp")
    own = lax.broadcasted_iota(jnp.int32, (8, 288), 0) == clip
    for m in range(24):
        d, j = divmod(m, 3)
        rows = tail[48 * d + 16 * j : 48 * d + 16 * j + 8, 864:1152].astype(F32)
        row = jnp.sum(jnp.where(own, rows, 0.0), axis=0, keepdims=True)
        mod[m // 4 : m // 4 + 1, 288 * (m % 4) : 288 * (m % 4) + 288] = row
        out[48 * m : 48 * m + 48, :] = tail[48 * d : 48 * d + 48, 288 * j : 288 * j + 288]
    for i, block in enumerate((t0, t1, t2, t3)):
        for f in range(2):
            normed, _ = norm_rows(block[f].astype(F32))
            at = 256 * f + 64 * i
            hidden[at : at + 64, :] = (normed * (1.0 + mod[1:2, :]) + mod[0:1, :]).astype(BF16)
    for k, offset in enumerate(NEAR_FIRST):
        at = pl.multiple_of(member_at(offset) * 160 + 112, 16)
        full[pl.ds(at, 48), :] = jnp.concatenate([halves[40 * k : 40 * k + 40, :], jnp.zeros((8, 1152), BF16)], axis=0)
    slots[...] = dot_nt(hidden[...], full[...]).astype(BF16)
    first = lax.axis_index("blk") % 2 == 0
    for e in range(4):
        at = 320 * e
        parts[3 * e] = slots[:, at : at + 72]
        parts[3 * e + 2] = slots[:, at + 160 : at + 232]
        near = jnp.where(first, slots[:, at + 72 : at + 108], slots[:, at + 272 : at + 308])
        far = jnp.where(first, slots[:, at + 112 : at + 148], slots[:, at + 232 : at + 268])
        parts[3 * e + 1, :, 0:36] = near
        parts[3 * e + 1, :, 36:72] = far
    scale = HEAD_DIM ** (-0.5)
    for f in range(2):
        rows = slice(256 * f, 256 * f + 256)
        for h in range(4):
            scores = dot_nt(parts[h, rows, :], parts[4 + h, rows, :]) * scale
            weights = jnp.exp(scores - jnp.max(scores, axis=-1, keepdims=True))
            prob = weights / jnp.sum(weights, axis=-1, keepdims=True)
            probs[4 * f + h] = prob
            mixed = dot_nn(prob.astype(BF16), parts[8 + h, rows, :])
            attended[h, rows, :] = mixed
            low[rows, 72 * h : 72 * h + 72] = mixed.astype(BF16)
    split_halves(dot_nt(low[...], out[...]), keep, send)


def middle_body(keep, near, far, t0, t1, mod, hidden, normed, root, branch, middle):
    for f in range(2):
        for i, block in enumerate((t0, t1)):
            rows = slice(128 * f + 64 * i, 128 * f + 64 * i + 64)
            cross = slice(128 * f + 64 * (1 - i), 128 * f + 64 * (1 - i) + 64)
            part = keep[rows, :] + near[rows, :].astype(F32) + far[cross, :].astype(F32)
            mid = block[f].astype(F32) + mod[2:3, :] * part
            norm, inv = norm_rows(mid)
            hidden[rows, :] = (norm * (1.0 + mod[4:5, :]) + mod[3:4, :]).astype(BF16)
            normed[rows, :] = norm
            root[rows, :] = jnp.broadcast_to(inv, (64, 128))
            if i == 0:
                branch[64 * f : 64 * f + 64, :] = part
                middle[64 * f : 64 * f + 64, :] = mid


def write_parts(total, outs):
    cut = outs[7].shape[0]
    for k in range(8):
        at = pl.multiple_of(member_at(NEAR_FIRST[k]) * 144, 144)
        if k < 7:
            outs[k][...] = total[pl.ds(at, 144), :]
        else:
            outs[7][...] = total[pl.ds(at, cut), :]
            outs[8][...] = total[pl.ds(at + cut, 144 - cut), :]


def up_body(mine, theirs, g0, g1, g2, g3, mod, *refs):
    chunks = refs[:10]
    hidden, act, slope, d_branch = refs[10:14]
    parts = refs[14:23]
    up, total = refs[23:]
    load_chunks(chunks, UP_PLACES, up)
    join_halves(mine, theirs, hidden)
    for f in range(2):
        for i, block in enumerate((g0, g1, g2, g3)):
            row = 256 * f + 64 * i
            d_branch[row : row + 64, :] = (mod[5:6, :] * block[f].astype(F32)).astype(BF16)
    for at in range(0, 512, 256):
        rows = slice(at, at + 256)
        pre = dot_nt(hidden[rows, :], up[...])
        square = pre * pre
        bend = jnp.tanh(GELU_IN * (pre + GELU_CUBE * (square * pre)))
        half = 0.5 * (1.0 + bend)
        act[rows, :] = (pre * half).astype(BF16)
        inner = GELU_IN * (1.0 + (3.0 * GELU_CUBE) * square)
        slope[rows, :] = half + (0.5 * pre) * ((1.0 - bend * bend) * inner)
    total[...] = dot_tn(d_branch[...], act[...]).astype(BF16)
    write_parts(total, parts)


def down_body(d_branch, slope, *refs):
    chunks = refs[:12]
    d_pre, keep, send, down, up = refs[12:]
    load_chunks(chunks, DOWN_PLACES, down)
    load_chunks(chunks, UP_PLACES, up)
    d_pre[...] = (dot_nn(d_branch[...], down[...]) * slope[...]).astype(BF16)
    split_halves(dot_nn(d_pre[...], up[...]), keep, send)


def grad_body(left, right, *refs):
    parts, total = refs[:9], refs[9]
    total[...] = dot_tn(left[...], right[...]).astype(BF16)
    write_parts(total, parts)


def branch_b_body(act, g0, g1, g2, g3, *refs):
    chunks = refs[:12]
    keep, send, d_gate, full, total = refs[12:]
    load_chunks(chunks, DOWN_PLACES, full)
    total[...] = dot_nt(act[...], full[...])
    split_halves(total, keep, send)
    gate = jnp.zeros((1, 1152), F32)
    for f in range(2):
        for i, block in enumerate((g0, g1, g2, g3)):
            row = 256 * f + 64 * i
            gate = gate + jnp.sum(block[f].astype(F32) * total[row : row + 64, :], axis=0, keepdims=True)
    d_gate[...] = gate


def d_middle_body(keep, near, far, normed, root, g0, g1, branch, mod, d_low, d_mid, sums):
    d_shift = jnp.zeros((1, 1152), F32)
    d_scale = jnp.zeros((1, 1152), F32)
    d_gate = jnp.zeros((1, 1152), F32)
    for f in range(2):
        for i, block in enumerate((g0, g1)):
            rows = slice(128 * f + 64 * i, 128 * f + 64 * i + 64)
            cross = slice(128 * f + 64 * (1 - i), 128 * f + 64 * (1 - i) + 64)
            d_hidden = keep[rows, :] + near[rows, :].astype(F32) + far[cross, :].astype(F32)
            norm = normed[rows, :]
            back = norm_back(d_hidden * (1.0 + mod[4:5, :]), norm, root[rows, 0:1])
            mid = block[f].astype(F32) + back
            d_low[rows, :] = (mod[2:3, :] * mid).astype(BF16)
            if i == 0:
                own = slice(64 * f, 64 * f + 64)
                d_mid[own, :] = mid
                d_shift = d_shift + jnp.sum(d_hidden, axis=0, keepdims=True)
                d_scale = d_scale + jnp.sum(d_hidden * norm, axis=0, keepdims=True)
                d_gate = d_gate + jnp.sum(mid * branch[own, :], axis=0, keepdims=True)
    sums[0:1, :] = d_gate
    sums[1:2, :] = d_shift
    sums[2:3, :] = d_scale


def d_attend_body(mine, theirs, parts, probs, attended, out, d_branch, d_slots, d_others, d_att):
    join_halves(mine, theirs, d_branch)
    d_att[...] = dot_nn(d_branch[...], out[...]).astype(BF16)
    scale = HEAD_DIM ** (-0.5)

    first = lax.axis_index("blk") % 2 == 0
    d_slots[...] = jnp.zeros_like(d_slots)

    def place(rows, m, value):
        e, k = divmod(m, 3)
        low = value.astype(BF16)
        at = 224 * e
        if k == 0:
            d_slots[rows, at : at + 72] = low
        elif k == 2:
            d_slots[rows, at + 112 : at + 184] = low
        else:
            near = jnp.where(first, low[:, 0:36], low[:, 36:72])
            d_slots[rows, at + 72 : at + 108] = near
            d_slots[rows, at + 184 : at + 220] = near
            other = jnp.where(first, low[:, 36:72], low[:, 0:36])
            start = rows.start
            d_others[start : start + 128, 36 * e : 36 * e + 36] = other[128:256]
            d_others[start + 128 : start + 256, 36 * e : 36 * e + 36] = other[0:128]

    for f in range(2):
        rows = slice(256 * f, 256 * f + 256)
        for h in range(4):
            d_out = d_att[rows, 72 * h : 72 * h + 72]
            delta = jnp.sum(d_out.astype(F32) * attended[h, rows, :], axis=-1, keepdims=True)
            prob = probs[4 * f + h]
            d_prob = dot_nt(d_out, parts[8 + h, rows, :])
            d_score = (prob * (d_prob - delta)).astype(BF16)
            place(rows, h, dot_nn(d_score, parts[4 + h, rows, :]) * scale)
            place(rows, 4 + h, dot_tn(d_score, parts[h, rows, :]) * scale)
            place(rows, 8 + h, dot_tn(prob.astype(BF16), d_out))


def grad_first_body(d_mine, d_others, hidden, d_branch, low, *refs):
    outs, d_slots, total, below = refs[:9], refs[9], refs[10], refs[11]
    first = lax.axis_index("blk") % 2 == 0
    d_slots[...] = d_mine[...]
    for e in range(4):
        other = d_others[:, 36 * e : 36 * e + 36]
        for odd in range(2):
            at = 224 * e + 112 * odd + 72
            mine = d_mine[:, at : at + 36]
            d_slots[:, at : at + 36] = jnp.where(first == (odd == 0), mine, other)
    total[...] = dot_tn(d_slots[...], hidden[...]).astype(BF16)
    below[...] = dot_tn(d_branch[...], low[...]).astype(BF16)
    for k in range(8):
        at = pl.multiple_of(member_at(NEAR_FIRST[k]) * 112, 112)
        if k < 7:
            outs[k][0:112, :] = total[pl.ds(at, 112), :]
            tail, row = outs[k], 112
        else:
            outs[7][...] = total[pl.ds(at, 80), :]
            outs[8][0:32, :] = total[pl.ds(at + 80, 32), :]
            tail, row = outs[8], 32
        at = pl.multiple_of(member_at(NEAR_FIRST[k]) * 144, 144)
        for q in range(3):
            tail[row : row + 48, 288 * q : 288 * q + 288] = below[pl.ds(at + 48 * q, 48), :]
        tail[row : row + 48, 864:1152] = jnp.zeros((48, 288), BF16)


def d_hidden_a_body(d_slots, t0, t1, t2, t3, sums_b, d_gate_b, *refs):
    chunks = refs[:9]
    keep, send = refs[9:11]
    mods = refs[11:19]
    full, total, flat, d_mod = refs[19:]
    load_chunks(chunks, FIRST_PLACES, full, 0, 112)
    total[...] = dot_nn(d_slots[...], full[...])
    split_halves(total, keep, send)
    d_shift = jnp.zeros((1, 1152), F32)
    d_scale = jnp.zeros((1, 1152), F32)
    for f in range(2):
        for i, block in enumerate((t0, t1, t2, t3)):
            row = 256 * f + 64 * i
            norm, _ = norm_rows(block[f].astype(F32))
            part = total[row : row + 64, :]
            d_shift = d_shift + jnp.sum(part, axis=0, keepdims=True)
            d_scale = d_scale + jnp.sum(part * norm, axis=0, keepdims=True)
    d_mod[0:1, :] = d_shift
    d_mod[1:2, :] = d_scale
    d_mod[2:5, :] = sums_b[0:3, :]
    d_mod[5:6, :] = d_gate_b[...]
    for m in range(24):
        d, j = divmod(m, 3)
        flat[d : d + 1, 288 * j : 288 * j + 288] = d_mod[m // 4 : m // 4 + 1, 288 * (m % 4) : 288 * (m % 4) + 288]
    mine = lax.broadcasted_iota(jnp.int32, (8, 864), 0) == lax.axis_index("dp")
    for k, out in enumerate(mods):
        row = flat[pl.ds(member_at(NEAR_FIRST[k]), 1), :]
        out[...] = jnp.zeros((8, 1152), BF16)
        out[:, 0:864] = jnp.where(mine, row, 0.0).astype(BF16)


def own_half_body(keep, near, own, cross):
    for f in range(2):
        for i, block in enumerate((own, cross)):
            rows = slice(128 * f + 64 * i, 128 * f + 64 * i + 64)
            part = keep[rows, :] + near[rows, :].astype(F32)
            block[64 * f : 64 * f + 64, :] = part.astype(block.dtype)


def output_body(own, far, middle, mod, output):
    for f in range(2):
        rows = slice(64 * f, 64 * f + 64)
        output[f] = middle[rows, :] + mod[5:6, :] * (own[rows, :] + far[rows, :].astype(F32))


def grad_tokens_body(own, far, t0, d_mid, mod, grad):
    for f in range(2):
        rows = slice(64 * f, 64 * f + 64)
        norm, inv = norm_rows(t0[f].astype(F32))
        d_hidden = own[rows, :] + far[rows, :].astype(F32)
        grad[f] = d_mid[rows, :] + norm_back(d_hidden * (1.0 + mod[1:2, :]), norm, inv)


def cut_updown_body(u0, u1, u2, d0, d1, d2, here, near, cross, held):
    blk = lax.axis_index("blk")
    up = u0[...].astype(F32) + u1[0:144, :].astype(F32) + u2[0:144, :].astype(F32)
    down = d0[...].astype(F32) + d1[144:288, :].astype(F32) + d2[144:288, :].astype(F32)
    for t in range(4):
        held[t, :, 0:288] = up[:, 288 * t : 288 * t + 288].astype(BF16)
        held[t, :, 288:576] = down[:, 288 * t : 288 * t + 288].astype(BF16)
        held[t, :, 576:640] = jnp.zeros((144, 64), BF16)
    here[...] = held[blk]
    near[...] = held[blk ^ 1]
    cross[0:144, :] = held[blk ^ 2]
    cross[144:288, :] = held[blk ^ 3]


def final_updown_body(here, far, near, up, down, held):
    blk = lax.axis_index("blk")
    held[blk] = here[...]
    held[blk ^ 1] = near[0:144, :]
    held[blk ^ 2] = far[0:144, :]
    held[blk ^ 3] = near[144:288, :]
    for s in range(4):
        up[:, 144 * s : 144 * s + 144] = held[s, :, 0:288].astype(F32).T
        for part in range(2):
            at = 576 * part + 144 * s
            down[:, at : at + 144] = held[s, :, 288 + 144 * part : 432 + 144 * part].astype(F32)


def cut_heads_body(s0, s1, s2, m0, *refs):
    pieces, held = refs[:4], refs[4]
    blk = lax.axis_index("blk")
    total = s0[...].astype(F32) + s1[0:160, :].astype(F32) + s2[0:160, :].astype(F32)
    mods = m0[...].astype(F32) + s1[160:168, :].astype(F32) + s2[160:168, :].astype(F32)
    for t in range(4):
        held[t, :, 0:288] = jnp.zeros((144, 288), BF16)
        held[t, 0:108, 0:288] = total[0:108, 288 * t : 288 * t + 288].astype(BF16)
        held[t, 112:120, 0:216] = mods[:, 216 * t : 216 * t + 216].astype(BF16)
        for q in range(3):
            at = 288 * q + 72 * t
            held[t, 48 * q : 48 * q + 48, 288:360] = total[112:160, at : at + 72].astype(BF16)
        held[t, :, 360:384] = jnp.zeros((144, 24), BF16)
    for r in range(4):
        pieces[r][...] = held[blk ^ r]


def final_heads_body(timestep, p0, p1, p2, p3, qkv, out, table, held, placed, pieces, wide):
    blk = lax.axis_index("blk")
    mods = p0[112:120, 0:216].astype(F32) + p1[112:120, 0:216].astype(F32)
    mods = (mods + p2[112:120, 0:216].astype(F32) + p3[112:120, 0:216].astype(F32)).T
    wide[...] = jnp.zeros_like(wide)
    lane = lax.broadcasted_iota(jnp.int32, (216, 128), 1)
    for c in range(8):
        step = timestep[c]
        lanes = pl.ds(pl.multiple_of((step // 128) * 128, 128), 128)
        wide[:, lanes] = wide[:, lanes] + jnp.where(lane == step % 128, mods[:, c : c + 1], 0.0)
    table[...] = wide[:, 0 : table.shape[1]]
    for r, piece in enumerate((p0, p1, p2, p3)):
        pieces[blk ^ r] = piece[...]
    for sender in range(4):
        alone, shared = columns_of(sender)
        half = 36 * (sender & 1)
        placed[alone] = pieces[sender, 0:72, 0:288].astype(F32)
        placed[shared, half : half + 36, :] = pieces[sender, 72:108, 0:288].astype(F32)
        held[kind_of(sender)] = pieces[sender, :, 288:360].astype(F32)
    for i in range(6):
        qkv[:, 72 * i : 72 * i + 72] = placed[i].T
    for s in range(4):
        out[:, 72 * s : 72 * s + 72] = held[s]


def vmem(shape, kind=BF16):
    return (shape, kind)


def local_kernels(tokens, timestep, mod_table, w_qkv, w_out, w_up, w_down, cotangent):
    nd, nb = 8, 4
    ring = Ring(nd, lax.axis_index("dp"))
    group = Group(nb, lax.axis_index("blk"))
    width = tokens.shape[3]
    own_tokens = tokens[0]
    own_cot = cotangent[0]
    full_low = ((512, 1152), BF16)
    chunk_low = ((144, 1152), BF16)
    part_low = [chunk_low] * 7 + [((80, 1152), BF16), ((64, 1152), BF16)]
    half_low = ((256, 1152), BF16)
    half_wide = ((256, 1152), F32)
    own_wide = ((128, 1152), F32)

    def send_out(pieces):
        return [pieces[0]] + [group.swap(pieces[r], r) for r in (1, 2, 3)]

    def add_low(keep, near):
        return (keep + near.astype(F32)).astype(BF16)

    def own_half(keep, near, name):
        return run_kernel(own_half_body, [own_wide, ((128, 1152), BF16)], keep, near, name=name)

    picker = (timestep[:, None] == jnp.arange(mod_table.shape[0], dtype=jnp.int32)[None, :]).astype(BF16)
    table_cols = dot_nn(picker, mod_table).astype(BF16)
    heads_cut = run_kernel(
        pack_heads_body,
        [((144, 384), BF16)] * 4,
        w_qkv, w_out.T, table_cols,
        scratch=[vmem((2, 6, 36, 288)), vmem((4, 144, 72))],
        name="pack_heads",
    )
    heads_got = send_out(heads_cut)
    (first_own,) = run_kernel(
        join_heads_body,
        [((160, 1152), BF16)],
        *heads_got,
        scratch=[vmem((4, 144, 384)), vmem((8, 864), F32)],
        name="join_heads",
    )
    updown_cut = run_kernel(
        pack_updown_body,
        [((144, 640), BF16)] * 4,
        *after((w_up, w_down.T), heads_got[1]),
        scratch=[vmem((4, 144, 288)), vmem((4, 144, 288))],
        name="pack_updown",
    )
    updown_got = send_out(updown_cut)
    fore1, rear1, _ = step(ring, first_own, first_own)
    fore2, rear2, held = step(ring, fore1, rear1, own_tokens, *updown_got)
    far_t = group.swap(held[0], 2)
    up_own, down_own = run_kernel(
        join_updown_body, [chunk_low] * 2, *held[1:], scratch=[vmem((4, 144, 640))], name="join_updown"
    )
    fore3, rear3, held = step(ring, fore2, rear2, up_own, down_own, far_t, own_tokens, own_cot)
    up_own, down_own, far_t, own_t, own_c = held
    token_blocks = [own_tokens, far_t, group.swap(own_t, 1), group.swap(far_t, 1)]
    far_c = group.swap(own_c, 2)
    fore4, rear4, held = step(
        ring, stack(fore3[:80], up_own), stack(rear3[80:], up_own), far_c, own_cot, *token_blocks
    )
    far_c, own_c, *token_blocks = held
    cot_blocks = [own_cot, far_c, group.swap(own_c, 1), group.swap(far_c, 1)]
    first_got = [first_own, fore1, rear1, fore2, rear2, fore3, rear3, fore4, rear4]
    fore5, rear5, held = step(
        ring, stack(fore4[80:], down_own), stack(rear4[80:], down_own), *cot_blocks, *token_blocks, *first_got
    )
    cot_blocks, token_blocks, first_got = held[:4], held[4:8], held[8:]
    other_halves = stack(*(chunk[72:112] for chunk in first_got[:7]), first_got[7][72:80], first_got[8][:32])
    hidden_a, parts, probs, attended, low, out_full, mod, keep_a, send_a = run_kernel(
        attend_body,
        [
            full_low,
            ((12, 512, 72), BF16),
            ((8, 256, 256), F32),
            ((4, 512, 72), F32),
            ((512, 288), BF16),
            ((1152, 288), BF16),
            ((8, 1152), F32),
            half_wide,
            half_low,
        ],
        *token_blocks, group.swap(other_halves, 1), *first_got,
        scratch=[vmem((1280, 1152)), vmem((512, 1280)), vmem((384, 1152))],
        flops=4 * 10**9,
        name="attend",
    )
    fore6, rear6, (keep_a, send_a) = step(ring, fore5, rear5, keep_a, send_a)
    near_a = group.swap(send_a, 1)
    far_a = group.swap(add_low(keep_a, near_a), 2)
    fore7, rear7, (keep_a, near_a, far_a) = step(
        ring, stack(fore6[:80], fore6[144:]), rear6[80:], keep_a, near_a, far_a
    )
    hidden_mine, normed_b, root_b, branch_a, middle = run_kernel(
        middle_body,
        [half_low, half_wide, ((256, 128), F32), own_wide, own_wide],
        keep_a, near_a, far_a, *token_blocks[:2], mod,
        name="middle",
    )
    hidden_theirs = group.swap(hidden_mine, 1)
    fore8, rear8, (hidden_mine, hidden_theirs) = step(ring, fore7[80:160], rear7[144:], hidden_mine, hidden_theirs)
    up_got = [up_own, down_own, fore4, rear4, fore5, rear5, fore6, rear6, fore7, rear7]
    down_got = [*up_got, fore8, rear8]
    hidden_b, act, slope, d_branch_b, *grad_down = run_kernel(
        up_body,
        [full_low, full_low, ((512, 1152), F32), full_low] + part_low,
        hidden_mine, hidden_theirs, *cot_blocks, mod, *up_got,
        scratch=[vmem((1152, 1152)), vmem((1152, 1152))],
        flops=4 * 10**9,
        name="up",
    )
    fore1, rear1, held = step(ring, *grad_down[7:], d_branch_b, slope, *down_got)
    d_branch_b, slope, down_got = held[0], held[1], held[2:]
    d_pre, keep_d, send_d = run_kernel(
        down_body,
        [full_low, half_wide, half_low],
        d_branch_b, slope, *down_got,
        scratch=[vmem((1152, 1152)), vmem((1152, 1152))],
        flops=4 * 10**9,
        name="down",
    )
    near_d = group.swap(send_d, 1)
    low_d = add_low(keep_d, near_d)
    grad_up = run_kernel(
        grad_body,
        part_low,
        d_pre, hidden_b,
        scratch=[vmem((1152, 1152))],
        flops=2 * 10**9,
        name="grad_up",
    )
    fore2, rear2, (keep_d, near_d, low_d, act) = step(
        ring,
        stack(grad_up[7], sum_low(grad_down[6][:80], fore1), grad_down[6][80:]),
        stack(grad_up[8], grad_down[5][:80], sum_low(grad_down[5][80:], rear1)),
        keep_d, near_d, low_d, act,
    )
    far_d = group.swap(low_d, 2)
    keep_b, send_b, d_gate_b = run_kernel(
        branch_b_body,
        [half_wide, half_low, ((1, 1152), F32)],
        act, *cot_blocks, *down_got,
        scratch=[vmem((1152, 1152)), vmem((512, 1152), F32)],
        flops=2 * 10**9,
        name="branch_b",
    )
    near_b = group.swap(send_b, 1)
    fore3, rear3, (keep_d, near_d, far_d, keep_b, near_b) = step(
        ring,
        stack(sum_low(grad_up[6][:80], fore2[:80]), grad_up[6][80:], sum_low(grad_down[4], fore2[80:])),
        stack(grad_up[5][:80], sum_low(grad_up[5][80:], rear2[:64]), sum_low(grad_down[3], rear2[64:])),
        keep_d, near_d, far_d, keep_b, near_b,
    )
    d_low, d_mid, sums_b = run_kernel(
        d_middle_body,
        [half_low, own_wide, ((3, 1152), F32)],
        keep_d, near_d, far_d, normed_b, root_b, *cot_blocks[:2], branch_a, mod,
        name="d_middle",
    )
    d_branch_a, d_mine, d_others = run_kernel(
        d_attend_body,
        [full_low, ((512, 896), BF16), ((512, 144), BF16)],
        d_low, group.swap(d_low, 1), parts, probs, attended, out_full,
        scratch=[vmem((512, 288))],
        flops=3 * 10**9,
        name="d_attend",
    )
    d_others = group.swap(d_others, 1)
    fore4, rear4, held = step(
        ring,
        stack(sum_low(grad_up[4], fore3[:144]), sum_low(grad_down[2], fore3[144:])),
        stack(sum_low(grad_up[3], rear3[:144]), sum_low(grad_down[1], rear3[144:])),
        keep_b, near_b, d_mine, d_others, d_branch_a,
    )
    keep_b, near_b, d_mine, d_others, d_branch_a = held
    own_b, cross_b = own_half(keep_b, near_b, "own_b")
    far_b = group.swap(cross_b, 2)
    *grad_first, d_slots = run_kernel(
        grad_first_body,
        [((160, 1152), BF16)] * 7 + [((80, 1152), BF16)] * 2 + [((512, 896), BF16)],
        d_mine, d_others, hidden_a, d_branch_a, low,
        scratch=[vmem((896, 1152)), vmem((1152, 288))],
        flops=2 * 10**9,
        name="grad_first",
    )
    keep_h, send_h, *mods = run_kernel(
        d_hidden_a_body,
        [half_wide, half_low] + [((8, 1152), BF16)] * 8,
        d_slots, *token_blocks, sums_b, d_gate_b, *first_got,
        scratch=[
            vmem((896, 1152)),
            vmem((512, 1152), F32),
            vmem((8, 864), F32),
            vmem((6, 1152), F32),
        ],
        flops=2 * 10**9,
        name="d_hidden_a",
    )
    fore5, rear5, (keep_h, send_h, own_b, far_b) = step(
        ring,
        stack(sum_low(grad_up[2], fore4[:144]), grad_first[7], mods[7]),
        stack(sum_low(grad_up[1], rear4[:144]), grad_first[8]),
        keep_h, send_h, own_b, far_b,
    )
    near_h = group.swap(send_h, 1)
    fore6, rear6, held = step(
        ring,
        stack(sum_low(grad_first[6][:80], fore5[144:224]), grad_first[6][80:], sum_low(mods[6], fore5[224:])),
        stack(grad_first[5][:80], sum_low(grad_first[5][80:], rear5[144:]), mods[5]),
        keep_h, near_h, fore4, rear4, fore5, rear5,
    )
    keep_h, near_h, *up_down = held
    own_h, cross_h = own_half(keep_h, near_h, "own_h")
    far_h = group.swap(cross_h, 2)
    here, near_u, cross_u = run_kernel(
        cut_updown_body,
        [((144, 640), BF16)] * 2 + [((288, 640), BF16)],
        grad_up[0], *up_down[2:], grad_down[0], *up_down[:2],
        scratch=[vmem((4, 144, 640))],
        name="cut_updown",
    )
    fore7, rear7, held = step(
        ring,
        stack(sum_low(grad_first[4], fore6[:160]), sum_low(mods[4], fore6[160:])),
        stack(sum_low(grad_first[3], rear6[:160]), sum_low(mods[3], rear6[160:])),
        here, near_u, cross_u,
    )
    here, near_u, cross_u = held
    far_u = group.swap(cross_u, 2)
    fore8, rear8, held = step(
        ring,
        stack(sum_low(grad_first[2], fore7[:160]), sum_low(mods[2], fore7[160:])),
        stack(sum_low(grad_first[1], rear7[:160]), sum_low(mods[1], rear7[160:])),
        own_b, far_b, here, near_u,
    )
    own_b, far_b, here, near_u = held
    (output,) = run_kernel(
        output_body, [((2, 64, 1152), F32)], own_b, far_b, middle, mod, name="output"
    )
    (grad_tokens,) = run_kernel(
        grad_tokens_body, [((2, 64, 1152), F32)], own_h, far_h, own_tokens, d_mid, mod, name="grad_tokens"
    )
    final_up, final_down = run_kernel(
        final_updown_body,
        [((288, 576), F32), ((144, 1152), F32)],
        here, far_u, group.swap(stack(near_u, far_u[144:]), 1),
        scratch=[vmem((4, 144, 640))],
        name="final_updown",
    )
    heads_cut = run_kernel(
        cut_heads_body, [((144, 384), BF16)] * 4, grad_first[0], fore8, rear8, mods[0], scratch=[vmem((4, 144, 384))], name="cut_heads"
    )
    final_qkv, final_out, grad_table = run_kernel(
        final_heads_body,
        [((288, 432), F32), ((144, 288), F32), ((216, mod_table.shape[0]), F32)],
        timestep, *send_out(heads_cut),
        scalars=1,
        scratch=[
            vmem((4, 144, 72), F32),
            vmem((6, 72, 288), F32),
            vmem((4, 144, 384)),
            vmem((216, -(-mod_table.shape[0] // 128) * 128), F32),
        ],
        name="final_heads",
    )
    return (output[None], grad_tokens[None], grad_table.T, final_qkv, final_out.T, final_up, final_down.T)


def local(tokens, timestep, mod_table, w_qkv, w_out, w_up, w_down, cotangent):
    sizes = (lax.axis_size("dp"), lax.axis_size("blk"), tokens.shape, w_qkv.shape, w_up.shape, w_down.shape)
    known = (8, 4, (1, 2, 64, 1152), (288, 432), (288, 576), (1152, 144))
    chosen = local_kernels if sizes == known else local_plain
    return chosen(tokens, timestep, mod_table, w_qkv, w_out, w_up, w_down, cotangent)


def solution(mesh):
    in_specs = (
        P("dp", None, "blk", None),
        P(),
        P(None, ("dp", "blk")),
        P("blk", "dp"),
        P("blk", "dp"),
        P("blk", "dp"),
        P("blk", "dp"),
        P("dp", None, "blk", None),
    )
    out_specs = (
        P("dp", None, "blk", None),
        P("dp", None, "blk", None),
        P(None, ("dp", "blk")),
        P("blk", "dp"),
        P("blk", "dp"),
        P("blk", "dp"),
        P("blk", "dp"),
    )
    return jax.shard_map(local, mesh=mesh, in_specs=in_specs, out_specs=out_specs, check_vma=False)
```
